256 devices in a mesh: seq: 32 (over x, y, core), clip: 8 (over z).
Axes of the slice: x: 4, y: 4, z: 8, core: 2. Of those that a mesh axis runs over, the one named last changes fastest.
Arguments:
- tokens: bfloat16 [32, 128, 64, 192], P('clip', None, 'seq'), may hold values from -6 to 6
- conv_one: bfloat16 [3, 3, 3, 192, 192], replicated, may hold values from -0.078125 to 0.078125
- conv_two: bfloat16 [3, 3, 3, 192, 96], replicated, may hold values from -0.078125 to 0.078125
- pixel_grad: bfloat16 [32, 256, 128, 96], P('clip', 'seq'), may hold values from -6 to 6
Outputs:
- decoded: bfloat16 [32, 256, 128, 96], P('clip', 'seq')
- token_grad: bfloat16 [32, 128, 64, 192], P('clip', None, 'seq')
The draws below stay inside these ranges and needn't reach their ends.
All inputs are finite; a program needn't handle non-finite values.
Results may differ from the reference program's by a relative error of at most 0.0052.
Values may be sent and summed in bfloat16 or wider, within the bound.
No kernel may reach another device: no remote copies, remote signals or barrier semaphores. Data moves between devices by JAX's collectives and lax.ppermute only.
A program may use at most 64 MiB of HBM per device.

```python
import jax
import jax.numpy as jnp
from jax import lax

C1 = 192
C2 = 96
GROUPS = 32
W = 64
FRAMES = 32
HEIGHT = 128


def common_field(key):
    return jax.random.normal(key, (FRAMES, HEIGHT, W, C1), jnp.float32)


def frame_trend(key):
    ramp = (jnp.arange(FRAMES, dtype=jnp.float32) / float(FRAMES - 1) - 0.5) * 1.1
    jitter = jax.random.uniform(key, (FRAMES,), jnp.float32, -0.2, 0.2)
    return jnp.exp(ramp + jitter).reshape(FRAMES, 1, 1, 1)


def row_ramp():
    return (jnp.arange(HEIGHT, dtype=jnp.float32) / float(HEIGHT - 1) - 0.5).reshape(1, HEIGHT, 1, 1)


def axis_ramp(count, position):
    ramp = jnp.arange(count, dtype=jnp.float32) / float(count - 1) - 0.5
    shape = [1, 1, 1, 1]
    shape[position] = count
    return ramp.reshape(shape)


def draw_tokens(key, part):
    base = common_field(key)
    key = jax.random.fold_in(key, 11)
    keys = jax.random.split(key, 5)
    scale_frames = frame_trend(keys[0])
    signs = (jax.random.randint(keys[1], (GROUPS,), 0, 2) * 2 - 1).astype(jnp.float32)
    sizes = jax.random.uniform(keys[2], (GROUPS,), jnp.float32, 0.3, 1.0)
    offset = jnp.repeat(signs * sizes, C1 // GROUPS) + 0.3 * jax.random.normal(keys[3], (C1,), jnp.float32)
    shift_frames = 0.3 * jax.random.normal(keys[4], (FRAMES, 1, 1, 1), jnp.float32)
    columns = axis_ramp(W, 2)
    noise = base
    scale_rows = jnp.exp(1.2 * row_ramp())
    shift_rows = 1.4 * row_ramp()
    scale_cols = jnp.exp(0.8 * columns)
    shift_cols = 1.2 * columns
    values = noise * scale_frames * scale_rows * scale_cols + offset + shift_frames + shift_rows + shift_cols
    return jnp.clip(values, -6.0, 6.0).astype(jnp.bfloat16)


def draw_pixel_grad(key, part):
    base = common_field(key)
    key = jax.random.fold_in(key, 23)
    keys = jax.random.split(key, 2)
    shape = (FRAMES, 2 * HEIGHT, 2 * W, C2)
    linked = jnp.repeat(jnp.repeat(base[..., :C2], 2, axis=1), 2, axis=2)
    offset = 0.6 * jax.random.normal(keys[1], (C2,), jnp.float32)
    columns = axis_ramp(2 * W, 2)
    rows = axis_ramp(2 * HEIGHT, 1)
    noise = jax.random.normal(keys[0], shape, jnp.float32)
    scale_cols = jnp.exp(0.8 * columns)
    shift_cols = columns
    shift_rows = 0.8 * rows
    values = (noise + 0.5 * linked) * scale_cols + offset + shift_cols + shift_rows
    return jnp.clip(values, -6.0, 6.0).astype(jnp.bfloat16)


def centred(own_key, extent, deviation, limit, held_as=jnp.bfloat16):
    return jnp.clip(deviation * jax.random.normal(own_key, extent, jnp.float32), -limit, limit).astype(held_as)


def setup_inputs(seed: int = 0) -> dict:
    key_of = jax.random.split(jax.random.key(seed), 5)
    tokens = draw_tokens(jax.random.fold_in(key_of[4], 71), 0)
    conv_one = centred(key_of[1], (3, 3, 3, C1, C1), (27 * C1) ** -0.5, 0.078125)
    conv_two = centred(key_of[2], (3, 3, 3, C1, C2), (27 * C1) ** -0.5, 0.078125)
    pixel_grad = draw_pixel_grad(jax.random.fold_in(key_of[4], 71), 0)
    return {"tokens": tokens, "conv_one": conv_one, "conv_two": conv_two, "pixel_grad": pixel_grad}


def causal_conv(padded, kernel, frames):
    rows = padded.shape[1] - 2
    cols = padded.shape[2] - 2
    chans = padded.shape[3]
    outs = kernel.shape[4]
    flat_kernel = kernel.reshape(3, 3, 3 * chans, outs)

    def one_frame(start):
        window = lax.dynamic_slice_in_dim(padded, start, 3, 0)
        stacked = jnp.concatenate([window[:, :, 0:cols], window[:, :, 1:cols + 1], window[:, :, 2:cols + 2]], axis=-1)
        running = jnp.zeros((rows * cols, outs), jnp.float32)
        for tap_time in range(3):
            for tap_row in range(3):
                piece = stacked[tap_time, tap_row:tap_row + rows].reshape(rows * cols, 3 * chans)
                running = running + jnp.dot(piece, flat_kernel[tap_time, tap_row], preferred_element_type=jnp.float32)
        return running.reshape(rows, cols, outs)
    return lax.map(one_frame, jnp.arange(frames, dtype=jnp.int32))

def flipped(kernel):
    return jnp.swapaxes(kernel[::-1, ::-1, ::-1], 3, 4)

def grouped(field):
    shape = field.shape
    return field.reshape(shape[0], shape[1], shape[2], GROUPS, shape[3] // GROUPS)

def reference(tokens, conv_one, conv_two, pixel_grad):
    frames = tokens.shape[0]
    values = grouped(tokens.astype(jnp.float32))
    mean = lax.optimization_barrier(jnp.mean(values, axis=(0, 1, 2, 4), keepdims=True))
    var = lax.optimization_barrier(jnp.mean((values - mean) ** 2, axis=(0, 1, 2, 4), keepdims=True))
    rscale = lax.rsqrt(var + 1e-06)
    normed = (values - mean) * rscale
    act = jax.nn.silu(normed).reshape(tokens.shape).astype(jnp.bfloat16)
    padded = jnp.pad(act, ((2, 0), (1, 1), (1, 1), (0, 0)))
    mid = (tokens.astype(jnp.float32) + causal_conv(padded, conv_one, frames)).astype(jnp.bfloat16)
    upper = jnp.repeat(jnp.repeat(mid, 2, axis=1), 2, axis=2)
    padded_up = jnp.pad(upper, ((2, 0), (1, 1), (1, 1), (0, 0)))
    decoded = causal_conv(padded_up, conv_two, frames).astype(jnp.bfloat16)
    grad_pad = jnp.pad(pixel_grad, ((0, 2), (1, 1), (1, 1), (0, 0)))
    up_grad = causal_conv(grad_pad, flipped(conv_two), frames)
    shape = mid.shape
    mid_grad = up_grad.reshape(shape[0], shape[1], 2, shape[2], 2, shape[3]).sum(axis=(2, 4)).astype(jnp.bfloat16)
    mid_pad = jnp.pad(mid_grad, ((0, 2), (1, 1), (1, 1), (0, 0)))
    act_grad = grouped(causal_conv(mid_pad, flipped(conv_one), frames))
    sigmoid = jax.nn.sigmoid(normed)
    norm_grad = act_grad * sigmoid * (1.0 + normed * (1.0 - sigmoid))
    first = lax.optimization_barrier(jnp.mean(norm_grad, axis=(0, 1, 2, 4), keepdims=True))
    second = lax.optimization_barrier(jnp.mean(norm_grad * normed, axis=(0, 1, 2, 4), keepdims=True))
    back = ((norm_grad - first - normed * second) * rscale).reshape(tokens.shape)
    token_grad = (mid_grad.astype(jnp.float32) + back).astype(jnp.bfloat16)
    return (decoded, token_grad)
```

```python
import functools

import jax
import jax.numpy as jnp
from jax import lax
from jax.experimental import pallas as pl
from jax.experimental.pallas import tpu as pltpu
from jax.sharding import PartitionSpec as P

GROUPS = 32
F32 = jnp.float32
BF16 = jnp.bfloat16
VMEM_LIMIT = 48 * 2**20
TAPS = ((2,), (1, 2), (0, 1), (0,))


def vmem(count):
    return [pl.BlockSpec(memory_space=pltpu.VMEM)] * count


def smem():
    return pl.BlockSpec(memory_space=pltpu.SMEM)


def call(kernel, name, outs, in_specs, scratch, flops):
    return pl.pallas_call(
        kernel,
        name=name,
        out_shape=outs,
        in_specs=in_specs,
        out_specs=jax.tree.map(lambda _: pl.BlockSpec(memory_space=pltpu.VMEM), outs),
        scratch_shapes=scratch,
        compiler_params=pltpu.CompilerParams(vmem_limit_bytes=VMEM_LIMIT),
        cost_estimate=pl.CostEstimate(flops=flops, bytes_accessed=4 * 2**20, transcendentals=0),
    )


def combine_kernel(w_ref, out_ref):
    ins, outs = w_ref.shape[3], w_ref.shape[4]

    def one_time(a, carry):
        w = [[w_ref[a, b, d].astype(F32) for d in range(3)] for b in range(3)]
        for p in range(4):
            rows = [functools.reduce(jnp.add, [w[b][d] for b in TAPS[p]]) for d in range(3)]
            for q in range(4):
                value = functools.reduce(jnp.add, [rows[d] for d in TAPS[q]])
                out_ref[a, p, q] = jnp.pad(value, ((0, 0), (0, 128 - outs))).astype(BF16)
        return carry

    lax.fori_loop(0, 3, one_time, 0)


def combined_weights(conv_two):
    ins = conv_two.shape[3]
    return call(
        combine_kernel,
        "combine_weights",
        jax.ShapeDtypeStruct((3, 4, 4, ins, 128), BF16),
        vmem(1),
        [],
        10**6,
    )(conv_two)


def spread_columns(value, buffer, t, r, chans):
    cols = value.shape[0]
    index = lax.broadcasted_iota(jnp.int32, value.shape, 0)
    left = jnp.where(index == 0, 0.0, pltpu.roll(value, 1, 0))
    right = jnp.where(index == cols - 1, 0.0, pltpu.roll(value, cols - 1, 0))
    buffer[t, r, :, 0:chans] = left.astype(BF16)
    buffer[t, r, :, 256 : 256 + chans] = value.astype(BF16)
    buffer[t, r, :, 512 : 512 + chans] = right.astype(BF16)


def fill(buffer, pieces, chans, transform):
    for ref, source, count, t0, r0, keep in pieces:
        rows = ref.shape[1]

        def one_frame(i, carry):
            for r in range(rows):
                value = transform(ref[source + i, r].astype(F32), keep)
                spread_columns(value, buffer, t0 + i, r0 + r, chans)
            return carry

        lax.fori_loop(0, count, one_frame, 0)


def nt_dot(lhs, rhs):
    return lax.dot_general(lhs, rhs, (((1,), (1,)), ((), ())), preferred_element_type=F32)


def down_kernel(layout, frames, rows, flags, weights, *refs):
    sources = refs[: len(layout)]
    out_ref, buffer, wide = refs[len(layout) :]
    cols = out_ref.shape[2]
    outs = out_ref.shape[3]
    chans = sources[0].shape[3]
    wide[...] = jnp.zeros_like(wide)
    for ref, (source, count, t0, r0) in zip(sources, layout):
        lines = ref.shape[1]

        def one_frame(i, carry):
            for r in range(lines):
                wide[r, 8 : 8 + 2 * cols, 0:chans] = ref[source + i, r].astype(F32)
            for r in range(lines):
                line = r0 + r
                for j in range(4):
                    part = wide[r, pl.ds(7 + j, cols, stride=2), :]
                    buffer[t0 + i, line % 2, line // 2, :, 128 * j : 128 * (j + 1)] = part.astype(BF16)
            return carry

        lax.fori_loop(0, count, one_frame, 0)

    def one_out(t, carry):
        total = jnp.zeros((rows * cols, outs), F32)
        for dt in range(3):
            for p in range(4):
                lhs = buffer[t + dt, p % 2, p // 2 : p // 2 + rows].reshape(rows * cols, 512)
                rhs = jnp.concatenate([weights[2 - dt, p, q] for q in range(4)], axis=-1)
                total = total + nt_dot(lhs, rhs)
        total = total.reshape(rows, cols, outs)
        out_ref[t, 0] = (total[0] * flags[0]).astype(BF16)
        out_ref[t, 1 : rows - 1] = total[1 : rows - 1].astype(BF16)
        out_ref[t, rows - 1] = (total[rows - 1] * flags[1]).astype(BF16)
        return carry

    lax.fori_loop(0, frames, one_out, 0)


def down(name, flags, weights, pieces, frames, rows, cols, outs):
    layout = tuple((s, n, t0, r0) for _, s, n, t0, r0 in pieces)
    lines = max(a.shape[1] for a, *_ in pieces)
    return call(
        functools.partial(down_kernel, layout, frames, rows),
        name,
        jax.ShapeDtypeStruct((frames, rows, cols, outs), BF16),
        [smem()] + vmem(1 + len(pieces)),
        [
            pltpu.VMEM((frames + 2, 2, rows + 1, cols, 512), BF16),
            pltpu.VMEM((lines, 2 * cols + 16, 128), F32),
        ],
        2 * frames * rows * cols * 24 * 65536,
    )(flags, weights, *[a for a, *_ in pieces])


def back_kernel(layout, frames, first, flags, stats, weights, tile_ref, *refs):
    sources = refs[: len(layout)]
    out_ref, sums_ref, buffer = refs[len(layout) :]
    rows, cols, chans = out_ref.shape[1:]
    fill(
        buffer,
        [(ref, s, n, t0, 0, None) for ref, (s, n, t0) in zip(sources, layout)],
        chans,
        lambda value, keep: value,
    )
    mean = stats[0:1]
    scale = stats[1:2]
    sums_ref[...] = jnp.zeros_like(sums_ref)

    def one_out(t, carry):
        total = jnp.zeros((rows * cols, chans), F32)
        for dt in range(3):
            for dr in range(3):
                for dc in range(3):
                    lhs = buffer[t + dt, dr : dr + rows, :, 256 * dc : 256 * dc + chans]
                    lhs = lhs.reshape(rows * cols, chans)
                    total = total + nt_dot(lhs, weights[2 - dt, 2 - dr, 2 - dc])
        normed = (tile_ref[first + t].reshape(rows * cols, chans).astype(F32) - mean) * scale
        sigmoid = 1.0 / (1.0 + jnp.exp(-normed))
        grad = total * sigmoid * (1.0 + normed * (1.0 - sigmoid))
        sums_ref[0:1] += jnp.sum(grad, axis=0, keepdims=True)
        sums_ref[1:2] += jnp.sum(grad * normed, axis=0, keepdims=True)
        own = buffer[t, 1 : 1 + rows, :, 256 : 256 + chans].reshape(rows * cols, chans)
        base = own.astype(F32) + grad * scale
        out_ref[t] = base.astype(BF16).reshape(rows, cols, chans)
        return carry

    lax.fori_loop(0, frames, one_out, 0)


def back(name, flags, stats, weights, tile, pieces, frames, first):
    layout = tuple((s, n, t0) for _, s, n, t0 in pieces)
    _, rows, cols, chans = tile.shape
    return call(
        functools.partial(back_kernel, layout, frames, first),
        name,
        (
            jax.ShapeDtypeStruct((frames, rows, cols, chans), BF16),
            jax.ShapeDtypeStruct((2, chans), F32),
        ),
        [smem()] + vmem(3 + len(pieces)),
        [pltpu.VMEM((frames + 2, rows + 2, cols, 768), BF16)],
        2 * frames * rows * cols * 27 * 65536,
    )(flags, stats, weights, tile, *[a for a, *_ in pieces])


def mid_kernel(layout, frames, rows, first, flags, stats, weights, *refs):
    sources = refs[: len(layout)]
    out_ref, buffer = refs[len(layout) :]
    cols, chans = out_ref.shape[2:]
    mean = stats[0:1]
    scale = stats[1:2]

    def activate(value, keep):
        normed = (value - mean) * scale
        act = normed / (1.0 + jnp.exp(-normed))
        for flag in keep:
            act = act * flags[flag]
        return act

    fill(
        buffer,
        [(ref, *where) for ref, where in zip(sources, layout)],
        chans,
        activate,
    )
    own, up, down_ref = sources[:3]

    def one_out(t, carry):
        total = jnp.zeros((rows * cols, chans), F32)
        for dt in range(3):
            for dr in range(3):
                for dc in range(3):
                    lhs = buffer[t + dt, dr : dr + rows, :, 256 * dc : 256 * dc + chans]
                    lhs = lhs.reshape(rows * cols, chans)
                    total = total + jnp.dot(lhs, weights[dt, dr, dc], preferred_element_type=F32)
        total = total.reshape(rows, cols, chans)
        at = first + t
        out_ref[t, 0] = ((total[0] + up[at, 1].astype(F32)) * flags[0]).astype(BF16)
        out_ref[t, 1 : rows - 1] = (total[1 : rows - 1] + own[at].astype(F32)).astype(BF16)
        out_ref[t, rows - 1] = (
            (total[rows - 1] + down_ref[at, 0].astype(F32)) * flags[1]
        ).astype(BF16)
        return carry

    lax.fori_loop(0, frames, one_out, 0)


def middle(name, flags, stats, weights, pieces, frames, rows, first):
    layout = tuple(tuple(where) for _, *where in pieces)
    _, _, cols, chans = pieces[0][0].shape
    return call(
        functools.partial(mid_kernel, layout, frames, rows, first),
        name,
        jax.ShapeDtypeStruct((frames, rows, cols, chans), BF16),
        [smem()] + vmem(2 + len(pieces)),
        [pltpu.VMEM((frames + 2, rows + 2, cols, 768), BF16)],
        2 * frames * rows * cols * 27 * 65536,
    )(flags, stats, weights, *[a for a, *_ in pieces])


def decode_kernel(layout, frames, weights, *refs):
    sources = refs[: len(layout)]
    out_ref, buffer, wide = refs[len(layout) :]
    chans = sources[0].shape[3]
    cols = sources[0].shape[2]
    rows = out_ref.shape[1] // 2
    outs = out_ref.shape[3]
    fill(
        buffer,
        [(ref, s, n, t0, 0, None) for ref, (s, n, t0) in zip(sources, layout)],
        chans,
        lambda value, keep: value,
    )
    zero = jnp.zeros((chans, 128), BF16)

    def one_out(t, carry):
        for i, taps in enumerate((((0, 3), (1, 1)), ((1, 2), (2, 0)))):
            total = jnp.zeros((rows * cols, 256), F32)
            for dt in range(3):
                for dr, p in taps:
                    w = weights.at[dt, p]
                    pairs = ((w[3], zero), (w[1], w[2]), (zero, w[0]))
                    for dc, pair in enumerate(pairs):
                        lhs = buffer[t + dt, dr : dr + rows, :, 256 * dc : 256 * dc + chans]
                        lhs = lhs.reshape(rows * cols, chans)
                        rhs = jnp.concatenate(pair, axis=-1)
                        total = total + jnp.dot(lhs, rhs, preferred_element_type=F32)
            total = total.reshape(rows, cols, 256)
            for r in range(rows):
                wide[2 * r + i, pl.ds(0, cols, stride=2), :] = total[r, :, 0:128]
                wide[2 * r + i, pl.ds(1, cols, stride=2), :] = total[r, :, 128:256]
        out_ref[t] = wide[:, :, 0:outs].astype(BF16)
        return carry

    lax.fori_loop(0, frames, one_out, 0)


def decode(name, weights, pieces, frames, outs):
    layout = tuple((s, n, t0) for _, s, n, t0 in pieces)
    _, ext, cols, _ = pieces[0][0].shape
    rows = ext - 2
    return call(
        functools.partial(decode_kernel, layout, frames),
        name,
        jax.ShapeDtypeStruct((frames, 2 * rows, 2 * cols, outs), BF16),
        vmem(1 + len(pieces)),
        [
            pltpu.VMEM((frames + 2, rows + 2, cols, 768), BF16),
            pltpu.VMEM((2 * rows, 2 * cols, 128), F32),
        ],
        2 * frames * rows * cols * 36 * 65536,
    )(weights, *[a for a, *_ in pieces])


def moved(block, clip_step, seq_step):
    clips, seqs = lax.axis_size("clip"), lax.axis_size("seq")
    if clip_step == 0:
        route = [(i - seq_step, i) for i in range(seqs) if 0 <= i - seq_step < seqs]
        return lax.ppermute(block, "seq", route)
    if seq_step == 0:
        route = [(i - clip_step, i) for i in range(clips) if 0 <= i - clip_step < clips]
        return lax.ppermute(block, "clip", route)
    route = [
        ((s - seq_step) * clips + c - clip_step, s * clips + c)
        for s in range(seqs)
        for c in range(clips)
        if 0 <= c - clip_step < clips and 0 <= s - seq_step < seqs
    ]
    return lax.ppermute(block, ("seq", "clip"), route)


def from_all(values):
    everyone = lax.axis_size("clip") * lax.axis_size("seq")
    rows = jnp.broadcast_to(values[None], (everyone, values.shape[0]))
    return lax.all_to_all(rows, ("seq", "clip"), 0, 0, tiled=True)


def per_group(channels):
    return channels.reshape(GROUPS, -1).sum(axis=1)


def per_channel(groups, chans):
    return jnp.repeat(groups, chans // GROUPS)


def body(tokens, conv_one, conv_two, pixel_grad):
    frames, height, stripe, chans = tokens.shape
    lines, wide, outs = pixel_grad.shape[1:]
    rows, cols = lines // 2, wide // 2
    clips, seqs = lax.axis_size("clip"), lax.axis_size("seq")
    clip, seq = lax.axis_index("clip"), lax.axis_index("seq")
    flags = jnp.stack([seq != 0, seq != seqs - 1, clip != 0]).astype(F32)

    px_up = moved(pixel_grad[:, lines - 3 :], 0, 1)
    px_down = moved(pixel_grad[:, :3], 0, -1)
    px_z = moved(pixel_grad[:2], -1, 0)
    px_zup = moved(pixel_grad[:2, lines - 3 :], -1, 1)
    px_zdown = moved(pixel_grad[:2, :3], -1, -1)

    own_count = frames * height * stripe * (chans // GROUPS)
    field = tokens.astype(F32)
    own_mean = per_group(jnp.sum(field, axis=(0, 1, 2))) / own_count
    own_spread = per_group(jnp.sum((field - per_channel(own_mean, chans)) ** 2, axis=(0, 1, 2)))
    gathered = from_all(jnp.concatenate([own_mean, own_spread]))
    tile = lax.all_to_all(tokens, "seq", split_axis=1, concat_axis=2, tiled=True)
    means, spreads = gathered[:, :GROUPS], gathered[:, GROUPS:]
    mean = jnp.mean(means, axis=0)
    var = jnp.mean(spreads, axis=0) / own_count + jnp.mean((means - mean) ** 2, axis=0)
    scale = lax.rsqrt(var + 1e-06)
    mean_c, scale_c = per_channel(mean, chans), per_channel(scale, chans)
    stats = jnp.stack([mean_c, scale_c])

    tile_up = moved(tile[:, rows - 2 :], 0, 1)
    tile_down = moved(tile[:, :2], 0, -1)
    tile_z = moved(tile[frames - 2 :], 1, 0)
    tile_zup = moved(tile[frames - 2 :, rows - 2 :], 1, 1)
    tile_zdown = moved(tile[frames - 2 :, :2], 1, -1)

    both = combined_weights(conv_two)

    pieces = [(pixel_grad, 0, 4, 0, 3), (px_up, 0, 4, 0, 0), (px_down, 0, 4, 0, 3 + lines)]
    grad_a = down("down_a", flags, both, pieces, 2, rows + 2, cols, chans)
    grad_z = moved(grad_a, -1, 0)
    pieces = [
        (pixel_grad, 2, 2, 0, 3),
        (px_up, 2, 2, 0, 0),
        (px_down, 2, 2, 0, 3 + lines),
        (px_z, 0, 2, 2, 3),
        (px_zup, 0, 2, 2, 0),
        (px_zdown, 0, 2, 2, 3 + lines),
    ]
    grad_b = down("down_b", flags, both, pieces, 2, rows + 2, cols, chans)
    pieces = [(grad_a, 0, 2, 0), (grad_b, 0, 2, 2), (grad_z, 0, 2, 4)]
    base, sums = back("back", flags, stats, conv_one, tile, pieces, frames, 0)
    spread = lax.all_to_all(base, "seq", split_axis=2, concat_axis=1, tiled=True)
    sums = from_all(jnp.concatenate([per_group(sums[0]), per_group(sums[1])]))

    pieces = [
        (tile, 0, 4, 0, 2, ()),
        (tile_up, 0, 4, 0, 0, (0,)),
        (tile_down, 0, 4, 0, 2 + rows, (1,)),
    ]
    mid_b = middle("mid_b", flags, stats, conv_one, pieces, 2, rows + 2, 2)
    mid_z = moved(mid_b, 1, 0)
    pieces = [
        (tile, 0, 2, 2, 2, ()),
        (tile_up, 0, 2, 2, 0, (0,)),
        (tile_down, 0, 2, 2, 2 + rows, (1,)),
        (tile_z, 0, 2, 0, 2, (2,)),
        (tile_zup, 0, 2, 0, 0, (0, 2)),
        (tile_zdown, 0, 2, 0, 2 + rows, (1, 2)),
    ]
    mid_a = middle("mid_a", flags, stats, conv_one, pieces, 2, rows + 2, 0)
    decoded = decode(
        "decode", both, [(mid_z, 0, 2, 0), (mid_a, 0, 2, 2), (mid_b, 0, 2, 4)], frames, outs
    )

    count = float(own_count * clips * seqs)
    total = jnp.sum(sums, axis=0) / count
    first = per_channel(total[:GROUPS], chans)
    second = per_channel(total[GROUPS:], chans)
    normed = (field - mean_c) * scale_c
    token_grad = (spread.astype(F32) - (first + normed * second) * scale_c).astype(BF16)
    return (decoded, token_grad)


def solution(mesh):
    return jax.shard_map(
        body,
        mesh=mesh,
        in_specs=(P("clip", None, "seq", None), P(), P(), P("clip", "seq", None, None)),
        out_specs=(P("clip", "seq", None, None), P("clip", None, "seq", None)),
        check_vma=False,
    )
```

```python
import functools

import jax
import jax.numpy as jnp
from jax import lax
from jax.experimental import pallas as pl
from jax.experimental.pallas import tpu as pltpu
from jax.sharding import PartitionSpec as P

GROUPS = 32
F32 = jnp.float32
BF16 = jnp.bfloat16
VMEM_LIMIT = 32 * 2**20
TAPS = ((2,), (1, 2), (0, 1), (0,))
EXTRA = 16


def vmem(count):
    return [pl.BlockSpec(memory_space=pltpu.VMEM)] * count


def smem():
    return pl.BlockSpec(memory_space=pltpu.SMEM)


def anywhere():
    return pl.BlockSpec(memory_space=pltpu.HBM)


def call(kernel, name, outs, in_specs, scratch, flops, moved_bytes=4 * 2**20):
    return pl.pallas_call(
        kernel,
        name=name,
        out_shape=outs,
        in_specs=in_specs,
        out_specs=jax.tree.map(lambda _: pl.BlockSpec(memory_space=pltpu.VMEM), outs),
        scratch_shapes=scratch,
        compiler_params=pltpu.CompilerParams(vmem_limit_bytes=VMEM_LIMIT),
        cost_estimate=pl.CostEstimate(flops=flops, bytes_accessed=moved_bytes, transcendentals=0),
    )


def array(shape, dtype=BF16):
    return jax.ShapeDtypeStruct(shape, dtype)


def kept(shape, dtype=BF16):
    return pltpu.VMEM(shape, dtype)


def near(block):
    return pltpu.with_memory_space_constraint(block, pltpu.VMEM)


def far(block):
    return pltpu.with_memory_space_constraint(block, pltpu.HBM)


def dot(lhs, rhs):
    return jnp.dot(lhs, rhs, preferred_element_type=F32)


def nt_dot(lhs, rhs):
    return lax.dot_general(lhs, rhs, (((1,), (1,)), ((), ())), preferred_element_type=F32)


def one_hot(rows, cols, place):
    width = min(cols, 128)
    target = place(lax.broadcasted_iota(jnp.int32, (rows, width), 0))
    target = target - lax.broadcasted_iota(jnp.int32, (rows, width), 1)
    blocks = [
        jnp.where(target == at, 1.0, 0.0).astype(BF16)[:, : cols - at]
        for at in range(0, cols, width)
    ]
    return jnp.concatenate(blocks, axis=1) if len(blocks) > 1 else blocks[0]


def same_group(chans):
    size = chans // GROUPS
    row = lax.broadcasted_iota(jnp.int32, (chans, chans), 0).astype(F32)
    col = lax.broadcasted_iota(jnp.int32, (chans, chans), 1).astype(F32)
    row, col = (jnp.floor((index + 0.5) / size) for index in (row, col))
    return jnp.where(row == col, 1.0, 0.0)


def group_sum(channels):
    return jnp.dot(
        channels,
        same_group(channels.shape[1]),
        precision=lax.Precision.HIGHEST,
        preferred_element_type=F32,
    )


def split_3(value):
    terms = []
    for _ in range(3):
        terms.append(value.astype(BF16).astype(F32))
        value = value - terms[-1]
    return terms


def extra_rows(one, two):
    rest = jnp.concatenate([one[:, 128:], two[:, 128:]], axis=1)
    row = lax.broadcasted_iota(jnp.int32, (EXTRA, 128), 0)
    out = jnp.zeros((EXTRA, 128), F32)
    for n, term in enumerate(split_3(one[:, :128]) + split_3(two[:, :128]) + split_3(rest)):
        out = jnp.where(row == n, term, out)
    return out


def from_extra(block):
    block = block.astype(F32)
    row = lax.broadcasted_iota(jnp.int32, block.shape, 1)
    one, two, rest = (
        jnp.sum(jnp.where((row >= k) & (row < k + 3), block, 0.0), axis=1) for k in (0, 3, 6)
    )
    return (
        jnp.concatenate([one, rest[:, :64]], axis=1),
        jnp.concatenate([two, rest[:, 64:]], axis=1),
    )


def store_dense(ref, frame, value):
    frames = ref.shape[0] * 2 // 3
    lane = 64 * (frame % 2)
    ref[frame] = value[..., :128]
    ref[frames + frame // 2, :, :, lane : lane + 64] = value[..., 128:]


def load_dense(ref, frame):
    frames = ref.shape[0] * 2 // 3
    lane = 64 * (frame % 2)
    return ref[frame], ref[frames + frame // 2, :, :, lane : lane + 64]


def fill(buffer, pieces, transform):
    rows = buffer.shape[1]
    for ref, source, count, t0, later in pieces:

        def one_frame(i, carry):
            for r in range(rows):
                buffer[t0 + i, r] = transform(ref[source + i, r], r, later)
            return carry

        lax.fori_loop(0, count, one_frame, 0)


def from_left(value, cols):
    column = lax.broadcasted_iota(jnp.int32, value.shape, 0) & (cols - 1)
    return jnp.where(column == 0, 0.0, pltpu.roll(value, 1, 0))


def from_right(value, cols):
    size = value.shape[0]
    column = lax.broadcasted_iota(jnp.int32, value.shape, 0) & (cols - 1)
    return jnp.where(column == cols - 1, 0.0, pltpu.roll(value, size - 1, 0))


def fetch(source, target, sem):
    copy = pltpu.make_async_copy(source, target, sem)
    copy.start()
    return copy


def combine_kernel(w_ref, out_ref):
    outs = w_ref.shape[4]

    def one_time(a, carry):
        w = [[w_ref[a, b, d].astype(F32) for d in range(3)] for b in range(3)]
        for p in range(4):
            rows = [functools.reduce(jnp.add, [w[b][d] for b in TAPS[p]]) for d in range(3)]
            for q in range(4):
                value = functools.reduce(jnp.add, [rows[d] for d in TAPS[q]])
                out_ref[a, p, q] = jnp.pad(value, ((0, 0), (0, 128 - outs))).astype(BF16)
        return carry

    lax.fori_loop(0, 3, one_time, 0)


def combined_weights(conv_two):
    shape = kept((3, 4, 4, conv_two.shape[3], 128))
    return call(combine_kernel, "combine_weights", shape, vmem(1), [], 10**6)(conv_two)


def edges_kernel(x_ref, first_ref, last_ref):
    lines = x_ref.shape[1]
    first_ref[...] = x_ref[:, 0:3]
    last_ref[...] = x_ref[:, lines - 3 : lines]


def edges(pixels):
    frames, _, outs, wide = pixels.shape
    shape = array((frames, 3, outs, wide))
    return call(edges_kernel, "edges", (shape, shape), vmem(1), [], 10**6)(pixels)


def moments_kernel(x_ref, out_ref):
    frames, stripe, chans, height = x_ref.shape
    total = jnp.zeros((chans, height), F32)
    for t in range(frames):
        for c in range(stripe):
            total = total + x_ref[t, c].astype(F32)
    mean = jnp.sum(total, axis=1, keepdims=True) / float(frames * stripe * height)
    spread = jnp.zeros((chans, height), F32)
    for t in range(frames):
        for c in range(stripe):
            spread = spread + (x_ref[t, c].astype(F32) - mean) ** 2
    spread = jnp.sum(spread, axis=1, keepdims=True)
    rows = [jnp.broadcast_to(v, (chans, 128)).T[0:1] for v in (mean, spread)]
    out_ref[...] = jnp.broadcast_to(jnp.concatenate(rows, axis=0)[None], out_ref.shape)


def moments(tokens, clips):
    shape = array((clips, 2, tokens.shape[2]), F32)
    return call(moments_kernel, "moments", shape, vmem(1), [], 10**6)(tokens)


def merged(means, spreads, held):
    mean = jnp.sum(means, axis=0, keepdims=True) / means.shape[0]
    spread = jnp.sum(spreads, axis=0, keepdims=True)
    return mean, spread + held * jnp.sum((means - mean) ** 2, axis=0, keepdims=True)


def pack_kernel(held, x_ref, parts_ref, out_ref):
    frames, stripe, chans, height = x_ref.shape
    seqs = out_ref.shape[0]
    rows = height // seqs
    select = one_hot(8 * seqs, height, lambda i: rows * (i >> 3) - 2 + (i & 7))

    def picked(x):
        return nt_dot(select, x).reshape(seqs, 8, 128)

    for n in range(frames // 2):
        pair = [x_ref.at[2 * n + k] for k in range(2)]
        blocks = [[x[c, 0:128] for c in range(stripe)] for x in pair]
        tails = [[x[c, 128:chans] for x in pair] for c in range(stripe)]
        blocks.append([jnp.concatenate(tail, axis=0) for tail in tails])
        for k, columns in enumerate(blocks):
            at = 48 * n + 16 * k
            rows_of = [picked(column) for column in columns]
            out_ref[:, at : at + 16] = jnp.concatenate(rows_of, axis=1).astype(BF16)
    extra = extra_rows(*merged(parts_ref[:, 0], parts_ref[:, 1], held)).astype(BF16)
    out_ref[:, 24 * frames :] = jnp.broadcast_to(extra[None], (seqs, EXTRA, 128))


def pack(tokens, parts, seqs, held):
    shape = array((seqs, 24 * tokens.shape[0] + EXTRA, 128))
    return call(functools.partial(pack_kernel, held), "pack", shape, vmem(2), [], 10**9)(
        tokens, parts
    )


def unpack_kernel(held, x_ref, tile_ref, last_ref, stats_ref):
    seqs = x_ref.shape[0]
    frames, rows, cols, chans = tile_ref.shape
    size = rows * cols

    order = one_hot(size, 16 * seqs, lambda i: ((i >> 1) & 31) * 16 + (i & 1) * 8 + (i >> 6))
    for n in range(frames // 2):
        blocks = [x_ref[:, 48 * n + 16 * k : 48 * n + 16 * (k + 1)] for k in range(3)]
        blocks = [block.reshape(16 * seqs, 128) for block in blocks]
        main = dot(order, jnp.concatenate(blocks[:2], axis=1)).astype(BF16)
        rest = dot(order, blocks[2]).astype(BF16)
        for k in range(2):
            t = 2 * n + k
            for ref, at in ((tile_ref, t), (last_ref, t - frames + 2)):
                if at >= 0:
                    part = main[:, 128 * k : 128 * (k + 1)]
                    ref[at, :, :, 0:128] = part.reshape(rows, cols, 128)
                    part = rest[:, 64 * k : 64 * (k + 1)]
                    ref[at, :, :, 128:chans] = part.reshape(rows, cols, 64)
    size = chans // GROUPS
    means, spreads = from_extra(x_ref[:, 24 * frames :])
    mean = group_sum(jnp.broadcast_to(jnp.sum(means, axis=0, keepdims=True), (8, chans)))
    mean = mean[0:1] / (seqs * size)
    spread = jnp.sum(spreads, axis=0, keepdims=True)
    spread = spread + held * jnp.sum((means - mean) ** 2, axis=0, keepdims=True)
    var = group_sum(jnp.broadcast_to(spread, (8, chans)))[0:1] / (held * seqs * size)
    stats_ref[...] = jnp.concatenate([mean, lax.rsqrt(var + 1e-06)], axis=0)


def unpack(blocks, frames, cols, chans, held):
    return call(
        functools.partial(unpack_kernel, held),
        "unpack",
        (
            kept((frames, 8, cols, chans)),
            kept((2, 8, cols, chans)),
            kept((2, chans), F32),
        ),
        vmem(1),
        [],
        10**9,
    )(blocks)


def down_kernel(first, plan, weights, flags, pixels, above, below, store, buffer):
    _, _, cols, _ = buffer.shape[1:]
    rows, outs = buffer.shape[2] - 1, weights.shape[3]
    chans, wide = pixels.shape[2:]
    select = one_hot(2 * cols, wide, lambda i: 2 * (i & (cols - 1)) + (i // cols))
    blank = jnp.zeros((128 - chans, wide), BF16)

    def one_frame(i, carry):
        at = first + i
        lines = [above.at[at, r] for r in range(3)]
        lines += [pixels.at[at, r] for r in range(pixels.shape[1])]
        lines += [below.at[at, r] for r in range(3)]
        for n in range(0, len(lines), 2):
            pair = [lines[n][...], blank, lines[n + 1][...], blank]
            picked = nt_dot(select, jnp.concatenate(pair, axis=0)).astype(BF16)
            for k in range(2):
                for j in range(2):
                    buffer[i, k, n // 2, :, 128 * j : 128 * (j + 1)] = picked[
                        cols * j : cols * (j + 1), 128 * k : 128 * (k + 1)
                    ]
        return carry

    lax.fori_loop(0, buffer.shape[0], one_frame, 0)

    size = rows * cols

    def products(frame, count, a, totals):
        here, left, right = totals
        frames = slice(frame - first, frame - first + count)
        lines = [
            buffer[frames, p % 2, p // 2 : p // 2 + rows].reshape(count * size, 256)
            for p in range(4)
        ]
        w = weights.at[a]
        for p in range(4):
            here = here + nt_dot(lines[p], jnp.concatenate([w[p, 1], w[p, 2]], axis=-1))
        for p in range(0, 4, 2):
            odd = jnp.concatenate([lines[p][:, 128:], lines[p + 1][:, 128:]], axis=-1)
            left = left + nt_dot(odd, jnp.concatenate([w[p, 0], w[p + 1, 0]], axis=-1))
            even = jnp.concatenate([lines[p][:, :128], lines[p + 1][:, :128]], axis=-1)
            right = right + nt_dot(even, jnp.concatenate([w[p, 3], w[p + 1, 3]], axis=-1))
        return here, left, right

    def zeros(count):
        return [jnp.zeros((count * size, outs), F32) for _ in range(3)]

    for n, (terms, extra, member) in enumerate(plan):
        totals = zeros(2)
        for frame, a in terms:
            totals = products(frame, 2, a, totals)
        here, left, right = totals
        total = here + from_left(left, cols) + from_right(right, cols)
        parts = [total[:size], total[size:]]
        if extra:
            here, left, right = products(*extra[:1], 1, *extra[1:], zeros(1))
            more = here + from_left(left, cols) + from_right(right, cols)
            parts[member] = parts[member] + more
        for k, part in enumerate(parts):
            part = part.reshape(rows, cols, outs)
            store(
                2 * n + k,
                [part[0:1] * flags[0], part[1 : rows - 1], part[rows - 1 :] * flags[1]],
            )


def early_kernel(plan, weights, flags, pixels, above, below, own_ref, sent_ref, buffer):
    def store(n, parts):
        value = jnp.concatenate([part.astype(BF16) for part in parts], axis=0)
        store_dense(sent_ref, n, value)
        if n < 2:
            own_ref[n] = value

    down_kernel(0, plan, weights, flags, pixels, above, below, store, buffer)


def late_kernel(first, plan, one_hbm, weights, flags, pixels, above, below, *refs):
    out_ref, one_ref, buffer, sem = refs
    copy = pltpu.make_async_copy(one_hbm, one_ref, sem)
    copy.start()

    def store(n, parts):
        out_ref[n] = jnp.concatenate(parts, axis=0)

    down_kernel(first, plan, weights, flags, pixels, above, below, store, buffer)
    copy.wait()


def down_cost(plan, size):
    return 2 * sum(2 * len(terms) + 1 for terms, *_ in plan) * size * 8 * 65536


def down_early(weights, flags, pixels, above, below, rows, cols):
    frames, outs = pixels.shape[0], weights.shape[3]
    plan = ((((0, 2), (1, 1), (2, 0)), (), 0), (((0, 0),), (0, 1), 1))
    return call(
        functools.partial(early_kernel, plan),
        "down_early",
        (kept((2, rows, cols, outs)), array((6, rows, cols, 128))),
        vmem(1) + [smem()] + vmem(3),
        [pltpu.VMEM((frames, 2, rows + 1, cols, 256), BF16)],
        down_cost(plan, rows * cols),
    )(weights, flags, pixels, above, below)


def down_late(conv_one, weights, flags, pixels, above, below, rows, cols):
    frames, outs = pixels.shape[0], weights.shape[3]
    plan = ((((2, 2),), (3, 1), 0),)
    return call(
        functools.partial(late_kernel, frames - 2, plan),
        "down_late",
        (kept((2, rows, cols, outs), F32), kept(conv_one.shape)),
        [anywhere()] + vmem(1) + [smem()] + vmem(3),
        [pltpu.VMEM((2, 2, rows + 1, cols, 256), BF16), pltpu.SemaphoreType.DMA],
        down_cost(plan, rows * cols),
    )(far(conv_one), weights, flags, pixels, above, below)


def back_kernel(stats, weights, tile_ref, early_ref, late_ref, next_ref, out_ref, buffer, rest):
    seqs = out_ref.shape[0]
    frames, _, cols, chans = tile_ref.shape
    rows = buffer.shape[1] - 2
    size = 2 * rows * cols
    for k in range(2):
        buffer[k] = early_ref[k]
        main, tail = load_dense(next_ref, k)
        buffer[frames + k, :, :, 0:128] = main
        buffer[frames + k, :, :, 128:chans] = tail
        main, tail = load_dense(next_ref, 2 + k)
        late = late_ref[k]
        main = (late[..., :128] + main.astype(F32)).astype(BF16)
        tail = (late[..., 128:] + tail.astype(F32)).astype(BF16)
        buffer[frames - 2 + k, :, :, 0:128] = main
        buffer[frames - 2 + k, :, :, 128:chans] = tail
    mean = stats[0:1]
    scale = stats[1:2]
    order = one_hot(
        size,
        size,
        lambda i: ((i >> 3) & 1) * (rows * cols) + (i & 3) * cols + 2 * (i >> 4) + ((i >> 2) & 1),
    )

    def two_frames(n, carry):
        first_sum, second_sum = carry
        t = 2 * n
        total = [jnp.zeros((size, chans), F32) for _ in range(3)]
        for dt in range(3):
            for dr in range(3):
                lhs = buffer[pl.ds(t + dt, 2), dr : dr + rows].reshape(size, chans)
                for dc in range(3):
                    total[dc] = total[dc] + nt_dot(lhs, weights[2 - dt, 2 - dr, 2 - dc])
        total = total[1] + from_left(total[0], cols) + from_right(total[2], cols)
        tile = tile_ref[pl.ds(t, 2), 2 : 2 + rows].reshape(size, chans)
        normed = (tile.astype(F32) - mean) * scale
        sigmoid = 1.0 / (1.0 + jnp.exp(-normed))
        grad = total * sigmoid * (1.0 + normed * (1.0 - sigmoid))
        first_sum = first_sum + jnp.sum(grad, axis=0, keepdims=True)
        second_sum = second_sum + jnp.sum(grad * normed, axis=0, keepdims=True)
        own = buffer[pl.ds(t, 2), 1 : 1 + rows].reshape(size, chans)
        base = (own.astype(F32) + grad * scale).astype(BF16)
        home = dot(order, base)
        main = home[:, :128].reshape(seqs, 16, 128).astype(BF16)
        out_ref[:, pl.ds(pl.multiple_of(16 * n, 16), 16)] = main
        tail = home[:, 128:].reshape(seqs, 2, 8, chans - 128)
        for k in range(2):
            rest[n, :, :, 64 * k : 64 * (k + 1)] = tail[:, k]
        return first_sum, second_sum

    none = jnp.zeros((1, chans), F32)
    sums = lax.fori_loop(0, frames // 2, two_frames, (none, none))
    both = jnp.concatenate([rest[n] for n in range(frames // 2)], axis=1)
    out_ref[:, 8 * frames : 12 * frames] = both.astype(BF16)
    extra = extra_rows(*sums).astype(BF16)
    out_ref[:, 12 * frames :] = jnp.broadcast_to(extra[None], (seqs, EXTRA, 128))


def back(stats, weights, tile, early, late, following, seqs):
    frames = tile.shape[0]
    _, ext, cols, chans = early.shape
    return call(
        back_kernel,
        "back",
        array((seqs, 12 * frames + EXTRA, 128)),
        vmem(6),
        [
            pltpu.VMEM((frames + 2, ext, cols, chans), BF16),
            pltpu.VMEM((frames // 2, seqs, 8, 128), F32),
        ],
        2 * frames * (ext - 2) * cols * 27 * 65536,
    )(stats, weights, tile, early, late, following)


def sums_kernel(x_ref, out_ref):
    one, two = from_extra(x_ref[...])
    sums = [jnp.sum(v, axis=0, keepdims=True) for v in (one, two)]
    out_ref[...] = jnp.broadcast_to(jnp.concatenate(sums, axis=0)[None], out_ref.shape)


def local_sums(blocks, frames, chans, clips):
    seqs = blocks.shape[0]
    at = 12 * frames // EXTRA
    return pl.pallas_call(
        sums_kernel,
        name="local_sums",
        grid=(1,),
        out_shape=array((clips, 2, chans), F32),
        in_specs=[pl.BlockSpec((seqs, EXTRA, 128), lambda i: (0, at, 0))],
        out_specs=pl.BlockSpec((clips, 2, chans), lambda i: (0, 0, 0)),
        compiler_params=pltpu.CompilerParams(vmem_limit_bytes=VMEM_LIMIT),
        cost_estimate=pl.CostEstimate(flops=10**6, bytes_accessed=10**5, transcendentals=0),
    )(blocks)


def token_kernel(count, x_ref, tokens_ref, stats_ref, parts_ref, out_ref):
    frames, stripe, chans, height = tokens_ref.shape
    seqs = x_ref.shape[0]
    sums = jnp.sum(parts_ref[...], axis=0)
    sums = group_sum(jnp.concatenate([sums, jnp.zeros((6, chans), F32)], axis=0)) / count
    first, second = (jnp.broadcast_to(sums[k : k + 1], (128, chans)).T for k in range(2))
    mean, scale = (jnp.broadcast_to(stats_ref[k : k + 1], (128, chans)).T for k in range(2))
    eye = one_hot(128, 128, lambda i: i)
    lanes = 16 * seqs

    order = one_hot(lanes, lanes, lambda i: ((i >> 2) & 3) * height + (i >> 4) * 4 + (i & 3))

    def turned(at):
        block = x_ref[:, at : at + 16].reshape(lanes, 128)
        return dot(nt_dot(eye, block).astype(BF16), order)

    rest = turned(8 * frames)
    for n in range(frames // 2):
        main = turned(16 * n)
        for k in range(2 * stripe):
            t, c = 2 * n + k // stripe, k % stripe
            at = stripe * n + c
            base = jnp.concatenate(
                [
                    main[:, height * k : height * (k + 1)],
                    rest[64 * (k // stripe) : 64 * (k // stripe + 1), height * at : height * (at + 1)],
                ],
                axis=0,
            )
            normed = (tokens_ref[t, c].astype(F32) - mean) * scale
            out_ref[t, c] = (base - (first + normed * second) * scale).astype(BF16)


def token_gradient(blocks, tokens, stats, parts, count):
    return call(
        functools.partial(token_kernel, count),
        "token_gradient",
        array(tokens.shape),
        vmem(4),
        [],
        10**9,
    )(blocks, tokens, stats, parts)


def fetch(source, target, sems):
    copies = [pltpu.make_async_copy(source.at[k], target.at[k], sems.at[k]) for k in range(3)]
    for copy in copies:
        copy.start()
    return copies


def mid_kernel(flags, stats, w_hbm, tile_ref, before_ref, out_ref, sent_ref, buffer, weights, sems):
    copies = fetch(w_hbm, weights, sems)
    frames, rows, cols, chans = out_ref.shape
    size = 2 * rows * cols
    mean = stats[0:1]
    scale = stats[1:2]

    def activate(value, row, later):
        normed = (value.astype(F32) - mean) * scale
        act = normed / (1.0 + jnp.exp(-normed))
        if row < 2:
            act = act * flags[0]
        if row >= rows:
            act = act * flags[1]
        if later:
            act = act * flags[2]
        return act.astype(BF16)

    fill(buffer, [(before_ref, 0, 2, 0, True), (tile_ref, 0, frames, 2, False)], activate)
    for copy in copies:
        copy.wait()

    def two_frames(n, carry):
        t = 2 * n
        total = [jnp.zeros((size, chans), F32) for _ in range(3)]
        for dt in range(3):
            for dr in range(3):
                lhs = buffer[pl.ds(t + dt, 2), dr : dr + rows].reshape(size, chans)
                for dc in range(3):
                    total[dc] = total[dc] + dot(lhs, weights[dt, dr, dc])
        total = total[1] + from_left(total[0], cols) + from_right(total[2], cols)
        total = total.reshape(2, rows, cols, chans)
        total = total + tile_ref[pl.ds(t, 2), 1 : 1 + rows].astype(F32)
        out_ref[pl.ds(t, 2), 0:1] = (total[:, 0:1] * flags[0]).astype(BF16)
        out_ref[pl.ds(t, 2), 1 : rows - 1] = total[:, 1 : rows - 1].astype(BF16)
        out_ref[pl.ds(t, 2), rows - 1 : rows] = (total[:, rows - 1 :] * flags[1]).astype(BF16)
        return carry

    lax.fori_loop(0, frames // 2, two_frames, 0)
    for k in range(2):
        store_dense(sent_ref, k, out_ref[frames - 2 + k])


def middle(flags, stats, weights, tile, before):
    frames, ext, cols, chans = tile.shape
    rows = ext - 2
    return call(
        mid_kernel,
        "middle",
        (kept((frames, rows, cols, chans)), array((3, rows, cols, 128))),
        [smem()] + vmem(1) + [anywhere()] + vmem(2),
        [
            pltpu.VMEM((frames + 2, ext, cols, chans), BF16),
            pltpu.VMEM(weights.shape, BF16),
            pltpu.SemaphoreType.DMA((3,)),
        ],
        2 * frames * rows * cols * 27 * 65536,
    )(flags, stats, far(weights), tile, before)


def decode_kernel(w_hbm, before_ref, mid_ref, out_ref, buffer, wide, weights, sems):
    copies = fetch(w_hbm, weights, sems)
    frames, _, cols, chans = mid_ref.shape
    lines, outs, _ = out_ref.shape[1:]
    rows = lines // 2
    for k in range(2):
        main, tail = load_dense(before_ref, k)
        buffer[k, :, :, 0:128] = main
        buffer[k, :, :, 128:chans] = tail
    buffer[2:] = mid_ref[...]
    eye = one_hot(outs, 128, lambda i: i)
    size = 2 * rows * cols

    for t in range(0, frames, 2):
        for i, taps in enumerate((((0, 3), (1, 1)), ((1, 2), (2, 0)))):
            here, aside = (jnp.zeros((size, 256), F32) for _ in range(2))
            for dt in range(3):
                if t + i == 0:
                    copies[dt].wait()
                for dr, p in taps:
                    w = weights.at[dt, p]
                    lhs = buffer[t + dt : t + dt + 2, dr : dr + rows].reshape(size, chans)
                    here = here + dot(lhs, jnp.concatenate([w[1], w[2]], axis=-1))
                    aside = aside + dot(lhs, jnp.concatenate([w[3], w[0]], axis=-1))
            even = (here[:, :128] + from_left(aside[:, :128], cols)).reshape(2, rows, cols, 128)
            odd = (here[:, 128:] + from_right(aside[:, 128:], cols)).reshape(2, rows, cols, 128)
            for k in range(2):
                for r in range(rows):
                    wide[k, 2 * r + i, pl.ds(0, cols, stride=2), :] = even[k, r]
                    wide[k, 2 * r + i, pl.ds(1, cols, stride=2), :] = odd[k, r]
        for k in range(2):
            for r in range(rows):
                pair = wide[k, 2 * r : 2 * r + 2].reshape(4 * cols, 128).astype(BF16)
                turned = nt_dot(eye, pair).astype(BF16)
                out_ref[t + k, 2 * r] = turned[:, 0 : 2 * cols]
                out_ref[t + k, 2 * r + 1] = turned[:, 2 * cols :]


def decode(weights, before, mid, outs):
    frames, ext, cols, chans = mid.shape
    rows = ext - 2
    return call(
        decode_kernel,
        "decode",
        array((frames, 2 * rows, outs, 2 * cols)),
        [anywhere()] + vmem(2),
        [
            pltpu.VMEM((frames + 2, ext, cols, chans), BF16),
            pltpu.VMEM((2, 2 * rows, 2 * cols, 128), F32),
            pltpu.VMEM(weights.shape, BF16),
            pltpu.SemaphoreType.DMA((3,)),
        ],
        2 * frames * rows * cols * 24 * 65536,
    )(far(weights), before, mid)


def moved(block, clip_step, seq_step):
    clips, seqs = lax.axis_size("clip"), lax.axis_size("seq")
    if clip_step == 0:
        route = [(i - seq_step, i) for i in range(seqs) if 0 <= i - seq_step < seqs]
        return lax.ppermute(block, "seq", route)
    if seq_step == 0:
        route = [(i - clip_step, i) for i in range(clips) if 0 <= i - clip_step < clips]
        return lax.ppermute(block, "clip", route)
    route = [
        ((s - seq_step) * clips + c - clip_step, s * clips + c)
        for s in range(seqs)
        for c in range(clips)
        if 0 <= c - clip_step < clips and 0 <= s - seq_step < seqs
    ]
    return lax.ppermute(block, ("seq", "clip"), route)


def exchanged(blocks, axis):
    return lax.all_to_all(blocks, axis, 0, 0, tiled=True)


def body(tokens, conv_one, conv_two, pixel_grad):
    frames, height, stripe, chans = tokens.shape
    lines, wide, outs = pixel_grad.shape[1:]
    rows, cols = lines // 2, wide // 2
    clips, seqs = lax.axis_size("clip"), lax.axis_size("seq")
    clip, seq = lax.axis_index("clip"), lax.axis_index("seq")
    flags = jnp.stack([seq != 0, seq != seqs - 1, clip != 0]).astype(F32)
    tokens = tokens.transpose(0, 2, 3, 1)
    pixels = pixel_grad.transpose(0, 1, 3, 2)
    held = float(frames * height * stripe)

    own_parts = moments(tokens, clips)
    pixels, own_parts = lax.optimization_barrier((pixels, own_parts))
    parts = exchanged(own_parts, "clip")
    first, last = edges(pixels)
    above, below = moved(last, 0, 1), moved(first, 0, -1)
    packed = pack(tokens, parts, seqs, held)
    both = combined_weights(conv_two)
    above, below, both, packed = lax.optimization_barrier((above, below, both, packed))

    blocks = exchanged(packed, "seq")
    early, sent = down_early(near(both), flags, pixels, above, below, rows + 2, cols)
    following = moved(sent, -1, 0)
    early = near(early)
    tile, tile_last, stats = unpack(blocks, frames, cols, chans, held * clips)
    tile_z = moved(tile_last, 1, 0)
    above, below, tile = lax.optimization_barrier((above, below, tile))
    tile, stats = near(tile), near(stats)

    late, near_one = down_late(conv_one, near(both), flags, pixels, above, below, rows + 2, cols)
    blocks = back(stats, near(near_one), tile, early, near(late), following, seqs)
    home = exchanged(blocks, "seq")

    mid, mid_last = middle(flags, stats, conv_one, tile, tile_z)
    decoded = decode(both, moved(mid_last, 1, 0), near(mid), outs)

    sums = exchanged(local_sums(home, frames, chans, clips), "clip")
    sums, decoded = lax.optimization_barrier((sums, decoded))
    count = held * seqs * clips * (chans // GROUPS)
    token_grad = token_gradient(home, tokens, stats, sums, count)
    return (decoded.transpose(0, 1, 3, 2), token_grad.transpose(0, 3, 1, 2))


def solution(mesh):
    return jax.shard_map(
        body,
        mesh=mesh,
        in_specs=(P("clip", None, "seq", None), P(), P(), P("clip", "seq", None, None)),
        out_specs=(P("clip", "seq", None, None), P("clip", None, "seq", None)),
        check_vma=False,
    )
```

```python
import functools

import jax
import jax.numpy as jnp
from jax import lax
from jax.experimental import pallas as pl
from jax.experimental.pallas import tpu as pltpu
from jax.sharding import PartitionSpec as P

GROUPS = 32
F32 = jnp.float32
BF16 = jnp.bfloat16
VMEM_LIMIT = 32 * 2**20
TAPS = ((2,), (1, 2), (0, 1), (0,))
EXTRA = 16


def vmem(count):
    return [pl.BlockSpec(memory_space=pltpu.VMEM)] * count


def smem():
    return pl.BlockSpec(memory_space=pltpu.SMEM)


def anywhere():
    return pl.BlockSpec(memory_space=pltpu.HBM)


def call(kernel, name, outs, in_specs, scratch, flops, moved_bytes=4 * 2**20):
    return pl.pallas_call(
        kernel,
        name=name,
        out_shape=outs,
        in_specs=in_specs,
        out_specs=jax.tree.map(lambda _: pl.BlockSpec(memory_space=pltpu.VMEM), outs),
        scratch_shapes=scratch,
        compiler_params=pltpu.CompilerParams(vmem_limit_bytes=VMEM_LIMIT),
        cost_estimate=pl.CostEstimate(flops=flops, bytes_accessed=moved_bytes, transcendentals=0),
    )


def array(shape, dtype=BF16):
    return jax.ShapeDtypeStruct(shape, dtype)


def kept(shape, dtype=BF16):
    return pltpu.VMEM(shape, dtype)


def near(block):
    return pltpu.with_memory_space_constraint(block, pltpu.VMEM)


def far(block):
    return pltpu.with_memory_space_constraint(block, pltpu.HBM)


def dot(lhs, rhs):
    return jnp.dot(lhs, rhs, preferred_element_type=F32)


def nt_dot(lhs, rhs):
    return lax.dot_general(lhs, rhs, (((1,), (1,)), ((), ())), preferred_element_type=F32)


def one_hot(rows, cols, place):
    width = min(cols, 128)
    target = place(lax.broadcasted_iota(jnp.int32, (rows, width), 0))
    target = target - lax.broadcasted_iota(jnp.int32, (rows, width), 1)
    blocks = [
        jnp.where(target == at, 1.0, 0.0).astype(BF16)[:, : cols - at]
        for at in range(0, cols, width)
    ]
    return jnp.concatenate(blocks, axis=1) if len(blocks) > 1 else blocks[0]


def same_group(chans):
    size = chans // GROUPS
    row = lax.broadcasted_iota(jnp.int32, (chans, chans), 0).astype(F32)
    col = lax.broadcasted_iota(jnp.int32, (chans, chans), 1).astype(F32)
    row, col = (jnp.floor((index + 0.5) / size) for index in (row, col))
    return jnp.where(row == col, 1.0, 0.0)


def group_sum(channels):
    return jnp.dot(
        channels,
        same_group(channels.shape[1]),
        precision=lax.Precision.HIGHEST,
        preferred_element_type=F32,
    )


def split_3(value):
    terms = []
    for _ in range(3):
        terms.append(value.astype(BF16).astype(F32))
        value = value - terms[-1]
    return terms


def extra_rows(one, two):
    rest = jnp.concatenate([one[:, 128:], two[:, 128:]], axis=1)
    row = lax.broadcasted_iota(jnp.int32, (EXTRA, 128), 0)
    out = jnp.zeros((EXTRA, 128), F32)
    for n, term in enumerate(split_3(one[:, :128]) + split_3(two[:, :128]) + split_3(rest)):
        out = jnp.where(row == n, term, out)
    return out


def from_extra(block):
    block = block.astype(F32)
    row = lax.broadcasted_iota(jnp.int32, block.shape, 1)
    one, two, rest = (
        jnp.sum(jnp.where((row >= k) & (row < k + 3), block, 0.0), axis=1) for k in (0, 3, 6)
    )
    return (
        jnp.concatenate([one, rest[:, :64]], axis=1),
        jnp.concatenate([two, rest[:, 64:]], axis=1),
    )


def store_dense(ref, frame, value):
    frames = ref.shape[0] * 2 // 3
    lane = 64 * (frame % 2)
    ref[frame] = value[..., :128]
    ref[frames + frame // 2, :, :, lane : lane + 64] = value[..., 128:]


def load_dense(ref, frame):
    frames = ref.shape[0] * 2 // 3
    lane = 64 * (frame % 2)
    return ref[frame], ref[frames + frame // 2, :, :, lane : lane + 64]


def from_left(value, cols):
    column = lax.broadcasted_iota(jnp.int32, value.shape, 0) & (cols - 1)
    return jnp.where(column == 0, 0.0, pltpu.roll(value, 1, 0))


def from_right(value, cols):
    size = value.shape[0]
    column = lax.broadcasted_iota(jnp.int32, value.shape, 0) & (cols - 1)
    return jnp.where(column == cols - 1, 0.0, pltpu.roll(value, size - 1, 0))


def fetch(source, target, sem):
    copy = pltpu.make_async_copy(source, target, sem)
    copy.start()
    return copy


def combine_kernel(w_ref, out_ref):
    outs = w_ref.shape[4]

    def one_time(a, carry):
        w = [[w_ref[a, b, d].astype(F32) for d in range(3)] for b in range(3)]
        for p in range(4):
            rows = [functools.reduce(jnp.add, [w[b][d] for b in TAPS[p]]) for d in range(3)]
            for q in range(4):
                value = functools.reduce(jnp.add, [rows[d] for d in TAPS[q]])
                out_ref[a, p, q] = jnp.pad(value, ((0, 0), (0, 128 - outs))).astype(BF16)
        return carry

    lax.fori_loop(0, 3, one_time, 0)


def combined_weights(conv_two):
    shape = kept((3, 4, 4, conv_two.shape[3], 128))
    return call(combine_kernel, "combine_weights", shape, vmem(1), [], 10**6)(conv_two)


def edges_kernel(x_hbm, first_hbm, last_hbm, near_ref, sems):
    lines = x_hbm.shape[1]
    ends = ((0, first_hbm), (lines - 3, last_hbm))
    for k, (at, _) in enumerate(ends):
        pltpu.make_async_copy(x_hbm.at[:, pl.ds(at, 3)], near_ref.at[k], sems.at[0, k]).start()
    copies = []
    for k, (at, ref) in enumerate(ends):
        pltpu.make_async_copy(x_hbm.at[:, pl.ds(at, 3)], near_ref.at[k], sems.at[0, k]).wait()
        copies.append(pltpu.make_async_copy(near_ref.at[k], ref, sems.at[1, k]))
        copies[k].start()
    for copy in copies:
        copy.wait()


def edges(pixels):
    frames, _, outs, wide = pixels.shape
    shape = pltpu.HBM((frames, 3, outs, wide), BF16)
    return pl.pallas_call(
        edges_kernel,
        name="edges",
        out_shape=(shape, shape),
        in_specs=[anywhere()],
        out_specs=(anywhere(), anywhere()),
        scratch_shapes=[
            pltpu.VMEM((2, *shape.shape), BF16),
            pltpu.SemaphoreType.DMA((2, 2)),
        ],
        cost_estimate=pl.CostEstimate(flops=10**6, bytes_accessed=10**6, transcendentals=0),
    )(far(pixels))


def own_moments(x_ref):
    frames, stripe, chans, height = x_ref.shape
    total = jnp.zeros((chans, height), F32)
    for t in range(frames):
        for c in range(stripe):
            total = total + x_ref[t, c].astype(F32)
    mean = jnp.sum(total, axis=1, keepdims=True) / float(frames * stripe * height)
    spread = jnp.zeros((chans, height), F32)
    for t in range(frames):
        for c in range(stripe):
            spread = spread + (x_ref[t, c].astype(F32) - mean) ** 2
    spread = jnp.sum(spread, axis=1, keepdims=True)
    return [jnp.broadcast_to(v, (chans, 128)).T[0:1] for v in (mean, spread)]


def merged(means, spreads, held):
    mean = jnp.sum(means, axis=0, keepdims=True) / means.shape[0]
    spread = jnp.sum(spreads, axis=0, keepdims=True)
    return mean, spread + held * jnp.sum((means - mean) ** 2, axis=0, keepdims=True)


def pack_kernel(x_ref, out_ref):
    frames, stripe, chans, height = x_ref.shape
    seqs = out_ref.shape[0]
    rows = height // seqs
    select = one_hot(8 * seqs, height, lambda i: rows * (i >> 3) - 2 + (i & 7))

    def picked(x):
        return nt_dot(select, x).reshape(seqs, 8, 128)

    for n in range(frames // 2):
        pair = [x_ref.at[2 * n + k] for k in range(2)]
        blocks = [[x[c, 0:128] for c in range(stripe)] for x in pair]
        tails = [[x[c, 128:chans] for x in pair] for c in range(stripe)]
        blocks.append([jnp.concatenate(tail, axis=0) for tail in tails])
        for k, columns in enumerate(blocks):
            at = 48 * n + 16 * k
            rows_of = [picked(column) for column in columns]
            out_ref[:, at : at + 16] = jnp.concatenate(rows_of, axis=1).astype(BF16)
    extra = extra_rows(*own_moments(x_ref)).astype(BF16)
    out_ref[:, 24 * frames :] = jnp.broadcast_to(extra[None], (seqs, EXTRA, 128))


def pack(tokens, seqs):
    shape = pltpu.HBM((seqs, 24 * tokens.shape[0] + EXTRA, 128), BF16)
    return call(pack_kernel, "pack", shape, vmem(1), [], 10**9)(tokens)


def unpack_kernel(held, x_ref, tile_ref, last_ref, parts_ref):
    seqs = x_ref.shape[0]
    frames, rows, cols, chans = tile_ref.shape
    size = rows * cols

    order = one_hot(size, 16 * seqs, lambda i: ((i >> 1) & 31) * 16 + (i & 1) * 8 + (i >> 6))
    for n in range(frames // 2):
        blocks = [x_ref[:, 48 * n + 16 * k : 48 * n + 16 * (k + 1)] for k in range(3)]
        blocks = [block.reshape(16 * seqs, 128) for block in blocks]
        main = dot(order, jnp.concatenate(blocks[:2], axis=1)).astype(BF16)
        rest = dot(order, blocks[2]).astype(BF16)
        for k in range(2):
            t = 2 * n + k
            for ref, at in ((tile_ref, t), (last_ref, t - frames + 2)):
                if at >= 0:
                    part = main[:, 128 * k : 128 * (k + 1)]
                    ref[at, :, :, 0:128] = part.reshape(rows, cols, 128)
                    part = rest[:, 64 * k : 64 * (k + 1)]
                    ref[at, :, :, 128:chans] = part.reshape(rows, cols, 64)
    parts = merged(*from_extra(x_ref[:, 24 * frames :]), held)
    parts_ref[...] = jnp.broadcast_to(jnp.concatenate(parts, axis=0)[None], parts_ref.shape)


def unpack(blocks, frames, cols, chans, clips, held):
    return call(
        functools.partial(unpack_kernel, held),
        "unpack",
        (
            pltpu.HBM((frames, 8, cols, chans), BF16),
            pltpu.HBM((2, 8, cols, chans), BF16),
            pltpu.HBM((clips, 2, chans), F32),
        ),
        vmem(1),
        [],
        10**9,
    )(blocks)


def stats_kernel(held, parts_ref, stats_ref):
    clips, _, chans = parts_ref.shape
    means, spreads = parts_ref[:, 0], parts_ref[:, 1]
    size = chans // GROUPS
    mean = group_sum(jnp.broadcast_to(jnp.sum(means, axis=0, keepdims=True), (8, chans)))
    mean = mean[0:1] / (clips * size)
    spread = jnp.sum(spreads, axis=0, keepdims=True)
    spread = spread + held * jnp.sum((means - mean) ** 2, axis=0, keepdims=True)
    var = group_sum(jnp.broadcast_to(spread, (8, chans)))[0:1] / (held * clips * size)
    stats_ref[...] = jnp.concatenate([mean, lax.rsqrt(var + 1e-06)], axis=0)


def group_stats(parts, held):
    shape = kept(parts.shape[1:], F32)
    kernel = functools.partial(stats_kernel, held)
    return call(kernel, "group_stats", shape, vmem(1), [], 10**6)(parts)


def down_kernel(first, plan, weights, flags, sources, store, buffer, beside, sems):
    _, _, cols, _ = buffer.shape[1:]
    rows, outs = buffer.shape[2] - 1, weights.shape[3]
    pixels, *sides = sources
    count = buffer.shape[0]
    lines, chans, wide = pixels.shape[1:]
    copies = [
        pltpu.make_async_copy(side.at[pl.ds(first, count)], beside.at[k], sems.at[k])
        for k, side in enumerate(sides)
    ]
    for copy in copies:
        copy.start()
    select = one_hot(2 * cols, wide, lambda i: 2 * (i & (cols - 1)) + (i // cols))
    blank = jnp.zeros((128 - chans, wide), BF16)

    def line(i, n):
        if 3 <= n < 3 + lines:
            return pixels[first + i, n - 3]
        return beside[0, i, n] if n < 3 else beside[1, i, n - 3 - lines]

    def place(inner):
        def one_frame(i, carry):
            for n in range(0, lines + 6, 2):
                if (3 < n < 2 + lines) == inner:
                    pair = [line(i, n), blank, line(i, n + 1), blank]
                    picked = nt_dot(select, jnp.concatenate(pair, axis=0)).astype(BF16)
                    for k in range(2):
                        for j in range(2):
                            buffer[i, k, n // 2, :, 128 * j : 128 * (j + 1)] = picked[
                                cols * j : cols * (j + 1), 128 * k : 128 * (k + 1)
                            ]
            return carry

        lax.fori_loop(0, count, one_frame, 0)

    place(True)
    for copy in copies:
        copy.wait()
    place(False)

    size = rows * cols

    def products(frame, count, a, totals):
        here, left, right = totals
        frames = slice(frame - first, frame - first + count)
        lines = [
            buffer[frames, p % 2, p // 2 : p // 2 + rows].reshape(count * size, 256)
            for p in range(4)
        ]
        w = weights.at[a]
        for p in range(4):
            here = here + nt_dot(lines[p], jnp.concatenate([w[p, 1], w[p, 2]], axis=-1))
        for p in range(0, 4, 2):
            odd = jnp.concatenate([lines[p][:, 128:], lines[p + 1][:, 128:]], axis=-1)
            left = left + nt_dot(odd, jnp.concatenate([w[p, 0], w[p + 1, 0]], axis=-1))
            even = jnp.concatenate([lines[p][:, :128], lines[p + 1][:, :128]], axis=-1)
            right = right + nt_dot(even, jnp.concatenate([w[p, 3], w[p + 1, 3]], axis=-1))
        return here, left, right

    def zeros(count):
        return [jnp.zeros((count * size, outs), F32) for _ in range(3)]

    for n, (terms, extra, member) in enumerate(plan):
        totals = zeros(2)
        for frame, a in terms:
            totals = products(frame, 2, a, totals)
        here, left, right = totals
        total = here + from_left(left, cols) + from_right(right, cols)
        parts = [total[:size], total[size:]]
        if extra:
            here, left, right = products(*extra[:1], 1, *extra[1:], zeros(1))
            more = here + from_left(left, cols) + from_right(right, cols)
            parts[member] = parts[member] + more
        for k, part in enumerate(parts):
            part = part.reshape(rows, cols, outs)
            store(
                2 * n + k,
                [part[0:1] * flags[0], part[1 : rows - 1], part[rows - 1 :] * flags[1]],
            )


def early_kernel(plan, weights, flags, pixels, above, below, sent_ref, *scratch):
    def store(n, parts):
        store_dense(sent_ref, n, jnp.concatenate([part.astype(BF16) for part in parts], axis=0))

    down_kernel(0, plan, weights, flags, (pixels, above, below), store, *scratch)


def late_kernel(first, plan, weights, flags, pixels, above, below, out_ref, *scratch):
    def store(n, parts):
        out_ref[n] = jnp.concatenate(parts, axis=0)

    down_kernel(first, plan, weights, flags, (pixels, above, below), store, *scratch)


def down_scratch(count, pixels, rows, cols):
    _, _, chans, wide = pixels.shape
    return [
        pltpu.VMEM((count, 2, rows + 1, cols, 256), BF16),
        pltpu.VMEM((2, count, 3, chans, wide), BF16),
        pltpu.SemaphoreType.DMA((2,)),
    ]


def down_cost(plan, size):
    return 2 * sum(2 * len(terms) + 1 for terms, *_ in plan) * size * 8 * 65536


def down_early(weights, flags, pixels, above, below, rows, cols):
    frames = pixels.shape[0]
    plan = ((((0, 2), (1, 1), (2, 0)), (), 0), (((0, 0),), (0, 1), 1))
    return call(
        functools.partial(early_kernel, plan),
        "down_early",
        pltpu.HBM((6, rows, cols, 128), BF16),
        vmem(1) + [smem()] + vmem(1) + [anywhere()] * 2,
        down_scratch(frames, pixels, rows, cols),
        down_cost(plan, rows * cols),
    )(weights, flags, near(pixels), far(above), far(below))


def down_late(weights, flags, pixels, above, below, rows, cols):
    frames, outs = pixels.shape[0], weights.shape[3]
    plan = ((((2, 2),), (3, 1), 0),)
    return call(
        functools.partial(late_kernel, frames - 2, plan),
        "down_late",
        pltpu.HBM((2, rows, cols, outs), F32),
        vmem(1) + [smem()] + vmem(1) + [anywhere()] * 2,
        down_scratch(2, pixels, rows, cols),
        down_cost(plan, rows * cols),
    )(weights, flags, near(pixels), far(above), far(below))


def back_kernel(
    stats, w_hbm, tile_hbm, own_hbm, late_hbm, next_hbm, out_ref, *scratch
):
    main, rows_pair, frames_pair, rest, weights, tile_ref, own_ref, late_ref, next_ref, sems = scratch
    frames, rows, cols, chans = tile_ref.shape
    pairs = (
        (own_hbm.at[pl.ds(0, 2)], own_ref.at[pl.ds(0, 2)]),
        (own_hbm.at[pl.ds(4, 1)], own_ref.at[pl.ds(2, 1)]),
        (next_hbm, next_ref),
        (late_hbm, late_ref),
        (w_hbm, weights),
        (tile_hbm.at[:, pl.ds(2, rows)], tile_ref),
    )
    copies = [pltpu.make_async_copy(*pair, sems.at[k]) for k, pair in enumerate(pairs)]
    for copy in copies:
        copy.start()
    seqs = out_ref.shape[0]
    size = 2 * rows * cols
    buffer = Packed(main, rows_pair, frames_pair)
    buffer.clear()
    for copy in copies[:3]:
        copy.wait()
    for k in range(2):
        for at, ref in ((k, own_ref), (frames + k, next_ref)):
            block, tail = load_dense(ref, k)
            for r in range(rows + 2):
                buffer.put(at, r, block[r], tail[r])
    copies[3].wait()
    for k in range(2):
        block, tail = load_dense(next_ref, 2 + k)
        late = late_ref[k]
        block = (late[..., :128] + block.astype(F32)).astype(BF16)
        tail = (late[..., 128:] + tail.astype(F32)).astype(BF16)
        for r in range(rows + 2):
            buffer.put(frames - 2 + k, r, block[r], tail[r])
    for copy in copies[4:]:
        copy.wait()
    mean = stats[0:1]
    scale = stats[1:2]
    order = one_hot(
        size,
        size,
        lambda i: ((i >> 3) & 1) * (rows * cols) + (i & 3) * cols + 2 * (i >> 4) + ((i >> 2) & 1),
    )

    def two_frames(n, carry):
        first_sum, second_sum = carry
        t = 2 * n
        total = [jnp.zeros((size, chans), F32) for _ in range(3)]
        for lhs, holds in buffer.operands(t, 2, rows):
            for dc in range(3):
                taps = [
                    weights[2 - tap[0], 2 - tap[1], 2 - dc, :, PARTS[tap[2]]]
                    if tap
                    else jnp.zeros((chans, 64), BF16)
                    for tap in holds
                ]
                total[dc] = total[dc] + nt_dot(lhs, jnp.concatenate(taps, axis=1))
        total = total[1] + from_left(total[0], cols) + from_right(total[2], cols)
        tile = tile_ref[pl.ds(t, 2)].reshape(size, chans)
        normed = (tile.astype(F32) - mean) * scale
        sigmoid = 1.0 / (1.0 + jnp.exp(-normed))
        grad = total * sigmoid * (1.0 + normed * (1.0 - sigmoid))
        first_sum = first_sum + jnp.sum(grad, axis=0, keepdims=True)
        second_sum = second_sum + jnp.sum(grad * normed, axis=0, keepdims=True)
        own = [
            ref[pl.ds(t, 2), 1 : 1 + rows].reshape(size, 128) for ref in (main, rows_pair)
        ]
        own = jnp.concatenate(own, axis=1)[:, :chans].astype(F32)
        base = (own + grad * scale).astype(BF16)
        home = dot(order, base)
        block = home[:, :128].reshape(seqs, 16, 128).astype(BF16)
        out_ref[:, pl.ds(pl.multiple_of(16 * n, 16), 16)] = block
        tail = home[:, 128:].reshape(seqs, 2, 8, chans - 128)
        for k in range(2):
            rest[n, :, :, 64 * k : 64 * (k + 1)] = tail[:, k]
        return first_sum, second_sum

    none = jnp.zeros((1, chans), F32)
    sums = lax.fori_loop(0, frames // 2, two_frames, (none, none))
    both = jnp.concatenate([rest[n] for n in range(frames // 2)], axis=1)
    out_ref[:, 8 * frames : 12 * frames] = both.astype(BF16)
    extra = extra_rows(*sums).astype(BF16)
    out_ref[:, 12 * frames :] = jnp.broadcast_to(extra[None], (seqs, EXTRA, 128))


def back(stats, weights, tile, own, late, following, seqs):
    frames, ext, cols, chans = tile.shape
    rows = ext - 4
    return call(
        back_kernel,
        "back",
        pltpu.HBM((seqs, 12 * frames + EXTRA, 128), BF16),
        vmem(1) + [anywhere()] * 5,
        [
            *packed_scratch(frames + 2, rows + 2, cols),
            pltpu.VMEM((frames // 2, seqs, 8, 128), F32),
            pltpu.VMEM(weights.shape, BF16),
            pltpu.VMEM((frames, rows, cols, chans), BF16),
            pltpu.VMEM((3, *own.shape[1:]), BF16),
            pltpu.VMEM(late.shape, F32),
            pltpu.VMEM(following.shape, BF16),
            pltpu.SemaphoreType.DMA((6,)),
        ],
        2 * frames * rows * cols * 21 * 65536,
    )(stats, far(weights), far(tile), far(own), far(late), far(following))


def sums_kernel(x_ref, out_ref):
    one, two = from_extra(x_ref[...])
    sums = [jnp.sum(v, axis=0, keepdims=True) for v in (one, two)]
    out_ref[...] = jnp.broadcast_to(jnp.concatenate(sums, axis=0)[None], out_ref.shape)


def local_sums(blocks, frames, chans, clips):
    seqs = blocks.shape[0]
    at = 12 * frames // EXTRA
    return pl.pallas_call(
        sums_kernel,
        name="local_sums",
        grid=(1,),
        out_shape=array((clips, 2, chans), F32),
        in_specs=[pl.BlockSpec((seqs, EXTRA, 128), lambda i: (0, at, 0))],
        out_specs=pl.BlockSpec((clips, 2, chans), lambda i: (0, 0, 0)),
        compiler_params=pltpu.CompilerParams(vmem_limit_bytes=VMEM_LIMIT),
        cost_estimate=pl.CostEstimate(flops=10**6, bytes_accessed=10**5, transcendentals=0),
    )(blocks)


def token_kernel(count, x_ref, tokens_ref, stats_ref, parts_ref, out_ref):
    frames, stripe, chans, height = tokens_ref.shape
    seqs = x_ref.shape[0]
    sums = jnp.sum(parts_ref[...], axis=0)
    sums = group_sum(jnp.concatenate([sums, jnp.zeros((6, chans), F32)], axis=0)) / count
    first, second = (jnp.broadcast_to(sums[k : k + 1], (128, chans)).T for k in range(2))
    mean, scale = (jnp.broadcast_to(stats_ref[k : k + 1], (128, chans)).T for k in range(2))
    eye = one_hot(128, 128, lambda i: i)
    lanes = 16 * seqs

    order = one_hot(lanes, lanes, lambda i: ((i >> 2) & 3) * height + (i >> 4) * 4 + (i & 3))

    def turned(at):
        block = x_ref[:, at : at + 16].reshape(lanes, 128)
        return dot(nt_dot(eye, block).astype(BF16), order)

    rest = turned(8 * frames)
    for n in range(frames // 2):
        main = turned(16 * n)
        for k in range(2 * stripe):
            t, c = 2 * n + k // stripe, k % stripe
            at = stripe * n + c
            base = jnp.concatenate(
                [
                    main[:, height * k : height * (k + 1)],
                    rest[64 * (k // stripe) : 64 * (k // stripe + 1), height * at : height * (at + 1)],
                ],
                axis=0,
            )
            normed = (tokens_ref[t, c].astype(F32) - mean) * scale
            out_ref[t, c] = (base - (first + normed * second) * scale).astype(BF16)


def token_gradient(blocks, tokens, stats, parts, count):
    return call(
        functools.partial(token_kernel, count),
        "token_gradient",
        array(tokens.shape),
        vmem(4),
        [],
        10**9,
    )(blocks, tokens, stats, parts)


class Packed:
    def __init__(self, main, rows_pair, frames_pair):
        self.main, self.rows_pair, self.frames_pair = main, rows_pair, frames_pair

    def clear(self):
        self.rows_pair[...] = jnp.zeros_like(self.rows_pair)
        self.frames_pair[...] = jnp.zeros_like(self.frames_pair)

    def put(self, t, r, main, rest):
        self.main[t, r] = main
        self.rows_pair[t, r, :, 0:64] = rest
        self.frames_pair[t, r, :, 0:64] = rest
        if r > 0:
            self.rows_pair[t, r - 1, :, 64:128] = rest
        if not (isinstance(t, int) and t == 0):
            self.frames_pair[t - 1, r, :, 64:128] = rest

    def operands(self, t, count, rows):
        def get(ref, dt, dr):
            block = ref[pl.ds(t + dt, count), dr : dr + rows]
            return block.reshape(count * rows * block.shape[2], 128)

        tiles = [(get(self.main, dt, dr), [(dt, dr, 0)]) for dt in range(3) for dr in range(3)]
        for dt in range(3):
            tiles.append((get(self.rows_pair, dt, 0), [(dt, 0, 1), (dt, 1, 1)]))
        tiles.append((get(self.frames_pair, 0, 2), [(0, 2, 1), (1, 2, 1)]))
        tiles.append((get(self.rows_pair, 2, 2), [(2, 2, 1), None]))
        return [
            (jnp.concatenate([one, two], axis=1), has + more)
            for (one, has), (two, more) in zip(tiles[::2], tiles[1::2])
        ]


def packed_scratch(frames, rows, cols):
    return [pltpu.VMEM((frames, rows, cols, 128), BF16) for _ in range(3)]


PARTS = (slice(0, 128), slice(128, 192))


def fetch(source, target, sems):
    copies = [pltpu.make_async_copy(source.at[k], target.at[k], sems.at[k]) for k in range(3)]
    for copy in copies:
        copy.start()
    return copies


def mid_kernel(
    flags, stats, w_hbm, tile_hbm, before_ref, out_ref, sent_ref, *scratch
):
    main, rows_pair, frames_pair, weights, sems, tile_ref, sem = scratch
    tile_copy = pltpu.make_async_copy(tile_hbm, tile_ref, sem)
    tile_copy.start()
    copies = fetch(w_hbm, weights, sems)
    frames, rows, cols, chans = out_ref.shape
    size = 2 * rows * cols
    mean = stats[0:1]
    scale = stats[1:2]

    def activate(value, row, later):
        normed = (value.astype(F32) - mean) * scale
        act = normed / (1.0 + jnp.exp(-normed))
        if row < 2:
            act = act * flags[0]
        if row >= rows:
            act = act * flags[1]
        if later:
            act = act * flags[2]
        return act.astype(BF16)

    buffer = Packed(main, rows_pair, frames_pair)
    buffer.clear()
    for t in range(2):
        for r in range(rows + 2):
            act = activate(before_ref[t, r], r, True)
            buffer.put(t, r, act[:, :128], act[:, 128:])
    tile_copy.wait()

    def one_frame(t, carry):
        for r in range(rows + 2):
            act = activate(tile_ref[t, r], r, False)
            buffer.put(t + 2, r, act[:, :128], act[:, 128:])
        return carry

    lax.fori_loop(0, frames, one_frame, 0)
    for copy in copies:
        copy.wait()

    def two_frames(n, carry):
        t = 2 * n
        total = [jnp.zeros((size, chans), F32) for _ in range(3)]
        for lhs, holds in buffer.operands(t, 2, rows):
            for dc in range(3):
                taps = [
                    weights[tap[0], tap[1], dc, PARTS[tap[2]]]
                    if tap
                    else jnp.zeros((64, chans), BF16)
                    for tap in holds
                ]
                total[dc] = total[dc] + dot(lhs, jnp.concatenate(taps, axis=0))
        total = total[1] + from_left(total[0], cols) + from_right(total[2], cols)
        total = total.reshape(2, rows, cols, chans)
        total = total + tile_ref[pl.ds(t, 2), 1 : 1 + rows].astype(F32)
        out_ref[pl.ds(t, 2), 0:1] = (total[:, 0:1] * flags[0]).astype(BF16)
        out_ref[pl.ds(t, 2), 1 : rows - 1] = total[:, 1 : rows - 1].astype(BF16)
        out_ref[pl.ds(t, 2), rows - 1 : rows] = (total[:, rows - 1 :] * flags[1]).astype(BF16)
        return carry

    lax.fori_loop(0, frames // 2, two_frames, 0)
    for k in range(2):
        store_dense(sent_ref, k, out_ref[frames - 2 + k])


def middle(flags, stats, weights, tile, before):
    frames, ext, cols, chans = tile.shape
    rows = ext - 2
    return call(
        mid_kernel,
        "middle",
        (kept((frames, rows, cols, chans)), array((3, rows, cols, 128))),
        [smem()] + vmem(1) + [anywhere()] * 2 + vmem(1),
        [
            *packed_scratch(frames + 2, ext, cols),
            pltpu.VMEM(weights.shape, BF16),
            pltpu.SemaphoreType.DMA((3,)),
            pltpu.VMEM(tile.shape, BF16),
            pltpu.SemaphoreType.DMA,
        ],
        2 * frames * rows * cols * 27 * 65536,
    )(flags, stats, far(weights), tile, before)


def decode_kernel(
    w_hbm, before_ref, mid_ref, out_ref, main_ref, pair_ref, wide, weights, sems
):
    copies = fetch(w_hbm, weights, sems)
    frames, ext, cols, chans = mid_ref.shape
    lines, outs, _ = out_ref.shape[1:]
    rows = lines // 2
    pair_ref[:, ext - 1] = jnp.zeros_like(pair_ref[:, ext - 1])

    def put(at, main, rest):
        main_ref[at] = main
        pair_ref[at, :, :, 0:64] = rest
        pair_ref[at, 0 : ext - 1, :, 64:128] = rest[1:]

    for k in range(2):
        put(k, *load_dense(before_ref, k))

    def one_frame(t, carry):
        value = mid_ref[t]
        put(t + 2, value[..., :128], value[..., 128:])
        return carry

    lax.fori_loop(0, frames, one_frame, 0)
    eye = one_hot(outs, 128, lambda i: i)
    size = 2 * rows * cols

    for t in range(0, frames, 2):
        for i, taps in enumerate((((0, 3), (1, 1)), ((1, 2), (2, 0)))):
            here, aside = (jnp.zeros((size, 256), F32) for _ in range(2))
            tiles = []
            for dt in range(3):
                if t + i == 0:
                    copies[dt].wait()
                at = slice(t + dt, t + dt + 2)
                (dr, p), (below, q) = taps
                for ref, row, parts in (
                    (main_ref, dr, [(p, slice(0, 128))]),
                    (main_ref, below, [(q, slice(0, 128))]),
                    (pair_ref, dr, [(p, slice(128, 192)), (q, slice(128, 192))]),
                ):
                    lhs = ref[at, row : row + rows].reshape(size, 128)
                    tiles.append((lhs, [(weights.at[dt, tap], part) for tap, part in parts]))
            for n in range(0, len(tiles), 2):
                lhs = jnp.concatenate([lhs for lhs, _ in tiles[n : n + 2]], axis=1)
                taken = [tap for _, some in tiles[n : n + 2] for tap in some]
                for into, (one, two) in enumerate(((1, 2), (3, 0))):
                    rhs = [
                        jnp.concatenate([w[one, part], w[two, part]], axis=1) for w, part in taken
                    ]
                    rhs = jnp.concatenate(rhs, axis=0)
                    if into == 0:
                        here = here + dot(lhs, rhs)
                    else:
                        aside = aside + dot(lhs, rhs)
            even = (here[:, :128] + from_left(aside[:, :128], cols)).reshape(2, rows, cols, 128)
            odd = (here[:, 128:] + from_right(aside[:, 128:], cols)).reshape(2, rows, cols, 128)
            for k in range(2):
                for r in range(rows):
                    wide[k, 2 * r + i, pl.ds(0, cols, stride=2), :] = even[k, r]
                    wide[k, 2 * r + i, pl.ds(1, cols, stride=2), :] = odd[k, r]
        for k in range(2):
            for r in range(rows):
                pair = wide[k, 2 * r : 2 * r + 2].reshape(4 * cols, 128).astype(BF16)
                turned = nt_dot(eye, pair).astype(BF16)
                out_ref[t + k, 2 * r] = turned[:, 0 : 2 * cols]
                out_ref[t + k, 2 * r + 1] = turned[:, 2 * cols :]


def decode(weights, before, mid, outs):
    frames, ext, cols, chans = mid.shape
    rows = ext - 2
    return call(
        decode_kernel,
        "decode",
        array((frames, 2 * rows, outs, 2 * cols)),
        [anywhere()] + vmem(2),
        [
            pltpu.VMEM((frames + 2, ext, cols, 128), BF16),
            pltpu.VMEM((frames + 2, ext, cols, 128), BF16),
            pltpu.VMEM((2, 2 * rows, 2 * cols, 128), F32),
            pltpu.VMEM(weights.shape, BF16),
            pltpu.SemaphoreType.DMA((3,)),
        ],
        2 * frames * rows * cols * 24 * 65536,
    )(far(weights), before, mid)


def moved(block, clip_step, seq_step):
    clips, seqs = lax.axis_size("clip"), lax.axis_size("seq")
    if clip_step == 0:
        route = [(i - seq_step, i) for i in range(seqs) if 0 <= i - seq_step < seqs]
        return lax.ppermute(block, "seq", route)
    if seq_step == 0:
        route = [(i - clip_step, i) for i in range(clips) if 0 <= i - clip_step < clips]
        return lax.ppermute(block, "clip", route)
    route = [
        ((s - seq_step) * clips + c - clip_step, s * clips + c)
        for s in range(seqs)
        for c in range(clips)
        if 0 <= c - clip_step < clips and 0 <= s - seq_step < seqs
    ]
    return lax.ppermute(block, ("seq", "clip"), route)


def exchanged(blocks, axis):
    return lax.all_to_all(blocks, axis, 0, 0, tiled=True)


def body(tokens, conv_one, conv_two, pixel_grad):
    frames, height, stripe, chans = tokens.shape
    lines, wide, outs = pixel_grad.shape[1:]
    rows, cols = lines // 2, wide // 2
    clips, seqs = lax.axis_size("clip"), lax.axis_size("seq")
    clip, seq = lax.axis_index("clip"), lax.axis_index("seq")
    flags = jnp.stack([seq != 0, seq != seqs - 1, clip != 0]).astype(F32)
    tokens = tokens.transpose(0, 2, 3, 1)
    pixels = pixel_grad.transpose(0, 1, 3, 2)
    held = float(frames * height * stripe)

    first, last = edges(pixels)
    above, below = moved(last, 0, 1), moved(first, 0, -1)
    packed = pack(tokens, seqs)
    both = combined_weights(conv_two)
    above, below, both, packed = lax.optimization_barrier((above, below, both, packed))

    blocks = exchanged(packed, "seq")
    own = far(down_early(near(both), flags, pixels, above, below, rows + 2, cols))
    following = moved(own, -1, 0)
    tile, tile_last, parts = unpack(blocks, frames, cols, chans, clips, held)
    tile = far(tile)
    late = down_late(near(both), flags, pixels, above, below, rows + 2, cols)
    parts, late = lax.optimization_barrier((exchanged(parts, "clip"), late))
    stats = group_stats(parts, held * seqs)
    tile_last, stats = lax.optimization_barrier((tile_last, stats))
    tile_z = moved(tile_last, 1, 0)
    stats = near(stats)

    home = exchanged(back(stats, conv_one, tile, own, late, following, seqs), "seq")

    mid, mid_last = middle(flags, stats, conv_one, tile, tile_z)
    decoded = decode(both, moved(mid_last, 1, 0), near(mid), outs)

    sums = exchanged(local_sums(home, frames, chans, clips), "clip")
    sums, decoded = lax.optimization_barrier((sums, decoded))
    count = held * seqs * clips * (chans // GROUPS)
    token_grad = token_gradient(home, tokens, stats, sums, count)
    return (decoded.transpose(0, 1, 3, 2), token_grad.transpose(0, 3, 1, 2))


def solution(mesh):
    return jax.shard_map(
        body,
        mesh=mesh,
        in_specs=(P("clip", None, "seq", None), P(), P(), P("clip", "seq", None, None)),
        out_specs=(P("clip", "seq", None, None), P("clip", None, "seq", None)),
        check_vma=False,
    )
```

```python
import functools

import jax
import jax.numpy as jnp
from jax import lax
from jax.experimental import pallas as pl
from jax.experimental.pallas import tpu as pltpu
from jax.sharding import PartitionSpec as P

GROUPS = 32
F32 = jnp.float32
BF16 = jnp.bfloat16
VMEM_LIMIT = 32 * 2**20
TAPS = ((2,), (1, 2), (0, 1), (0,))
EXTRA = 16


def vmem(count):
    return [pl.BlockSpec(memory_space=pltpu.VMEM)] * count


def smem():
    return pl.BlockSpec(memory_space=pltpu.SMEM)


def anywhere():
    return pl.BlockSpec(memory_space=pltpu.HBM)


def call(kernel, name, outs, in_specs, scratch, flops, moved_bytes=4 * 2**20):
    return pl.pallas_call(
        kernel,
        name=name,
        out_shape=outs,
        in_specs=in_specs,
        out_specs=jax.tree.map(lambda _: pl.BlockSpec(memory_space=pltpu.VMEM), outs),
        scratch_shapes=scratch,
        compiler_params=pltpu.CompilerParams(vmem_limit_bytes=VMEM_LIMIT),
        cost_estimate=pl.CostEstimate(flops=flops, bytes_accessed=moved_bytes, transcendentals=0),
    )


def array(shape, dtype=BF16):
    return jax.ShapeDtypeStruct(shape, dtype)


def kept(shape, dtype=BF16):
    return pltpu.VMEM(shape, dtype)


def near(block):
    return pltpu.with_memory_space_constraint(block, pltpu.VMEM)


def far(block):
    return pltpu.with_memory_space_constraint(block, pltpu.HBM)


def dot(lhs, rhs):
    return jnp.dot(lhs, rhs, preferred_element_type=F32)


def nt_dot(lhs, rhs):
    return lax.dot_general(lhs, rhs, (((1,), (1,)), ((), ())), preferred_element_type=F32)


def one_hot(rows, cols, place):
    width = min(cols, 128)
    target = place(lax.broadcasted_iota(jnp.int32, (rows, width), 0))
    target = target - lax.broadcasted_iota(jnp.int32, (rows, width), 1)
    blocks = [
        jnp.where(target == at, 1.0, 0.0).astype(BF16)[:, : cols - at]
        for at in range(0, cols, width)
    ]
    return jnp.concatenate(blocks, axis=1) if len(blocks) > 1 else blocks[0]


def same_group(chans):
    size = chans // GROUPS
    row = lax.broadcasted_iota(jnp.int32, (chans, chans), 0).astype(F32)
    col = lax.broadcasted_iota(jnp.int32, (chans, chans), 1).astype(F32)
    row, col = (jnp.floor((index + 0.5) / size) for index in (row, col))
    return jnp.where(row == col, 1.0, 0.0)


def group_sum(channels):
    return jnp.dot(
        channels,
        same_group(channels.shape[1]),
        precision=lax.Precision.HIGHEST,
        preferred_element_type=F32,
    )


def split_3(value):
    terms = []
    for _ in range(3):
        terms.append(value.astype(BF16).astype(F32))
        value = value - terms[-1]
    return terms


def extra_rows(one, two):
    rest = jnp.concatenate([one[:, 128:], two[:, 128:]], axis=1)
    row = lax.broadcasted_iota(jnp.int32, (EXTRA, 128), 0)
    out = jnp.zeros((EXTRA, 128), F32)
    for n, term in enumerate(split_3(one[:, :128]) + split_3(two[:, :128]) + split_3(rest)):
        out = jnp.where(row == n, term, out)
    return out


def from_extra(block):
    block = block.astype(F32)
    row = lax.broadcasted_iota(jnp.int32, block.shape, 1)
    one, two, rest = (
        jnp.sum(jnp.where((row >= k) & (row < k + 3), block, 0.0), axis=1) for k in (0, 3, 6)
    )
    return (
        jnp.concatenate([one, rest[:, :64]], axis=1),
        jnp.concatenate([two, rest[:, 64:]], axis=1),
    )


def store_dense(ref, frame, value):
    frames = ref.shape[0] * 2 // 3
    lane = 64 * (frame % 2)
    ref[frame] = value[..., :128]
    ref[frames + frame // 2, :, :, lane : lane + 64] = value[..., 128:]


def load_dense(ref, frame):
    frames = ref.shape[0] * 2 // 3
    lane = 64 * (frame % 2)
    return ref[frame], ref[frames + frame // 2, :, :, lane : lane + 64]


def from_left(value, cols):
    column = lax.broadcasted_iota(jnp.int32, value.shape, 0) & (cols - 1)
    return jnp.where(column == 0, 0.0, pltpu.roll(value, 1, 0))


def from_right(value, cols):
    size = value.shape[0]
    column = lax.broadcasted_iota(jnp.int32, value.shape, 0) & (cols - 1)
    return jnp.where(column == cols - 1, 0.0, pltpu.roll(value, size - 1, 0))


def fetch(source, target, sem):
    copy = pltpu.make_async_copy(source, target, sem)
    copy.start()
    return copy


def combine_kernel(w_ref, out_ref):
    outs = w_ref.shape[4]

    def one_time(a, carry):
        w = [[w_ref[a, b, d].astype(F32) for d in range(3)] for b in range(3)]
        for p in range(4):
            rows = [functools.reduce(jnp.add, [w[b][d] for b in TAPS[p]]) for d in range(3)]
            for q in range(4):
                value = functools.reduce(jnp.add, [rows[d] for d in TAPS[q]])
                out_ref[a, p, q] = jnp.pad(value, ((0, 0), (0, 128 - outs))).astype(BF16)
        return carry

    lax.fori_loop(0, 3, one_time, 0)


def combined_weights(conv_two):
    shape = kept((3, 4, 4, conv_two.shape[3], 128))
    return call(combine_kernel, "combine_weights", shape, vmem(1), [], 10**6)(conv_two)


def edges_kernel(x_hbm, first_hbm, last_hbm, near_ref, sems):
    lines = x_hbm.shape[1]
    ends = ((0, first_hbm), (lines - 3, last_hbm))
    for k, (at, _) in enumerate(ends):
        pltpu.make_async_copy(x_hbm.at[:, pl.ds(at, 3)], near_ref.at[k], sems.at[0, k]).start()
    copies = []
    for k, (at, ref) in enumerate(ends):
        pltpu.make_async_copy(x_hbm.at[:, pl.ds(at, 3)], near_ref.at[k], sems.at[0, k]).wait()
        copies.append(pltpu.make_async_copy(near_ref.at[k], ref, sems.at[1, k]))
        copies[k].start()
    for copy in copies:
        copy.wait()


def edges(pixels):
    frames, _, outs, wide = pixels.shape
    shape = pltpu.HBM((frames, 3, outs, wide), BF16)
    return pl.pallas_call(
        edges_kernel,
        name="edges",
        out_shape=(shape, shape),
        in_specs=[anywhere()],
        out_specs=(anywhere(), anywhere()),
        scratch_shapes=[
            pltpu.VMEM((2, *shape.shape), BF16),
            pltpu.SemaphoreType.DMA((2, 2)),
        ],
        cost_estimate=pl.CostEstimate(flops=10**6, bytes_accessed=10**6, transcendentals=0),
    )(far(pixels))


def own_moments(x_ref):
    frames, stripe, chans, height = x_ref.shape
    total = jnp.zeros((chans, height), F32)
    for t in range(frames):
        for c in range(stripe):
            total = total + x_ref[t, c].astype(F32)
    mean = jnp.sum(total, axis=1, keepdims=True) / float(frames * stripe * height)
    spread = jnp.zeros((chans, height), F32)
    for t in range(frames):
        for c in range(stripe):
            spread = spread + (x_ref[t, c].astype(F32) - mean) ** 2
    spread = jnp.sum(spread, axis=1, keepdims=True)
    return [jnp.broadcast_to(v, (chans, 128)).T[0:1] for v in (mean, spread)]


def merged(means, spreads, held):
    mean = jnp.sum(means, axis=0, keepdims=True) / means.shape[0]
    spread = jnp.sum(spreads, axis=0, keepdims=True)
    return mean, spread + held * jnp.sum((means - mean) ** 2, axis=0, keepdims=True)


def pack_kernel(x_ref, out_ref):
    frames, stripe, chans, height = x_ref.shape
    seqs = out_ref.shape[0]
    rows = height // seqs
    select = one_hot(8 * seqs, height, lambda i: rows * (i >> 3) - 2 + (i & 7))

    def picked(x):
        return nt_dot(select, x).reshape(seqs, 8, 128)

    for n in range(frames // 2):
        pair = [x_ref.at[2 * n + k] for k in range(2)]
        blocks = [[x[c, 0:128] for c in range(stripe)] for x in pair]
        tails = [[x[c, 128:chans] for x in pair] for c in range(stripe)]
        blocks.append([jnp.concatenate(tail, axis=0) for tail in tails])
        for k, columns in enumerate(blocks):
            at = 48 * n + 16 * k
            rows_of = [picked(column) for column in columns]
            out_ref[:, at : at + 16] = jnp.concatenate(rows_of, axis=1).astype(BF16)
    extra = extra_rows(*own_moments(x_ref)).astype(BF16)
    out_ref[:, 24 * frames :] = jnp.broadcast_to(extra[None], (seqs, EXTRA, 128))


def pack(tokens, seqs):
    shape = pltpu.HBM((seqs, 24 * tokens.shape[0] + EXTRA, 128), BF16)
    return call(pack_kernel, "pack", shape, vmem(1), [], 10**9)(tokens)


def unpack_kernel(held, x_ref, tile_ref, last_ref, parts_ref):
    seqs = x_ref.shape[0]
    frames, rows, cols, chans = tile_ref.shape
    size = rows * cols

    order = one_hot(size, 16 * seqs, lambda i: ((i >> 1) & 31) * 16 + (i & 1) * 8 + (i >> 6))
    for n in range(frames // 2):
        blocks = [x_ref[:, 48 * n + 16 * k : 48 * n + 16 * (k + 1)] for k in range(3)]
        blocks = [block.reshape(16 * seqs, 128) for block in blocks]
        main = dot(order, jnp.concatenate(blocks[:2], axis=1)).astype(BF16)
        rest = dot(order, blocks[2]).astype(BF16)
        for k in range(2):
            t = 2 * n + k
            for ref, at in ((tile_ref, t), (last_ref, t - frames + 2)):
                if at >= 0:
                    part = main[:, 128 * k : 128 * (k + 1)]
                    ref[at, :, :, 0:128] = part.reshape(rows, cols, 128)
                    part = rest[:, 64 * k : 64 * (k + 1)]
                    ref[at, :, :, 128:chans] = part.reshape(rows, cols, 64)
    parts = merged(*from_extra(x_ref[:, 24 * frames :]), held)
    parts_ref[...] = jnp.broadcast_to(jnp.concatenate(parts, axis=0)[None], parts_ref.shape)


def unpack(blocks, frames, cols, chans, clips, held):
    return call(
        functools.partial(unpack_kernel, held),
        "unpack",
        (
            pltpu.HBM((frames, 8, cols, chans), BF16),
            pltpu.HBM((2, 8, cols, chans), BF16),
            pltpu.HBM((clips, 2, chans), F32),
        ),
        vmem(1),
        [],
        10**9,
    )(blocks)


def group_stats(parts_ref, held):
    clips, _, chans = parts_ref.shape
    means, spreads = parts_ref[:, 0], parts_ref[:, 1]
    size = chans // GROUPS
    mean = group_sum(jnp.broadcast_to(jnp.sum(means, axis=0, keepdims=True), (8, chans)))
    mean = mean[0:1] / (clips * size)
    spread = jnp.sum(spreads, axis=0, keepdims=True)
    spread = spread + held * jnp.sum((means - mean) ** 2, axis=0, keepdims=True)
    var = group_sum(jnp.broadcast_to(spread, (8, chans)))[0:1] / (held * clips * size)
    return mean, lax.rsqrt(var + 1e-06)


def down_kernel(first, plan, weights, flags, sources, store, buffer, beside, sems):
    _, _, cols, _ = buffer.shape[1:]
    rows, outs = buffer.shape[2] - 1, weights.shape[3]
    pixels, *sides = sources
    count = buffer.shape[0]
    lines, chans, wide = pixels.shape[1:]
    copies = [
        pltpu.make_async_copy(side.at[pl.ds(first, count)], beside.at[k], sems.at[k])
        for k, side in enumerate(sides)
    ]
    for copy in copies:
        copy.start()
    select = one_hot(2 * cols, wide, lambda i: 2 * (i & (cols - 1)) + (i // cols))
    blank = jnp.zeros((128 - chans, wide), BF16)

    def line(i, n):
        if 3 <= n < 3 + lines:
            return pixels[first + i, n - 3]
        return beside[0, i, n] if n < 3 else beside[1, i, n - 3 - lines]

    def place(inner):
        def one_frame(i, carry):
            firsts = [n for n in range(0, lines + 6, 2) if (3 < n < 2 + lines) == inner]
            rhs = [x for n in firsts for k in range(2) for x in (line(i, n + k), blank)]
            picked = nt_dot(select, jnp.concatenate(rhs, axis=0)).astype(BF16)
            for m, n in enumerate(firsts):
                for k in range(2):
                    for j in range(2):
                        at = 256 * m + 128 * k
                        buffer[i, k, n // 2, :, 128 * j : 128 * (j + 1)] = picked[
                            cols * j : cols * (j + 1), at : at + 128
                        ]
            return carry

        lax.fori_loop(0, count, one_frame, 0)

    place(True)
    for copy in copies:
        copy.wait()
    place(False)

    size = rows * cols

    def products(frame, count, a, totals):
        here, left, right = totals
        frames = slice(frame - first, frame - first + count)
        lines = [
            buffer[frames, p % 2, p // 2 : p // 2 + rows].reshape(count * size, 256)
            for p in range(4)
        ]
        w = weights.at[a]
        for p in range(4):
            here = here + nt_dot(lines[p], jnp.concatenate([w[p, 1], w[p, 2]], axis=-1))
        for p in range(0, 4, 2):
            odd = jnp.concatenate([lines[p][:, 128:], lines[p + 1][:, 128:]], axis=-1)
            left = left + nt_dot(odd, jnp.concatenate([w[p, 0], w[p + 1, 0]], axis=-1))
            even = jnp.concatenate([lines[p][:, :128], lines[p + 1][:, :128]], axis=-1)
            right = right + nt_dot(even, jnp.concatenate([w[p, 3], w[p + 1, 3]], axis=-1))
        return here, left, right

    def zeros(count):
        return [jnp.zeros((count * size, outs), F32) for _ in range(3)]

    for n, (terms, extra, member) in enumerate(plan):
        totals = zeros(2)
        for frame, a in terms:
            totals = products(frame, 2, a, totals)
        here, left, right = totals
        total = here + from_left(left, cols) + from_right(right, cols)
        parts = [total[:size], total[size:]]
        if extra:
            here, left, right = products(*extra[:1], 1, *extra[1:], zeros(1))
            more = here + from_left(left, cols) + from_right(right, cols)
            parts[member] = parts[member] + more
        for k, part in enumerate(parts):
            part = part.reshape(rows, cols, outs)
            store(
                2 * n + k,
                [part[0:1] * flags[0], part[1 : rows - 1], part[rows - 1 :] * flags[1]],
            )


def early_kernel(plan, weights, flags, pixels, above, below, out_hbm, *scratch):
    *scratch, sent_ref, out_sems = scratch
    copies = [
        pltpu.make_async_copy(sent_ref.at[pl.ds(at, n)], out_hbm.at[pl.ds(at, n)], out_sems.at[k])
        for k, (at, n) in enumerate(((0, 2), (4, 1), (2, 2), (5, 1)))
    ]

    def store(n, parts):
        store_dense(sent_ref, n, jnp.concatenate([part.astype(BF16) for part in parts], axis=0))
        if n % 2 == 1:
            for copy in copies[n - 1 : n + 1]:
                copy.start()

    down_kernel(0, plan, weights, flags, (pixels, above, below), store, *scratch)
    for copy in copies:
        copy.wait()


def late_kernel(first, plan, weights, flags, pixels, above, below, out_ref, *scratch):
    def store(n, parts):
        out_ref[n] = jnp.concatenate(parts, axis=0)

    down_kernel(first, plan, weights, flags, (pixels, above, below), store, *scratch)


def down_scratch(count, pixels, rows, cols):
    _, _, chans, wide = pixels.shape
    return [
        pltpu.VMEM((count, 2, rows + 1, cols, 256), BF16),
        pltpu.VMEM((2, count, 3, chans, wide), BF16),
        pltpu.SemaphoreType.DMA((2,)),
    ]


def down_cost(plan, size):
    return 2 * sum(2 * len(terms) + 1 for terms, *_ in plan) * size * 8 * 65536


def down_early(weights, flags, pixels, above, below, rows, cols):
    frames = pixels.shape[0]
    plan = ((((0, 2), (1, 1), (2, 0)), (), 0), (((0, 0),), (0, 1), 1))
    return pl.pallas_call(
        functools.partial(early_kernel, plan),
        name="down_early",
        out_shape=pltpu.HBM((6, rows, cols, 128), BF16),
        in_specs=vmem(1) + [smem()] + vmem(1) + [anywhere()] * 2,
        out_specs=anywhere(),
        scratch_shapes=[
            *down_scratch(frames, pixels, rows, cols),
            pltpu.VMEM((6, rows, cols, 128), BF16),
            pltpu.SemaphoreType.DMA((4,)),
        ],
        compiler_params=pltpu.CompilerParams(vmem_limit_bytes=VMEM_LIMIT),
        cost_estimate=pl.CostEstimate(
            flops=down_cost(plan, rows * cols), bytes_accessed=4 * 2**20, transcendentals=0
        ),
    )(weights, flags, near(pixels), far(above), far(below))


def down_late(weights, flags, pixels, above, below, rows, cols):
    frames, outs = pixels.shape[0], weights.shape[3]
    plan = ((((2, 2),), (3, 1), 0),)
    return call(
        functools.partial(late_kernel, frames - 2, plan),
        "down_late",
        pltpu.HBM((2, rows, cols, outs), F32),
        vmem(1) + [smem()] + vmem(1) + [anywhere()] * 2,
        down_scratch(2, pixels, rows, cols),
        down_cost(plan, rows * cols),
    )(weights, flags, near(pixels), far(above), far(below))


def back_kernel(
    held, parts_ref, w_hbm, tile_hbm, own_hbm, late_hbm, next_hbm, out_ref, stats_ref, *scratch
):
    main, rows_pair, frames_pair, rest, weights, tile_ref, own_ref, late_ref, next_ref, sems = scratch
    frames, rows, cols, chans = tile_ref.shape
    pairs = (
        (own_hbm.at[pl.ds(0, 2)], own_ref.at[pl.ds(0, 2)]),
        (own_hbm.at[pl.ds(4, 1)], own_ref.at[pl.ds(2, 1)]),
        (next_hbm, next_ref),
        (late_hbm, late_ref),
        (w_hbm, weights),
        (tile_hbm.at[:, pl.ds(2, rows)], tile_ref),
    )
    copies = [pltpu.make_async_copy(*pair, sems.at[k]) for k, pair in enumerate(pairs)]
    for copy in copies:
        copy.start()
    seqs = out_ref.shape[0]
    size = 2 * rows * cols
    mean, scale = group_stats(parts_ref, held)
    stats_ref[...] = jnp.concatenate([mean, scale], axis=0)
    buffer = Packed(main, rows_pair, frames_pair)
    buffer.clear()
    for copy in copies[:3]:
        copy.wait()
    for k in range(2):
        for at, ref in ((k, own_ref), (frames + k, next_ref)):
            block, tail = load_dense(ref, k)
            for r in range(rows + 2):
                buffer.put(at, r, block[r], tail[r])
    copies[3].wait()
    for k in range(2):
        block, tail = load_dense(next_ref, 2 + k)
        late = late_ref[k]
        block = (late[..., :128] + block.astype(F32)).astype(BF16)
        tail = (late[..., 128:] + tail.astype(F32)).astype(BF16)
        for r in range(rows + 2):
            buffer.put(frames - 2 + k, r, block[r], tail[r])
    for copy in copies[4:]:
        copy.wait()
    order = one_hot(
        size,
        size,
        lambda i: ((i >> 3) & 1) * (rows * cols) + (i & 3) * cols + 2 * (i >> 4) + ((i >> 2) & 1),
    )

    def two_frames(n, carry):
        first_sum, second_sum = carry
        t = 2 * n
        total = [jnp.zeros((size, chans), F32) for _ in range(3)]
        for lhs, holds in buffer.operands(t, 2, rows):
            for dc in range(3):
                taps = [
                    weights[2 - tap[0], 2 - tap[1], 2 - dc, :, PARTS[tap[2]]]
                    if tap
                    else jnp.zeros((chans, 64), BF16)
                    for tap in holds
                ]
                total[dc] = total[dc] + nt_dot(lhs, jnp.concatenate(taps, axis=1))
        total = total[1] + from_left(total[0], cols) + from_right(total[2], cols)
        tile = tile_ref[pl.ds(t, 2)].reshape(size, chans)
        normed = (tile.astype(F32) - mean) * scale
        sigmoid = 1.0 / (1.0 + jnp.exp(-normed))
        grad = total * sigmoid * (1.0 + normed * (1.0 - sigmoid))
        first_sum = first_sum + jnp.sum(grad, axis=0, keepdims=True)
        second_sum = second_sum + jnp.sum(grad * normed, axis=0, keepdims=True)
        own = [
            ref[pl.ds(t, 2), 1 : 1 + rows].reshape(size, 128) for ref in (main, rows_pair)
        ]
        own = jnp.concatenate(own, axis=1)[:, :chans].astype(F32)
        base = (own + grad * scale).astype(BF16)
        home = dot(order, base)
        block = home[:, :128].reshape(seqs, 16, 128).astype(BF16)
        out_ref[:, pl.ds(pl.multiple_of(16 * n, 16), 16)] = block
        tail = home[:, 128:].reshape(seqs, 2, 8, chans - 128)
        for k in range(2):
            rest[n, :, :, 64 * k : 64 * (k + 1)] = tail[:, k]
        return first_sum, second_sum

    none = jnp.zeros((1, chans), F32)
    sums = lax.fori_loop(0, frames // 2, two_frames, (none, none))
    both = jnp.concatenate([rest[n] for n in range(frames // 2)], axis=1)
    out_ref[:, 8 * frames : 12 * frames] = both.astype(BF16)
    extra = extra_rows(*sums).astype(BF16)
    out_ref[:, 12 * frames :] = jnp.broadcast_to(extra[None], (seqs, EXTRA, 128))


def back(parts, held, weights, tile, own, late, following, seqs):
    frames, ext, cols, chans = tile.shape
    rows = ext - 4
    return call(
        functools.partial(back_kernel, held),
        "back",
        (pltpu.HBM((seqs, 12 * frames + EXTRA, 128), BF16), kept((2, chans), F32)),
        vmem(1) + [anywhere()] * 5,
        [
            *packed_scratch(frames + 2, rows + 2, cols),
            pltpu.VMEM((frames // 2, seqs, 8, 128), F32),
            pltpu.VMEM(weights.shape, BF16),
            pltpu.VMEM((frames, rows, cols, chans), BF16),
            pltpu.VMEM((3, *own.shape[1:]), BF16),
            pltpu.VMEM(late.shape, F32),
            pltpu.VMEM(following.shape, BF16),
            pltpu.SemaphoreType.DMA((6,)),
        ],
        2 * frames * rows * cols * 21 * 65536,
    )(parts, far(weights), far(tile), far(own), far(late), far(following))


def sums_kernel(x_ref, out_ref):
    one, two = from_extra(x_ref[...])
    sums = [jnp.sum(v, axis=0, keepdims=True) for v in (one, two)]
    out_ref[...] = jnp.broadcast_to(jnp.concatenate(sums, axis=0)[None], out_ref.shape)


def local_sums(blocks, frames, chans, clips):
    seqs = blocks.shape[0]
    at = 12 * frames // EXTRA
    return pl.pallas_call(
        sums_kernel,
        name="local_sums",
        grid=(1,),
        out_shape=array((clips, 2, chans), F32),
        in_specs=[pl.BlockSpec((seqs, EXTRA, 128), lambda i: (0, at, 0))],
        out_specs=pl.BlockSpec((clips, 2, chans), lambda i: (0, 0, 0)),
        compiler_params=pltpu.CompilerParams(vmem_limit_bytes=VMEM_LIMIT),
        cost_estimate=pl.CostEstimate(flops=10**6, bytes_accessed=10**5, transcendentals=0),
    )(blocks)


def token_kernel(count, x_ref, tokens_ref, stats_ref, parts_ref, out_ref):
    frames, stripe, chans, height = tokens_ref.shape
    seqs = x_ref.shape[0]
    sums = jnp.sum(parts_ref[...], axis=0)
    sums = group_sum(jnp.concatenate([sums, jnp.zeros((6, chans), F32)], axis=0)) / count
    first, second = (jnp.broadcast_to(sums[k : k + 1], (128, chans)).T for k in range(2))
    mean, scale = (jnp.broadcast_to(stats_ref[k : k + 1], (128, chans)).T for k in range(2))
    eye = one_hot(128, 128, lambda i: i)
    lanes = 16 * seqs

    order = one_hot(lanes, lanes, lambda i: ((i >> 2) & 3) * height + (i >> 4) * 4 + (i & 3))

    def turned(at):
        block = x_ref[:, at : at + 16].reshape(lanes, 128)
        return dot(nt_dot(eye, block).astype(BF16), order)

    rest = turned(8 * frames)
    for n in range(frames // 2):
        main = turned(16 * n)
        for k in range(2 * stripe):
            t, c = 2 * n + k // stripe, k % stripe
            at = stripe * n + c
            base = jnp.concatenate(
                [
                    main[:, height * k : height * (k + 1)],
                    rest[64 * (k // stripe) : 64 * (k // stripe + 1), height * at : height * (at + 1)],
                ],
                axis=0,
            )
            normed = (tokens_ref[t, c].astype(F32) - mean) * scale
            out_ref[t, c] = (base - (first + normed * second) * scale).astype(BF16)


def token_gradient(blocks, tokens, stats, parts, count):
    return call(
        functools.partial(token_kernel, count),
        "token_gradient",
        array(tokens.shape),
        vmem(4),
        [],
        10**9,
    )(blocks, tokens, stats, parts)


class Packed:
    def __init__(self, main, rows_pair, frames_pair):
        self.main, self.rows_pair, self.frames_pair = main, rows_pair, frames_pair

    def clear(self):
        self.rows_pair[...] = jnp.zeros_like(self.rows_pair)
        self.frames_pair[...] = jnp.zeros_like(self.frames_pair)

    def put(self, t, r, main, rest):
        self.main[t, r] = main
        self.rows_pair[t, r, :, 0:64] = rest
        self.frames_pair[t, r, :, 0:64] = rest
        if r > 0:
            self.rows_pair[t, r - 1, :, 64:128] = rest
        if not (isinstance(t, int) and t == 0):
            self.frames_pair[t - 1, r, :, 64:128] = rest

    def operands(self, t, count, rows):
        def get(ref, dt, dr):
            block = ref[pl.ds(t + dt, count), dr : dr + rows]
            return block.reshape(count * rows * block.shape[2], 128)

        tiles = [(get(self.main, dt, dr), [(dt, dr, 0)]) for dt in range(3) for dr in range(3)]
        for dt in range(3):
            tiles.append((get(self.rows_pair, dt, 0), [(dt, 0, 1), (dt, 1, 1)]))
        tiles.append((get(self.frames_pair, 0, 2), [(0, 2, 1), (1, 2, 1)]))
        tiles.append((get(self.rows_pair, 2, 2), [(2, 2, 1), None]))
        return [
            (jnp.concatenate([one, two], axis=1), has + more)
            for (one, has), (two, more) in zip(tiles[::2], tiles[1::2])
        ]


def packed_scratch(frames, rows, cols):
    return [pltpu.VMEM((frames, rows, cols, 128), BF16) for _ in range(3)]


PARTS = (slice(0, 128), slice(128, 192))


def fetch(source, target, sems):
    copies = [pltpu.make_async_copy(source.at[k], target.at[k], sems.at[k]) for k in range(3)]
    for copy in copies:
        copy.start()
    return copies


def mid_kernel(
    flags, stats, w_hbm, tile_hbm, before_ref, out_ref, sent_ref, *scratch
):
    main, rows_pair, frames_pair, weights, sems, tile_ref, sem = scratch
    tile_copy = pltpu.make_async_copy(tile_hbm, tile_ref, sem)
    tile_copy.start()
    copies = fetch(w_hbm, weights, sems)
    frames, rows, cols, chans = out_ref.shape
    size = 2 * rows * cols
    mean = stats[0:1]
    scale = stats[1:2]

    def activate(value, row, later):
        normed = (value.astype(F32) - mean) * scale
        act = normed / (1.0 + jnp.exp(-normed))
        if row < 2:
            act = act * flags[0]
        if row >= rows:
            act = act * flags[1]
        if later:
            act = act * flags[2]
        return act.astype(BF16)

    buffer = Packed(main, rows_pair, frames_pair)
    buffer.clear()
    for t in range(2):
        for r in range(rows + 2):
            act = activate(before_ref[t, r], r, True)
            buffer.put(t, r, act[:, :128], act[:, 128:])
    tile_copy.wait()

    def one_frame(t, carry):
        for r in range(rows + 2):
            act = activate(tile_ref[t, r], r, False)
            buffer.put(t + 2, r, act[:, :128], act[:, 128:])
        return carry

    lax.fori_loop(0, frames, one_frame, 0)
    for copy in copies:
        copy.wait()

    def two_frames(n, carry):
        t = 2 * n
        total = [jnp.zeros((size, chans), F32) for _ in range(3)]
        for lhs, holds in buffer.operands(t, 2, rows):
            for dc in range(3):
                taps = [
                    weights[tap[0], tap[1], dc, PARTS[tap[2]]]
                    if tap
                    else jnp.zeros((64, chans), BF16)
                    for tap in holds
                ]
                total[dc] = total[dc] + dot(lhs, jnp.concatenate(taps, axis=0))
        total = total[1] + from_left(total[0], cols) + from_right(total[2], cols)
        total = total.reshape(2, rows, cols, chans)
        total = total + tile_ref[pl.ds(t, 2), 1 : 1 + rows].astype(F32)
        out_ref[pl.ds(t, 2), 0:1] = (total[:, 0:1] * flags[0]).astype(BF16)
        out_ref[pl.ds(t, 2), 1 : rows - 1] = total[:, 1 : rows - 1].astype(BF16)
        out_ref[pl.ds(t, 2), rows - 1 : rows] = (total[:, rows - 1 :] * flags[1]).astype(BF16)
        return carry

    lax.fori_loop(0, frames // 2, two_frames, 0)
    for k in range(2):
        store_dense(sent_ref, k, out_ref[frames - 2 + k])


def middle(flags, stats, weights, tile, before):
    frames, ext, cols, chans = tile.shape
    rows = ext - 2
    return call(
        mid_kernel,
        "middle",
        (kept((frames, rows, cols, chans)), array((3, rows, cols, 128))),
        [smem()] + vmem(1) + [anywhere()] * 2 + vmem(1),
        [
            *packed_scratch(frames + 2, ext, cols),
            pltpu.VMEM(weights.shape, BF16),
            pltpu.SemaphoreType.DMA((3,)),
            pltpu.VMEM(tile.shape, BF16),
            pltpu.SemaphoreType.DMA,
        ],
        2 * frames * rows * cols * 27 * 65536,
    )(flags, stats, far(weights), tile, before)


def decode_kernel(
    w_hbm, before_ref, mid_ref, out_ref, main_ref, pair_ref, wide, weights, sems
):
    copies = fetch(w_hbm, weights, sems)
    frames, ext, cols, chans = mid_ref.shape
    lines, outs, _ = out_ref.shape[1:]
    rows = lines // 2
    pair_ref[:, ext - 1] = jnp.zeros_like(pair_ref[:, ext - 1])

    def put(at, main, rest):
        main_ref[at] = main
        pair_ref[at, :, :, 0:64] = rest
        pair_ref[at, 0 : ext - 1, :, 64:128] = rest[1:]

    for k in range(2):
        put(k, *load_dense(before_ref, k))

    def one_frame(t, carry):
        value = mid_ref[t]
        put(t + 2, value[..., :128], value[..., 128:])
        return carry

    lax.fori_loop(0, frames, one_frame, 0)
    eye = one_hot(outs, 128, lambda i: i)
    size = 2 * rows * cols

    for t in range(0, frames, 2):
        for i, taps in enumerate((((0, 3), (1, 1)), ((1, 2), (2, 0)))):
            here, aside = (jnp.zeros((size, 256), F32) for _ in range(2))
            tiles = []
            for dt in range(3):
                if t + i == 0:
                    copies[dt].wait()
                at = slice(t + dt, t + dt + 2)
                (dr, p), (below, q) = taps
                for ref, row, parts in (
                    (main_ref, dr, [(p, slice(0, 128))]),
                    (main_ref, below, [(q, slice(0, 128))]),
                    (pair_ref, dr, [(p, slice(128, 192)), (q, slice(128, 192))]),
                ):
                    lhs = ref[at, row : row + rows].reshape(size, 128)
                    tiles.append((lhs, [(weights.at[dt, tap], part) for tap, part in parts]))
            for n in range(0, len(tiles), 2):
                lhs = jnp.concatenate([lhs for lhs, _ in tiles[n : n + 2]], axis=1)
                taken = [tap for _, some in tiles[n : n + 2] for tap in some]
                for into, (one, two) in enumerate(((1, 2), (3, 0))):
                    rhs = [
                        jnp.concatenate([w[one, part], w[two, part]], axis=1) for w, part in taken
                    ]
                    rhs = jnp.concatenate(rhs, axis=0)
                    if into == 0:
                        here = here + dot(lhs, rhs)
                    else:
                        aside = aside + dot(lhs, rhs)
            even = (here[:, :128] + from_left(aside[:, :128], cols)).reshape(2, rows, cols, 128)
            odd = (here[:, 128:] + from_right(aside[:, 128:], cols)).reshape(2, rows, cols, 128)
            for k in range(2):
                for r in range(rows):
                    wide[k, 2 * r + i, pl.ds(0, cols, stride=2), :] = even[k, r]
                    wide[k, 2 * r + i, pl.ds(1, cols, stride=2), :] = odd[k, r]
        for k in range(2):
            for r in range(rows):
                pair = wide[k, 2 * r : 2 * r + 2].reshape(4 * cols, 128).astype(BF16)
                turned = nt_dot(eye, pair).astype(BF16)
                out_ref[t + k, 2 * r] = turned[:, 0 : 2 * cols]
                out_ref[t + k, 2 * r + 1] = turned[:, 2 * cols :]


def decode(weights, before, mid, outs):
    frames, ext, cols, chans = mid.shape
    rows = ext - 2
    return call(
        decode_kernel,
        "decode",
        array((frames, 2 * rows, outs, 2 * cols)),
        [anywhere()] + vmem(2),
        [
            pltpu.VMEM((frames + 2, ext, cols, 128), BF16),
            pltpu.VMEM((frames + 2, ext, cols, 128), BF16),
            pltpu.VMEM((2, 2 * rows, 2 * cols, 128), F32),
            pltpu.VMEM(weights.shape, BF16),
            pltpu.SemaphoreType.DMA((3,)),
        ],
        2 * frames * rows * cols * 24 * 65536,
    )(far(weights), before, mid)


def moved(block, clip_step, seq_step):
    clips, seqs = lax.axis_size("clip"), lax.axis_size("seq")
    if clip_step == 0:
        route = [(i - seq_step, i) for i in range(seqs) if 0 <= i - seq_step < seqs]
        return lax.ppermute(block, "seq", route)
    if seq_step == 0:
        route = [(i - clip_step, i) for i in range(clips) if 0 <= i - clip_step < clips]
        return lax.ppermute(block, "clip", route)
    route = [
        ((s - seq_step) * clips + c - clip_step, s * clips + c)
        for s in range(seqs)
        for c in range(clips)
        if 0 <= c - clip_step < clips and 0 <= s - seq_step < seqs
    ]
    return lax.ppermute(block, ("seq", "clip"), route)


def exchanged(blocks, axis):
    return lax.all_to_all(blocks, axis, 0, 0, tiled=True)


def body(tokens, conv_one, conv_two, pixel_grad):
    frames, height, stripe, chans = tokens.shape
    lines, wide, outs = pixel_grad.shape[1:]
    rows, cols = lines // 2, wide // 2
    clips, seqs = lax.axis_size("clip"), lax.axis_size("seq")
    clip, seq = lax.axis_index("clip"), lax.axis_index("seq")
    flags = jnp.stack([seq != 0, seq != seqs - 1, clip != 0]).astype(F32)
    tokens = tokens.transpose(0, 2, 3, 1)
    pixels = pixel_grad.transpose(0, 1, 3, 2)
    held = float(frames * height * stripe)

    first, last = edges(pixels)
    above, below = moved(last, 0, 1), moved(first, 0, -1)
    packed = pack(tokens, seqs)
    both = combined_weights(conv_two)
    above, both, packed = lax.optimization_barrier((above, both, packed))

    blocks = exchanged(packed, "seq")
    own = far(down_early(near(both), flags, pixels, above, below, rows + 2, cols))
    following = moved(own, -1, 0)
    tile, tile_last, parts = unpack(blocks, frames, cols, chans, clips, held)
    tile = far(tile)
    late = down_late(near(both), flags, pixels, above, below, rows + 2, cols)
    parts, late = lax.optimization_barrier((exchanged(parts, "clip"), late))
    parts, tile_last = lax.optimization_barrier((parts, tile_last))
    tile_z = moved(tile_last, 1, 0)

    blocks, stats = back(parts, held * seqs, conv_one, tile, own, late, following, seqs)
    home, stats = exchanged(blocks, "seq"), near(stats)

    mid, mid_last = middle(flags, stats, conv_one, tile, tile_z)
    decoded = decode(both, moved(mid_last, 1, 0), near(mid), outs)

    sums = exchanged(local_sums(home, frames, chans, clips), "clip")
    sums, decoded = lax.optimization_barrier((sums, decoded))
    count = held * seqs * clips * (chans // GROUPS)
    token_grad = token_gradient(home, tokens, stats, sums, count)
    return (decoded.transpose(0, 1, 3, 2), token_grad.transpose(0, 3, 1, 2))


def solution(mesh):
    return jax.shard_map(
        body,
        mesh=mesh,
        in_specs=(P("clip", None, "seq", None), P(), P(), P("clip", "seq", None, None)),
        out_specs=(P("clip", "seq", None, None), P("clip", None, "seq", None)),
        check_vma=False,
    )
```

```python
import functools

import jax
import jax.numpy as jnp
from jax import lax
from jax.experimental import pallas as pl
from jax.experimental.pallas import tpu as pltpu
from jax.sharding import PartitionSpec as P

GROUPS = 32
F32 = jnp.float32
BF16 = jnp.bfloat16
VMEM_LIMIT = 32 * 2**20
TAPS = ((2,), (1, 2), (0, 1), (0,))
EXTRA = 16


def vmem(count):
    return [pl.BlockSpec(memory_space=pltpu.VMEM)] * count


def smem():
    return pl.BlockSpec(memory_space=pltpu.SMEM)


def anywhere():
    return pl.BlockSpec(memory_space=pltpu.HBM)


def call(kernel, name, outs, in_specs, scratch, flops, moved_bytes=4 * 2**20):
    return pl.pallas_call(
        kernel,
        name=name,
        out_shape=outs,
        in_specs=in_specs,
        out_specs=jax.tree.map(lambda _: pl.BlockSpec(memory_space=pltpu.VMEM), outs),
        scratch_shapes=scratch,
        compiler_params=pltpu.CompilerParams(vmem_limit_bytes=VMEM_LIMIT),
        cost_estimate=pl.CostEstimate(flops=flops, bytes_accessed=moved_bytes, transcendentals=0),
    )


def array(shape, dtype=BF16):
    return jax.ShapeDtypeStruct(shape, dtype)


def kept(shape, dtype=BF16):
    return pltpu.VMEM(shape, dtype)


def near(block):
    return pltpu.with_memory_space_constraint(block, pltpu.VMEM)


def far(block):
    return pltpu.with_memory_space_constraint(block, pltpu.HBM)


def dot(lhs, rhs):
    return jnp.dot(lhs, rhs, preferred_element_type=F32)


def nt_dot(lhs, rhs):
    return lax.dot_general(lhs, rhs, (((1,), (1,)), ((), ())), preferred_element_type=F32)


def one_hot(rows, cols, place):
    width = min(cols, 128)
    target = place(lax.broadcasted_iota(jnp.int32, (rows, width), 0))
    target = target - lax.broadcasted_iota(jnp.int32, (rows, width), 1)
    blocks = [
        jnp.where(target == at, 1.0, 0.0).astype(BF16)[:, : cols - at]
        for at in range(0, cols, width)
    ]
    return jnp.concatenate(blocks, axis=1) if len(blocks) > 1 else blocks[0]


def same_group(chans):
    size = chans // GROUPS
    row = lax.broadcasted_iota(jnp.int32, (chans, chans), 0).astype(F32)
    col = lax.broadcasted_iota(jnp.int32, (chans, chans), 1).astype(F32)
    row, col = (jnp.floor((index + 0.5) / size) for index in (row, col))
    return jnp.where(row == col, 1.0, 0.0)


def group_sum(channels):
    return jnp.dot(
        channels,
        same_group(channels.shape[1]),
        precision=lax.Precision.HIGHEST,
        preferred_element_type=F32,
    )


def split_3(value):
    terms = []
    for _ in range(3):
        terms.append(value.astype(BF16).astype(F32))
        value = value - terms[-1]
    return terms


def extra_rows(one, two):
    rest = jnp.concatenate([one[:, 128:], two[:, 128:]], axis=1)
    row = lax.broadcasted_iota(jnp.int32, (EXTRA, 128), 0)
    out = jnp.zeros((EXTRA, 128), F32)
    for n, term in enumerate(split_3(one[:, :128]) + split_3(two[:, :128]) + split_3(rest)):
        out = jnp.where(row == n, term, out)
    return out


def from_extra(block):
    block = block.astype(F32)
    row = lax.broadcasted_iota(jnp.int32, block.shape, 1)
    one, two, rest = (
        jnp.sum(jnp.where((row >= k) & (row < k + 3), block, 0.0), axis=1) for k in (0, 3, 6)
    )
    return (
        jnp.concatenate([one, rest[:, :64]], axis=1),
        jnp.concatenate([two, rest[:, 64:]], axis=1),
    )


def store_dense(ref, frame, value):
    frames = ref.shape[0] * 2 // 3
    lane = 64 * (frame % 2)
    ref[frame] = value[..., :128]
    ref[frames + frame // 2, :, :, lane : lane + 64] = value[..., 128:]


def load_dense(ref, frame):
    frames = ref.shape[0] * 2 // 3
    lane = 64 * (frame % 2)
    return ref[frame], ref[frames + frame // 2, :, :, lane : lane + 64]


def from_left(value, cols):
    column = lax.broadcasted_iota(jnp.int32, value.shape, 0) & (cols - 1)
    return jnp.where(column == 0, 0.0, pltpu.roll(value, 1, 0))


def from_right(value, cols):
    size = value.shape[0]
    column = lax.broadcasted_iota(jnp.int32, value.shape, 0) & (cols - 1)
    return jnp.where(column == cols - 1, 0.0, pltpu.roll(value, size - 1, 0))


def fetch(source, target, sem):
    copy = pltpu.make_async_copy(source, target, sem)
    copy.start()
    return copy


def combine_kernel(w_ref, out_ref):
    outs = w_ref.shape[4]

    def one_time(a, carry):
        w = [[w_ref[a, b, d].astype(F32) for d in range(3)] for b in range(3)]
        for p in range(4):
            rows = [functools.reduce(jnp.add, [w[b][d] for b in TAPS[p]]) for d in range(3)]
            for q in range(4):
                value = functools.reduce(jnp.add, [rows[d] for d in TAPS[q]])
                out_ref[a, p, q] = jnp.pad(value, ((0, 0), (0, 128 - outs))).astype(BF16)
        return carry

    lax.fori_loop(0, 3, one_time, 0)


def combined_weights(conv_two):
    shape = kept((3, 4, 4, conv_two.shape[3], 128))
    return call(combine_kernel, "combine_weights", shape, vmem(1), [], 10**6)(conv_two)


def edges_kernel(x_hbm, first_hbm, last_hbm, near_ref, sems):
    lines = x_hbm.shape[1]
    ends = ((0, first_hbm), (lines - 3, last_hbm))
    for k, (at, _) in enumerate(ends):
        pltpu.make_async_copy(x_hbm.at[:, pl.ds(at, 3)], near_ref.at[k], sems.at[0, k]).start()
    copies = []
    for k, (at, ref) in enumerate(ends):
        pltpu.make_async_copy(x_hbm.at[:, pl.ds(at, 3)], near_ref.at[k], sems.at[0, k]).wait()
        copies.append(pltpu.make_async_copy(near_ref.at[k], ref, sems.at[1, k]))
        copies[k].start()
    for copy in copies:
        copy.wait()


def edges(pixels):
    frames, _, outs, wide = pixels.shape
    shape = pltpu.HBM((frames, 3, outs, wide), BF16)
    return pl.pallas_call(
        edges_kernel,
        name="edges",
        out_shape=(shape, shape),
        in_specs=[anywhere()],
        out_specs=(anywhere(), anywhere()),
        scratch_shapes=[
            pltpu.VMEM((2, *shape.shape), BF16),
            pltpu.SemaphoreType.DMA((2, 2)),
        ],
        cost_estimate=pl.CostEstimate(flops=10**6, bytes_accessed=10**6, transcendentals=0),
    )(far(pixels))


def own_moments(x_ref):
    frames, stripe, chans, height = x_ref.shape
    total = jnp.zeros((chans, height), F32)
    for t in range(frames):
        for c in range(stripe):
            total = total + x_ref[t, c].astype(F32)
    mean = jnp.sum(total, axis=1, keepdims=True) / float(frames * stripe * height)
    spread = jnp.zeros((chans, height), F32)
    for t in range(frames):
        for c in range(stripe):
            spread = spread + (x_ref[t, c].astype(F32) - mean) ** 2
    spread = jnp.sum(spread, axis=1, keepdims=True)
    return [jnp.broadcast_to(v, (chans, 128)).T[0:1] for v in (mean, spread)]


def merged(means, spreads, held):
    mean = jnp.sum(means, axis=0, keepdims=True) / means.shape[0]
    spread = jnp.sum(spreads, axis=0, keepdims=True)
    return mean, spread + held * jnp.sum((means - mean) ** 2, axis=0, keepdims=True)


def pack_kernel(x_ref, out_ref):
    frames, stripe, chans, height = x_ref.shape
    seqs = out_ref.shape[0]
    rows = height // seqs
    select = one_hot(8 * seqs, height, lambda i: rows * (i >> 3) - 2 + (i & 7))

    def picked(x):
        return nt_dot(select, x).reshape(seqs, 8, 128)

    for n in range(frames // 2):
        pair = [x_ref.at[2 * n + k] for k in range(2)]
        blocks = [[x[c, 0:128] for c in range(stripe)] for x in pair]
        tails = [[x[c, 128:chans] for x in pair] for c in range(stripe)]
        blocks.append([jnp.concatenate(tail, axis=0) for tail in tails])
        for k, columns in enumerate(blocks):
            at = 48 * n + 16 * k
            rows_of = [picked(column) for column in columns]
            out_ref[:, at : at + 16] = jnp.concatenate(rows_of, axis=1).astype(BF16)
    extra = extra_rows(*own_moments(x_ref)).astype(BF16)
    out_ref[:, 24 * frames :] = jnp.broadcast_to(extra[None], (seqs, EXTRA, 128))


def pack(tokens, seqs):
    shape = pltpu.HBM((seqs, 24 * tokens.shape[0] + EXTRA, 128), BF16)
    return call(pack_kernel, "pack", shape, vmem(1), [], 10**9)(tokens)


def unpack_kernel(held, x_ref, tile_ref, last_ref, parts_ref):
    seqs = x_ref.shape[0]
    frames, rows, cols, chans = tile_ref.shape
    size = rows * cols

    order = one_hot(size, 16 * seqs, lambda i: ((i >> 1) & 31) * 16 + (i & 1) * 8 + (i >> 6))
    for n in range(frames // 2):
        blocks = [x_ref[:, 48 * n + 16 * k : 48 * n + 16 * (k + 1)] for k in range(3)]
        blocks = [block.reshape(16 * seqs, 128) for block in blocks]
        main = dot(order, jnp.concatenate(blocks[:2], axis=1)).astype(BF16)
        rest = dot(order, blocks[2]).astype(BF16)
        for k in range(2):
            t = 2 * n + k
            for ref, at in ((tile_ref, t), (last_ref, t - frames + 2)):
                if at >= 0:
                    part = main[:, 128 * k : 128 * (k + 1)]
                    ref[at, :, :, 0:128] = part.reshape(rows, cols, 128)
                    part = rest[:, 64 * k : 64 * (k + 1)]
                    ref[at, :, :, 128:chans] = part.reshape(rows, cols, 64)
    parts = merged(*from_extra(x_ref[:, 24 * frames :]), held)
    parts_ref[...] = jnp.broadcast_to(jnp.concatenate(parts, axis=0)[None], parts_ref.shape)


def unpack(blocks, frames, cols, chans, clips, held):
    return call(
        functools.partial(unpack_kernel, held),
        "unpack",
        (
            pltpu.HBM((frames, 8, cols, chans), BF16),
            pltpu.HBM((2, 8, cols, chans), BF16),
            pltpu.HBM((clips, 2, chans), F32),
        ),
        vmem(1),
        [],
        10**9,
    )(blocks)


def group_stats(parts_ref, held):
    clips, _, chans = parts_ref.shape
    means, spreads = parts_ref[:, 0], parts_ref[:, 1]
    size = chans // GROUPS
    mean = group_sum(jnp.broadcast_to(jnp.sum(means, axis=0, keepdims=True), (8, chans)))
    mean = mean[0:1] / (clips * size)
    spread = jnp.sum(spreads, axis=0, keepdims=True)
    spread = spread + held * jnp.sum((means - mean) ** 2, axis=0, keepdims=True)
    var = group_sum(jnp.broadcast_to(spread, (8, chans)))[0:1] / (held * clips * size)
    return mean, lax.rsqrt(var + 1e-06)


def down_kernel(first, plan, weights, flags, sources, store, buffer, beside, sems):
    _, _, cols, _ = buffer.shape[1:]
    rows, outs = buffer.shape[2] - 1, weights.shape[3]
    pixels, *sides = sources
    count = buffer.shape[0]
    lines, chans, wide = pixels.shape[1:]
    copies = [
        pltpu.make_async_copy(side.at[pl.ds(first, count)], beside.at[k], sems.at[k])
        for k, side in enumerate(sides)
    ]
    for copy in copies:
        copy.start()
    select = one_hot(2 * cols, wide, lambda i: 2 * (i & (cols - 1)) + (i // cols))
    blank = jnp.zeros((128 - chans, wide), BF16)

    def line(i, n):
        if 3 <= n < 3 + lines:
            return pixels[first + i, n - 3]
        return beside[0, i, n] if n < 3 else beside[1, i, n - 3 - lines]

    def place(inner):
        def one_frame(i, carry):
            firsts = [n for n in range(0, lines + 6, 2) if (3 < n < 2 + lines) == inner]
            rhs = [x for n in firsts for k in range(2) for x in (line(i, n + k), blank)]
            picked = nt_dot(select, jnp.concatenate(rhs, axis=0)).astype(BF16)
            for m, n in enumerate(firsts):
                for k in range(2):
                    for j in range(2):
                        at = 256 * m + 128 * k
                        buffer[i, k, n // 2, :, 128 * j : 128 * (j + 1)] = picked[
                            cols * j : cols * (j + 1), at : at + 128
                        ]
            return carry

        lax.fori_loop(0, count, one_frame, 0)

    place(True)
    for copy in copies:
        copy.wait()
    place(False)

    size = rows * cols

    def products(frame, count, a, totals):
        here, left, right = totals
        frames = slice(frame - first, frame - first + count)
        lines = [
            buffer[frames, p % 2, p // 2 : p // 2 + rows].reshape(count * size, 256)
            for p in range(4)
        ]
        w = weights.at[a]
        for p in range(4):
            here = here + nt_dot(lines[p], jnp.concatenate([w[p, 1], w[p, 2]], axis=-1))
        for p in range(0, 4, 2):
            odd = jnp.concatenate([lines[p][:, 128:], lines[p + 1][:, 128:]], axis=-1)
            left = left + nt_dot(odd, jnp.concatenate([w[p, 0], w[p + 1, 0]], axis=-1))
            even = jnp.concatenate([lines[p][:, :128], lines[p + 1][:, :128]], axis=-1)
            right = right + nt_dot(even, jnp.concatenate([w[p, 3], w[p + 1, 3]], axis=-1))
        return here, left, right

    def zeros(count):
        return [jnp.zeros((count * size, outs), F32) for _ in range(3)]

    for n, (terms, extra, member) in enumerate(plan):
        totals = zeros(2)
        for frame, a in terms:
            totals = products(frame, 2, a, totals)
        here, left, right = totals
        total = here + from_left(left, cols) + from_right(right, cols)
        parts = [total[:size], total[size:]]
        if extra:
            here, left, right = products(*extra[:1], 1, *extra[1:], zeros(1))
            more = here + from_left(left, cols) + from_right(right, cols)
            parts[member] = parts[member] + more
        for k, part in enumerate(parts):
            part = part.reshape(rows, cols, outs)
            store(
                2 * n + k,
                [part[0:1] * flags[0], part[1 : rows - 1], part[rows - 1 :] * flags[1]],
            )


def early_kernel(plan, weights, flags, pixels, above, below, out_hbm, *scratch):
    *scratch, sent_ref, out_sems = scratch
    copies = [
        pltpu.make_async_copy(sent_ref.at[pl.ds(at, n)], out_hbm.at[pl.ds(at, n)], out_sems.at[k])
        for k, (at, n) in enumerate(((0, 2), (4, 1), (2, 2), (5, 1)))
    ]

    def store(n, parts):
        store_dense(sent_ref, n, jnp.concatenate([part.astype(BF16) for part in parts], axis=0))
        if n % 2 == 1:
            for copy in copies[n - 1 : n + 1]:
                copy.start()

    down_kernel(0, plan, weights, flags, (pixels, above, below), store, *scratch)
    for copy in copies:
        copy.wait()


def late_kernel(first, plan, weights, flags, pixels, above, below, out_ref, *scratch):
    def store(n, parts):
        out_ref[n] = jnp.concatenate(parts, axis=0)

    down_kernel(first, plan, weights, flags, (pixels, above, below), store, *scratch)


def down_scratch(count, pixels, rows, cols):
    _, _, chans, wide = pixels.shape
    return [
        pltpu.VMEM((count, 2, rows + 1, cols, 256), BF16),
        pltpu.VMEM((2, count, 3, chans, wide), BF16),
        pltpu.SemaphoreType.DMA((2,)),
    ]


def down_cost(plan, size):
    return 2 * sum(2 * len(terms) + 1 for terms, *_ in plan) * size * 8 * 65536


def down_early(weights, flags, pixels, above, below, rows, cols):
    frames = pixels.shape[0]
    plan = ((((0, 2), (1, 1), (2, 0)), (), 0), (((0, 0),), (0, 1), 1))
    return pl.pallas_call(
        functools.partial(early_kernel, plan),
        name="down_early",
        out_shape=pltpu.HBM((6, rows, cols, 128), BF16),
        in_specs=vmem(1) + [smem()] + vmem(1) + [anywhere()] * 2,
        out_specs=anywhere(),
        scratch_shapes=[
            *down_scratch(frames, pixels, rows, cols),
            pltpu.VMEM((6, rows, cols, 128), BF16),
            pltpu.SemaphoreType.DMA((4,)),
        ],
        compiler_params=pltpu.CompilerParams(vmem_limit_bytes=VMEM_LIMIT),
        cost_estimate=pl.CostEstimate(
            flops=down_cost(plan, rows * cols), bytes_accessed=4 * 2**20, transcendentals=0
        ),
    )(weights, flags, near(pixels), far(above), far(below))


def down_late(weights, flags, pixels, above, below, rows, cols):
    frames, outs = pixels.shape[0], weights.shape[3]
    plan = ((((2, 2),), (3, 1), 0),)
    return call(
        functools.partial(late_kernel, frames - 2, plan),
        "down_late",
        pltpu.HBM((2, rows, cols, outs), F32),
        vmem(1) + [smem()] + vmem(1) + [anywhere()] * 2,
        down_scratch(2, pixels, rows, cols),
        down_cost(plan, rows * cols),
    )(weights, flags, near(pixels), far(above), far(below))


def back_kernel(
    held, parts_ref, w_hbm, tile_hbm, own_hbm, late_hbm, next_hbm, out_ref, stats_ref, *scratch
):
    main, rows_pair, frames_pair, rest, weights, tile_ref, own_ref, late_ref, next_ref, sems = scratch
    frames, rows, cols, chans = tile_ref.shape
    pairs = (
        (own_hbm.at[pl.ds(0, 2)], own_ref.at[pl.ds(0, 2)]),
        (own_hbm.at[pl.ds(4, 1)], own_ref.at[pl.ds(2, 1)]),
        (next_hbm, next_ref),
        (late_hbm, late_ref),
        (w_hbm, weights),
        (tile_hbm.at[:, pl.ds(2, rows)], tile_ref),
    )
    copies = [pltpu.make_async_copy(*pair, sems.at[k]) for k, pair in enumerate(pairs)]
    for copy in copies:
        copy.start()
    seqs = out_ref.shape[0]
    size = 2 * rows * cols
    mean, scale = group_stats(parts_ref, held)
    stats_ref[...] = jnp.concatenate([mean, scale], axis=0)
    buffer = Packed(main, rows_pair, frames_pair)
    buffer.clear()
    for copy in copies[:3]:
        copy.wait()
    for k in range(2):
        for at, ref in ((k, own_ref), (frames + k, next_ref)):
            block, tail = load_dense(ref, k)
            for r in range(rows + 2):
                buffer.put(at, r, block[r], tail[r])
    copies[3].wait()
    for k in range(2):
        block, tail = load_dense(next_ref, 2 + k)
        late = late_ref[k]
        block = (late[..., :128] + block.astype(F32)).astype(BF16)
        tail = (late[..., 128:] + tail.astype(F32)).astype(BF16)
        for r in range(rows + 2):
            buffer.put(frames - 2 + k, r, block[r], tail[r])
    for copy in copies[4:]:
        copy.wait()
    order = one_hot(
        size,
        size,
        lambda i: ((i >> 3) & 1) * (rows * cols) + (i & 3) * cols + 2 * (i >> 4) + ((i >> 2) & 1),
    )

    def two_frames(n, carry):
        first_sum, second_sum = carry
        t = 2 * n
        total = [jnp.zeros((size, chans), F32) for _ in range(3)]
        for lhs, holds in buffer.operands(t, 2, rows):
            for dc in range(3):
                taps = [
                    weights[2 - tap[0], 2 - tap[1], 2 - dc, :, PARTS[tap[2]]]
                    if tap
                    else jnp.zeros((chans, 64), BF16)
                    for tap in holds
                ]
                total[dc] = total[dc] + nt_dot(lhs, jnp.concatenate(taps, axis=1))
        total = total[1] + from_left(total[0], cols) + from_right(total[2], cols)
        tile = tile_ref[pl.ds(t, 2)].reshape(size, chans)
        normed = (tile.astype(F32) - mean) * scale
        sigmoid = 1.0 / (1.0 + jnp.exp(-normed))
        grad = total * sigmoid * (1.0 + normed * (1.0 - sigmoid))
        first_sum = first_sum + jnp.sum(grad, axis=0, keepdims=True)
        second_sum = second_sum + jnp.sum(grad * normed, axis=0, keepdims=True)
        own = [
            ref[pl.ds(t, 2), 1 : 1 + rows].reshape(size, 128) for ref in (main, rows_pair)
        ]
        own = jnp.concatenate(own, axis=1)[:, :chans].astype(F32)
        base = (own + grad * scale).astype(BF16)
        home = dot(order, base)
        block = home[:, :128].reshape(seqs, 16, 128).astype(BF16)
        out_ref[:, pl.ds(pl.multiple_of(16 * n, 16), 16)] = block
        tail = home[:, 128:].reshape(seqs, 2, 8, chans - 128)
        for k in range(2):
            rest[n, :, :, 64 * k : 64 * (k + 1)] = tail[:, k]
        return first_sum, second_sum

    none = jnp.zeros((1, chans), F32)
    sums = lax.fori_loop(0, frames // 2, two_frames, (none, none))
    both = jnp.concatenate([rest[n] for n in range(frames // 2)], axis=1)
    out_ref[:, 8 * frames : 12 * frames] = both.astype(BF16)
    extra = extra_rows(*sums).astype(BF16)
    out_ref[:, 12 * frames :] = jnp.broadcast_to(extra[None], (seqs, EXTRA, 128))


def back(parts, held, weights, tile, own, late, following, seqs):
    frames, ext, cols, chans = tile.shape
    rows = ext - 4
    return call(
        functools.partial(back_kernel, held),
        "back",
        (pltpu.HBM((seqs, 12 * frames + EXTRA, 128), BF16), kept((2, chans), F32)),
        vmem(1) + [anywhere()] * 5,
        [
            *packed_scratch(frames + 2, rows + 2, cols),
            pltpu.VMEM((frames // 2, seqs, 8, 128), F32),
            pltpu.VMEM(weights.shape, BF16),
            pltpu.VMEM((frames, rows, cols, chans), BF16),
            pltpu.VMEM((3, *own.shape[1:]), BF16),
            pltpu.VMEM(late.shape, F32),
            pltpu.VMEM(following.shape, BF16),
            pltpu.SemaphoreType.DMA((6,)),
        ],
        2 * frames * rows * cols * 21 * 65536,
    )(parts, far(weights), far(tile), far(own), far(late), far(following))


def sums_kernel(x_ref, out_ref):
    one, two = from_extra(x_ref[...])
    sums = [jnp.sum(v, axis=0, keepdims=True) for v in (one, two)]
    out_ref[...] = jnp.broadcast_to(jnp.concatenate(sums, axis=0)[None], out_ref.shape)


def local_sums(blocks, frames, chans, clips):
    seqs = blocks.shape[0]
    at = 12 * frames // EXTRA
    return pl.pallas_call(
        sums_kernel,
        name="local_sums",
        grid=(1,),
        out_shape=array((clips, 2, chans), F32),
        in_specs=[pl.BlockSpec((seqs, EXTRA, 128), lambda i: (0, at, 0))],
        out_specs=pl.BlockSpec((clips, 2, chans), lambda i: (0, 0, 0)),
        compiler_params=pltpu.CompilerParams(vmem_limit_bytes=VMEM_LIMIT),
        cost_estimate=pl.CostEstimate(flops=10**6, bytes_accessed=10**5, transcendentals=0),
    )(blocks)


def token_kernel(count, x_ref, tokens_ref, stats_ref, parts_ref, out_ref):
    frames, stripe, chans, height = tokens_ref.shape
    seqs = x_ref.shape[0]
    sums = jnp.sum(parts_ref[...], axis=0)
    sums = group_sum(jnp.concatenate([sums, jnp.zeros((6, chans), F32)], axis=0)) / count
    first, second = (jnp.broadcast_to(sums[k : k + 1], (128, chans)).T for k in range(2))
    mean, scale = (jnp.broadcast_to(stats_ref[k : k + 1], (128, chans)).T for k in range(2))
    eye = one_hot(128, 128, lambda i: i)
    lanes = 16 * seqs

    order = one_hot(lanes, lanes, lambda i: ((i >> 2) & 3) * height + (i >> 4) * 4 + (i & 3))

    def turned(at):
        block = x_ref[:, at : at + 16].reshape(lanes, 128)
        return dot(nt_dot(eye, block).astype(BF16), order)

    rest = turned(8 * frames)
    for n in range(frames // 2):
        main = turned(16 * n)
        for k in range(2 * stripe):
            t, c = 2 * n + k // stripe, k % stripe
            at = stripe * n + c
            base = jnp.concatenate(
                [
                    main[:, height * k : height * (k + 1)],
                    rest[64 * (k // stripe) : 64 * (k // stripe + 1), height * at : height * (at + 1)],
                ],
                axis=0,
            )
            normed = (tokens_ref[t, c].astype(F32) - mean) * scale
            out_ref[t, c] = (base - (first + normed * second) * scale).astype(BF16)


def token_gradient(blocks, tokens, stats, parts, count):
    return call(
        functools.partial(token_kernel, count),
        "token_gradient",
        array(tokens.shape),
        vmem(4),
        [],
        10**9,
    )(blocks, tokens, stats, parts)


class Packed:
    def __init__(self, main, rows_pair, frames_pair):
        self.main, self.rows_pair, self.frames_pair = main, rows_pair, frames_pair

    def clear(self):
        self.rows_pair[...] = jnp.zeros_like(self.rows_pair)
        self.frames_pair[...] = jnp.zeros_like(self.frames_pair)

    def put(self, t, r, main, rest):
        self.main[t, r] = main
        self.rows_pair[t, r, :, 0:64] = rest
        self.frames_pair[t, r, :, 0:64] = rest
        if r > 0:
            self.rows_pair[t, r - 1, :, 64:128] = rest
        if not (isinstance(t, int) and t == 0):
            self.frames_pair[t - 1, r, :, 64:128] = rest

    def operands(self, t, count, rows):
        def get(ref, dt, dr):
            block = ref[pl.ds(t + dt, count), dr : dr + rows]
            return block.reshape(count * rows * block.shape[2], 128)

        tiles = [(get(self.main, dt, dr), [(dt, dr, 0)]) for dt in range(3) for dr in range(3)]
        for dt in range(3):
            tiles.append((get(self.rows_pair, dt, 0), [(dt, 0, 1), (dt, 1, 1)]))
        tiles.append((get(self.frames_pair, 0, 2), [(0, 2, 1), (1, 2, 1)]))
        tiles.append((get(self.rows_pair, 2, 2), [(2, 2, 1), None]))
        return [
            (jnp.concatenate([one, two], axis=1), has + more)
            for (one, has), (two, more) in zip(tiles[::2], tiles[1::2])
        ]


def packed_scratch(frames, rows, cols):
    return [pltpu.VMEM((frames, rows, cols, 128), BF16) for _ in range(3)]


PARTS = (slice(0, 128), slice(128, 192))


def fetch(source, target, sems):
    copies = [pltpu.make_async_copy(source.at[k], target.at[k], sems.at[k]) for k in range(3)]
    for copy in copies:
        copy.start()
    return copies


def mid_kernel(
    flags, stats, w_hbm, tile_hbm, before_ref, out_ref, sent_ref, *scratch
):
    main, rows_pair, frames_pair, weights, sems, tile_ref, sem = scratch
    tile_copy = pltpu.make_async_copy(tile_hbm, tile_ref, sem)
    tile_copy.start()
    copies = fetch(w_hbm, weights, sems)
    frames, rows, cols, chans = out_ref.shape
    size = 2 * rows * cols
    mean = stats[0:1]
    scale = stats[1:2]

    def activate(value, row, later):
        normed = (value.astype(F32) - mean) * scale
        act = normed / (1.0 + jnp.exp(-normed))
        if row < 2:
            act = act * flags[0]
        if row >= rows:
            act = act * flags[1]
        if later:
            act = act * flags[2]
        return act.astype(BF16)

    buffer = Packed(main, rows_pair, frames_pair)
    buffer.clear()
    for t in range(2):
        for r in range(rows + 2):
            act = activate(before_ref[t, r], r, True)
            buffer.put(t, r, act[:, :128], act[:, 128:])
    tile_copy.wait()

    def one_frame(t, carry):
        for r in range(rows + 2):
            act = activate(tile_ref[t, r], r, False)
            buffer.put(t + 2, r, act[:, :128], act[:, 128:])
        return carry

    lax.fori_loop(0, frames, one_frame, 0)
    for copy in copies:
        copy.wait()

    def two_frames(n, carry):
        t = 2 * n
        total = [jnp.zeros((size, chans), F32) for _ in range(3)]
        for lhs, holds in buffer.operands(t, 2, rows):
            for dc in range(3):
                taps = [
                    weights[tap[0], tap[1], dc, PARTS[tap[2]]]
                    if tap
                    else jnp.zeros((64, chans), BF16)
                    for tap in holds
                ]
                total[dc] = total[dc] + dot(lhs, jnp.concatenate(taps, axis=0))
        total = total[1] + from_left(total[0], cols) + from_right(total[2], cols)
        total = total.reshape(2, rows, cols, chans)
        total = total + tile_ref[pl.ds(t, 2), 1 : 1 + rows].astype(F32)
        out_ref[pl.ds(t, 2), 0:1] = (total[:, 0:1] * flags[0]).astype(BF16)
        out_ref[pl.ds(t, 2), 1 : rows - 1] = total[:, 1 : rows - 1].astype(BF16)
        out_ref[pl.ds(t, 2), rows - 1 : rows] = (total[:, rows - 1 :] * flags[1]).astype(BF16)
        return carry

    lax.fori_loop(0, frames // 2, two_frames, 0)
    for k in range(2):
        store_dense(sent_ref, k, out_ref[frames - 2 + k])


def middle(flags, stats, weights, tile, before):
    frames, ext, cols, chans = tile.shape
    rows = ext - 2
    return call(
        mid_kernel,
        "middle",
        (kept((frames, rows, cols, chans)), array((3, rows, cols, 128))),
        [smem()] + vmem(1) + [anywhere()] * 2 + vmem(1),
        [
            *packed_scratch(frames + 2, ext, cols),
            pltpu.VMEM(weights.shape, BF16),
            pltpu.SemaphoreType.DMA((3,)),
            pltpu.VMEM(tile.shape, BF16),
            pltpu.SemaphoreType.DMA,
        ],
        2 * frames * rows * cols * 27 * 65536,
    )(flags, stats, far(weights), tile, before)


def bring_kernel(x_hbm, out_ref, sem):
    copy = pltpu.make_async_copy(x_hbm, out_ref, sem)
    copy.start()
    copy.wait()


def brought(x):
    scratch = [pltpu.SemaphoreType.DMA]
    return near(call(bring_kernel, "bring", kept(x.shape), [anywhere()], scratch, 10**6)(far(x)))


def decode_kernel(weights, before_ref, mid_ref, out_ref, main_ref, pair_ref, wide):
    frames, ext, cols, chans = mid_ref.shape
    lines, outs, _ = out_ref.shape[1:]
    rows = lines // 2
    pair_ref[:, ext - 1] = jnp.zeros_like(pair_ref[:, ext - 1])

    def put(at, main, rest):
        main_ref[at] = main
        pair_ref[at, :, :, 0:64] = rest
        pair_ref[at, 0 : ext - 1, :, 64:128] = rest[1:]

    for k in range(2):
        put(k, *load_dense(before_ref, k))

    def one_frame(t, carry):
        value = mid_ref[t]
        put(t + 2, value[..., :128], value[..., 128:])
        return carry

    lax.fori_loop(0, frames, one_frame, 0)
    eye = one_hot(outs, 128, lambda i: i)
    size = 2 * rows * cols

    for t in range(0, frames, 2):
        for i, taps in enumerate((((0, 3), (1, 1)), ((1, 2), (2, 0)))):
            here, aside = (jnp.zeros((size, 256), F32) for _ in range(2))
            tiles = []
            for dt in range(3):
                at = slice(t + dt, t + dt + 2)
                (dr, p), (below, q) = taps
                for ref, row, parts in (
                    (main_ref, dr, [(p, slice(0, 128))]),
                    (main_ref, below, [(q, slice(0, 128))]),
                    (pair_ref, dr, [(p, slice(128, 192)), (q, slice(128, 192))]),
                ):
                    lhs = ref[at, row : row + rows].reshape(size, 128)
                    tiles.append((lhs, [(weights.at[dt, tap], part) for tap, part in parts]))
            for n in range(0, len(tiles), 2):
                lhs = jnp.concatenate([lhs for lhs, _ in tiles[n : n + 2]], axis=1)
                taken = [tap for _, some in tiles[n : n + 2] for tap in some]
                for into, (one, two) in enumerate(((1, 2), (3, 0))):
                    rhs = [
                        jnp.concatenate([w[one, part], w[two, part]], axis=1) for w, part in taken
                    ]
                    rhs = jnp.concatenate(rhs, axis=0)
                    if into == 0:
                        here = here + dot(lhs, rhs)
                    else:
                        aside = aside + dot(lhs, rhs)
            even = (here[:, :128] + from_left(aside[:, :128], cols)).reshape(2, rows, cols, 128)
            odd = (here[:, 128:] + from_right(aside[:, 128:], cols)).reshape(2, rows, cols, 128)
            for k in range(2):
                for r in range(rows):
                    wide[k, 2 * r + i, pl.ds(0, cols, stride=2), :] = even[k, r]
                    wide[k, 2 * r + i, pl.ds(1, cols, stride=2), :] = odd[k, r]
        for k in range(2):
            for r in range(rows):
                pair = wide[k, 2 * r : 2 * r + 2].reshape(4 * cols, 128).astype(BF16)
                turned = nt_dot(eye, pair).astype(BF16)
                out_ref[t + k, 2 * r] = turned[:, 0 : 2 * cols]
                out_ref[t + k, 2 * r + 1] = turned[:, 2 * cols :]


def decode(weights, before, mid, outs):
    frames, ext, cols, chans = mid.shape
    rows = ext - 2
    return call(
        decode_kernel,
        "decode",
        array((frames, 2 * rows, outs, 2 * cols)),
        vmem(3),
        [
            pltpu.VMEM((frames + 2, ext, cols, 128), BF16),
            pltpu.VMEM((frames + 2, ext, cols, 128), BF16),
            pltpu.VMEM((2, 2 * rows, 2 * cols, 128), F32),
        ],
        2 * frames * rows * cols * 24 * 65536,
    )(weights, before, mid)


def moved(block, clip_step, seq_step):
    clips, seqs = lax.axis_size("clip"), lax.axis_size("seq")
    if clip_step == 0:
        route = [(i - seq_step, i) for i in range(seqs) if 0 <= i - seq_step < seqs]
        return lax.ppermute(block, "seq", route)
    if seq_step == 0:
        route = [(i - clip_step, i) for i in range(clips) if 0 <= i - clip_step < clips]
        return lax.ppermute(block, "clip", route)
    route = [
        ((s - seq_step) * clips + c - clip_step, s * clips + c)
        for s in range(seqs)
        for c in range(clips)
        if 0 <= c - clip_step < clips and 0 <= s - seq_step < seqs
    ]
    return lax.ppermute(block, ("seq", "clip"), route)


def exchanged(blocks, axis):
    return lax.all_to_all(blocks, axis, 0, 0, tiled=True)


def body(tokens, conv_one, conv_two, pixel_grad):
    frames, height, stripe, chans = tokens.shape
    lines, wide, outs = pixel_grad.shape[1:]
    rows, cols = lines // 2, wide // 2
    clips, seqs = lax.axis_size("clip"), lax.axis_size("seq")
    clip, seq = lax.axis_index("clip"), lax.axis_index("seq")
    flags = jnp.stack([seq != 0, seq != seqs - 1, clip != 0]).astype(F32)
    tokens = tokens.transpose(0, 2, 3, 1)
    pixels = pixel_grad.transpose(0, 1, 3, 2)
    held = float(frames * height * stripe)

    first, last = edges(pixels)
    above, below = moved(last, 0, 1), moved(first, 0, -1)
    packed = pack(tokens, seqs)
    both = combined_weights(conv_two)
    above, both, packed = lax.optimization_barrier((above, both, packed))

    blocks = exchanged(packed, "seq")
    own = far(down_early(near(both), flags, pixels, above, below, rows + 2, cols))
    following = moved(own, -1, 0)
    tile, tile_last, parts = unpack(blocks, frames, cols, chans, clips, held)
    tile = far(tile)
    late = down_late(near(both), flags, pixels, above, below, rows + 2, cols)
    parts, late = lax.optimization_barrier((exchanged(parts, "clip"), late))
    parts, tile_last = lax.optimization_barrier((parts, tile_last))
    tile_z = moved(tile_last, 1, 0)

    blocks, stats = back(parts, held * seqs, conv_one, tile, own, late, following, seqs)
    home, stats = exchanged(blocks, "seq"), near(stats)

    mid, mid_last = middle(flags, stats, conv_one, tile, tile_z)
    sums, both = lax.optimization_barrier((local_sums(home, frames, chans, clips), both))
    decoded = decode(brought(both), moved(mid_last, 1, 0), near(mid), outs)

    sums = exchanged(sums, "clip")
    sums, decoded = lax.optimization_barrier((sums, decoded))
    count = held * seqs * clips * (chans // GROUPS)
    token_grad = token_gradient(home, tokens, stats, sums, count)
    return (decoded.transpose(0, 1, 3, 2), token_grad.transpose(0, 3, 1, 2))


def solution(mesh):
    return jax.shard_map(
        body,
        mesh=mesh,
        in_specs=(P("clip", None, "seq", None), P(), P(), P("clip", "seq", None, None)),
        out_specs=(P("clip", "seq", None, None), P("clip", None, "seq", None)),
        check_vma=False,
    )
```

```python
import functools

import jax
import jax.numpy as jnp
from jax import lax
from jax.experimental import pallas as pl
from jax.experimental.pallas import tpu as pltpu
from jax.sharding import PartitionSpec as P

GROUPS = 32
F32 = jnp.float32
BF16 = jnp.bfloat16
VMEM_LIMIT = 32 * 2**20
TAPS = ((2,), (1, 2), (0, 1), (0,))
EXTRA = 16


def vmem(count):
    return [pl.BlockSpec(memory_space=pltpu.VMEM)] * count


def smem():
    return pl.BlockSpec(memory_space=pltpu.SMEM)


def anywhere():
    return pl.BlockSpec(memory_space=pltpu.HBM)


def call(kernel, name, outs, in_specs, scratch, flops, moved_bytes=4 * 2**20):
    return pl.pallas_call(
        kernel,
        name=name,
        out_shape=outs,
        in_specs=in_specs,
        out_specs=jax.tree.map(lambda _: pl.BlockSpec(memory_space=pltpu.VMEM), outs),
        scratch_shapes=scratch,
        compiler_params=pltpu.CompilerParams(vmem_limit_bytes=VMEM_LIMIT),
        cost_estimate=pl.CostEstimate(flops=flops, bytes_accessed=moved_bytes, transcendentals=0),
    )


def array(shape, dtype=BF16):
    return jax.ShapeDtypeStruct(shape, dtype)


def kept(shape, dtype=BF16):
    return pltpu.VMEM(shape, dtype)


def near(block):
    return pltpu.with_memory_space_constraint(block, pltpu.VMEM)


def far(block):
    return pltpu.with_memory_space_constraint(block, pltpu.HBM)


def dot(lhs, rhs):
    return jnp.dot(lhs, rhs, preferred_element_type=F32)


def nt_dot(lhs, rhs):
    return lax.dot_general(lhs, rhs, (((1,), (1,)), ((), ())), preferred_element_type=F32)


def one_hot(rows, cols, place):
    width = min(cols, 128)
    target = place(lax.broadcasted_iota(jnp.int32, (rows, width), 0))
    target = target - lax.broadcasted_iota(jnp.int32, (rows, width), 1)
    blocks = [
        jnp.where(target == at, 1.0, 0.0).astype(BF16)[:, : cols - at]
        for at in range(0, cols, width)
    ]
    return jnp.concatenate(blocks, axis=1) if len(blocks) > 1 else blocks[0]


def same_group(chans):
    size = chans // GROUPS
    row = lax.broadcasted_iota(jnp.int32, (chans, chans), 0).astype(F32)
    col = lax.broadcasted_iota(jnp.int32, (chans, chans), 1).astype(F32)
    row, col = (jnp.floor((index + 0.5) / size) for index in (row, col))
    return jnp.where(row == col, 1.0, 0.0)


def group_sum(channels):
    return jnp.dot(
        channels,
        same_group(channels.shape[1]),
        precision=lax.Precision.HIGHEST,
        preferred_element_type=F32,
    )


def split_3(value):
    terms = []
    for _ in range(3):
        terms.append(value.astype(BF16).astype(F32))
        value = value - terms[-1]
    return terms


def extra_rows(one, two):
    rest = jnp.concatenate([one[:, 128:], two[:, 128:]], axis=1)
    row = lax.broadcasted_iota(jnp.int32, (EXTRA, 128), 0)
    out = jnp.zeros((EXTRA, 128), F32)
    for n, term in enumerate(split_3(one[:, :128]) + split_3(two[:, :128]) + split_3(rest)):
        out = jnp.where(row == n, term, out)
    return out


def from_extra(block):
    block = block.astype(F32)
    row = lax.broadcasted_iota(jnp.int32, block.shape, 1)
    one, two, rest = (
        jnp.sum(jnp.where((row >= k) & (row < k + 3), block, 0.0), axis=1) for k in (0, 3, 6)
    )
    return (
        jnp.concatenate([one, rest[:, :64]], axis=1),
        jnp.concatenate([two, rest[:, 64:]], axis=1),
    )


def store_dense(ref, frame, value):
    frames = ref.shape[0] * 2 // 3
    lane = 64 * (frame % 2)
    ref[frame] = value[..., :128]
    ref[frames + frame // 2, :, :, lane : lane + 64] = value[..., 128:]


def load_dense(ref, frame):
    frames = ref.shape[0] * 2 // 3
    lane = 64 * (frame % 2)
    return ref[frame], ref[frames + frame // 2, :, :, lane : lane + 64]


def from_left(value, cols):
    column = lax.broadcasted_iota(jnp.int32, value.shape, 0) & (cols - 1)
    return jnp.where(column == 0, 0.0, pltpu.roll(value, 1, 0))


def from_right(value, cols):
    size = value.shape[0]
    column = lax.broadcasted_iota(jnp.int32, value.shape, 0) & (cols - 1)
    return jnp.where(column == cols - 1, 0.0, pltpu.roll(value, size - 1, 0))


def fetch(source, target, sem):
    copy = pltpu.make_async_copy(source, target, sem)
    copy.start()
    return copy


def combine_kernel(w_ref, out_ref):
    outs = w_ref.shape[4]

    def one_time(a, carry):
        w = [[w_ref[a, b, d].astype(F32) for d in range(3)] for b in range(3)]
        for p in range(4):
            rows = [functools.reduce(jnp.add, [w[b][d] for b in TAPS[p]]) for d in range(3)]
            for q in range(4):
                value = functools.reduce(jnp.add, [rows[d] for d in TAPS[q]])
                out_ref[a, p, q] = jnp.pad(value, ((0, 0), (0, 128 - outs))).astype(BF16)
        return carry

    lax.fori_loop(0, 3, one_time, 0)


def combined_weights(conv_two):
    shape = kept((3, 4, 4, conv_two.shape[3], 128))
    return call(combine_kernel, "combine_weights", shape, vmem(1), [], 10**6)(conv_two)


def edges_kernel(x_hbm, tokens_hbm, first_hbm, last_hbm, tokens_ref, near_ref, sems, sem):
    lines = x_hbm.shape[1]
    ends = ((0, first_hbm), (lines - 3, last_hbm))
    for k, (at, _) in enumerate(ends):
        pltpu.make_async_copy(x_hbm.at[:, pl.ds(at, 3)], near_ref.at[k], sems.at[0, k]).start()
    copies = [pltpu.make_async_copy(tokens_hbm, tokens_ref, sem)]
    copies[0].start()
    for k, (at, ref) in enumerate(ends):
        pltpu.make_async_copy(x_hbm.at[:, pl.ds(at, 3)], near_ref.at[k], sems.at[0, k]).wait()
        copies.append(pltpu.make_async_copy(near_ref.at[k], ref, sems.at[1, k]))
        copies[k + 1].start()
    for copy in copies:
        copy.wait()


def edges(pixels, tokens):
    frames, _, outs, wide = pixels.shape
    shape = pltpu.HBM((frames, 3, outs, wide), BF16)
    return pl.pallas_call(
        edges_kernel,
        name="edges",
        out_shape=(shape, shape, kept(tokens.shape)),
        in_specs=[anywhere(), anywhere()],
        out_specs=(anywhere(), anywhere(), *vmem(1)),
        scratch_shapes=[
            pltpu.VMEM((2, *shape.shape), BF16),
            pltpu.SemaphoreType.DMA((2, 2)),
            pltpu.SemaphoreType.DMA,
        ],
        cost_estimate=pl.CostEstimate(flops=10**6, bytes_accessed=10**6, transcendentals=0),
    )(far(pixels), far(tokens))


def own_moments(x_ref):
    frames, stripe, chans, height = x_ref.shape
    total = jnp.zeros((chans, height), F32)
    for t in range(frames):
        for c in range(stripe):
            total = total + x_ref[t, c].astype(F32)
    mean = jnp.sum(total, axis=1, keepdims=True) / float(frames * stripe * height)
    spread = jnp.zeros((chans, height), F32)
    for t in range(frames):
        for c in range(stripe):
            spread = spread + (x_ref[t, c].astype(F32) - mean) ** 2
    spread = jnp.sum(spread, axis=1, keepdims=True)
    return [jnp.broadcast_to(v, (chans, 128)).T[0:1] for v in (mean, spread)]


def merged(means, spreads, held):
    mean = jnp.sum(means, axis=0, keepdims=True) / means.shape[0]
    spread = jnp.sum(spreads, axis=0, keepdims=True)
    return mean, spread + held * jnp.sum((means - mean) ** 2, axis=0, keepdims=True)


def pack_kernel(x_ref, out_ref):
    frames, stripe, chans, height = x_ref.shape
    seqs = out_ref.shape[0]
    rows = height // seqs
    select = one_hot(8 * seqs, height, lambda i: rows * (i >> 3) - 2 + (i & 7))

    def picked(x):
        return nt_dot(select, x).reshape(seqs, 8, 128)

    for n in range(frames // 2):
        pair = [x_ref.at[2 * n + k] for k in range(2)]
        blocks = [[x[c, 0:128] for c in range(stripe)] for x in pair]
        tails = [[x[c, 128:chans] for x in pair] for c in range(stripe)]
        blocks.append([jnp.concatenate(tail, axis=0) for tail in tails])
        for k, columns in enumerate(blocks):
            at = 48 * n + 16 * k
            rows_of = [picked(column) for column in columns]
            out_ref[:, at : at + 16] = jnp.concatenate(rows_of, axis=1).astype(BF16)
    extra = extra_rows(*own_moments(x_ref)).astype(BF16)
    out_ref[:, 24 * frames :] = jnp.broadcast_to(extra[None], (seqs, EXTRA, 128))


def pack(tokens, seqs):
    shape = pltpu.HBM((seqs, 24 * tokens.shape[0] + EXTRA, 128), BF16)
    return call(pack_kernel, "pack", shape, vmem(1), [], 10**9)(tokens)


def unpack_kernel(held, x_ref, tile_ref, last_ref, parts_ref):
    seqs = x_ref.shape[0]
    frames, rows, cols, chans = tile_ref.shape
    size = rows * cols

    order = one_hot(size, 16 * seqs, lambda i: ((i >> 1) & 31) * 16 + (i & 1) * 8 + (i >> 6))
    for n in range(frames // 2):
        blocks = [x_ref[:, 48 * n + 16 * k : 48 * n + 16 * (k + 1)] for k in range(3)]
        blocks = [block.reshape(16 * seqs, 128) for block in blocks]
        main = dot(order, jnp.concatenate(blocks[:2], axis=1)).astype(BF16)
        rest = dot(order, blocks[2]).astype(BF16)
        for k in range(2):
            t = 2 * n + k
            for ref, at in ((tile_ref, t), (last_ref, t - frames + 2)):
                if at >= 0:
                    part = main[:, 128 * k : 128 * (k + 1)]
                    ref[at, :, :, 0:128] = part.reshape(rows, cols, 128)
                    part = rest[:, 64 * k : 64 * (k + 1)]
                    ref[at, :, :, 128:chans] = part.reshape(rows, cols, 64)
    parts = merged(*from_extra(x_ref[:, 24 * frames :]), held)
    parts_ref[...] = jnp.broadcast_to(jnp.concatenate(parts, axis=0)[None], parts_ref.shape)


def unpack(blocks, frames, cols, chans, clips, held):
    return call(
        functools.partial(unpack_kernel, held),
        "unpack",
        (
            pltpu.HBM((frames, 8, cols, chans), BF16),
            pltpu.HBM((2, 8, cols, chans), BF16),
            pltpu.HBM((clips, 2, chans), F32),
        ),
        vmem(1),
        [],
        10**9,
    )(blocks)


def group_stats(parts_ref, held):
    clips, _, chans = parts_ref.shape
    means, spreads = parts_ref[:, 0], parts_ref[:, 1]
    size = chans // GROUPS
    mean = group_sum(jnp.broadcast_to(jnp.sum(means, axis=0, keepdims=True), (8, chans)))
    mean = mean[0:1] / (clips * size)
    spread = jnp.sum(spreads, axis=0, keepdims=True)
    spread = spread + held * jnp.sum((means - mean) ** 2, axis=0, keepdims=True)
    var = group_sum(jnp.broadcast_to(spread, (8, chans)))[0:1] / (held * clips * size)
    return mean, lax.rsqrt(var + 1e-06)


def down_kernel(first, plan, weights, flags, sources, store, buffer, beside, sems):
    _, _, cols, _ = buffer.shape[1:]
    rows, outs = buffer.shape[2] - 1, weights.shape[3]
    pixels, *sides = sources
    count = buffer.shape[0]
    lines, chans, wide = pixels.shape[1:]
    copies = [
        pltpu.make_async_copy(side.at[pl.ds(first, count)], beside.at[k], sems.at[k])
        for k, side in enumerate(sides)
    ]
    for copy in copies:
        copy.start()
    select = one_hot(2 * cols, wide, lambda i: 2 * (i & (cols - 1)) + (i // cols))
    blank = jnp.zeros((128 - chans, wide), BF16)

    def line(i, n):
        if 3 <= n < 3 + lines:
            return pixels[first + i, n - 3]
        return beside[0, i, n] if n < 3 else beside[1, i, n - 3 - lines]

    def place(inner):
        def one_frame(i, carry):
            firsts = [n for n in range(0, lines + 6, 2) if (3 < n < 2 + lines) == inner]
            rhs = [x for n in firsts for k in range(2) for x in (line(i, n + k), blank)]
            picked = nt_dot(select, jnp.concatenate(rhs, axis=0)).astype(BF16)
            for m, n in enumerate(firsts):
                for k in range(2):
                    for j in range(2):
                        at = 256 * m + 128 * k
                        buffer[i, k, n // 2, :, 128 * j : 128 * (j + 1)] = picked[
                            cols * j : cols * (j + 1), at : at + 128
                        ]
            return carry

        lax.fori_loop(0, count, one_frame, 0)

    place(True)
    for copy in copies:
        copy.wait()
    place(False)

    size = rows * cols

    def products(frame, count, a, totals):
        here, left, right = totals
        frames = slice(frame - first, frame - first + count)
        lines = [
            buffer[frames, p % 2, p // 2 : p // 2 + rows].reshape(count * size, 256)
            for p in range(4)
        ]
        w = weights.at[a]
        for p in range(4):
            here = here + nt_dot(lines[p], jnp.concatenate([w[p, 1], w[p, 2]], axis=-1))
        for p in range(0, 4, 2):
            odd = jnp.concatenate([lines[p][:, 128:], lines[p + 1][:, 128:]], axis=-1)
            left = left + nt_dot(odd, jnp.concatenate([w[p, 0], w[p + 1, 0]], axis=-1))
            even = jnp.concatenate([lines[p][:, :128], lines[p + 1][:, :128]], axis=-1)
            right = right + nt_dot(even, jnp.concatenate([w[p, 3], w[p + 1, 3]], axis=-1))
        return here, left, right

    def zeros(count):
        return [jnp.zeros((count * size, outs), F32) for _ in range(3)]

    for n, (terms, extra, member) in enumerate(plan):
        totals = zeros(2)
        for frame, a in terms:
            totals = products(frame, 2, a, totals)
        here, left, right = totals
        total = here + from_left(left, cols) + from_right(right, cols)
        parts = [total[:size], total[size:]]
        if extra:
            here, left, right = products(*extra[:1], 1, *extra[1:], zeros(1))
            more = here + from_left(left, cols) + from_right(right, cols)
            parts[member] = parts[member] + more
        for k, part in enumerate(parts):
            part = part.reshape(rows, cols, outs)
            store(
                2 * n + k,
                [part[0:1] * flags[0], part[1 : rows - 1], part[rows - 1 :] * flags[1]],
            )


def early_kernel(plan, weights, flags, pixels, above, below, out_hbm, *scratch):
    *scratch, sent_ref, out_sems = scratch
    copies = [
        pltpu.make_async_copy(sent_ref.at[pl.ds(at, n)], out_hbm.at[pl.ds(at, n)], out_sems.at[k])
        for k, (at, n) in enumerate(((0, 2), (4, 1), (2, 2), (5, 1)))
    ]

    def store(n, parts):
        store_dense(sent_ref, n, jnp.concatenate([part.astype(BF16) for part in parts], axis=0))
        if n % 2 == 1:
            for copy in copies[n - 1 : n + 1]:
                copy.start()

    down_kernel(0, plan, weights, flags, (pixels, above, below), store, *scratch)
    for copy in copies:
        copy.wait()


def late_kernel(first, plan, weights, flags, pixels, above, below, out_ref, *scratch):
    def store(n, parts):
        out_ref[n] = jnp.concatenate(parts, axis=0)

    down_kernel(first, plan, weights, flags, (pixels, above, below), store, *scratch)


def down_scratch(count, pixels, rows, cols):
    _, _, chans, wide = pixels.shape
    return [
        pltpu.VMEM((count, 2, rows + 1, cols, 256), BF16),
        pltpu.VMEM((2, count, 3, chans, wide), BF16),
        pltpu.SemaphoreType.DMA((2,)),
    ]


def down_cost(plan, size):
    return 2 * sum(2 * len(terms) + 1 for terms, *_ in plan) * size * 8 * 65536


def down_early(weights, flags, pixels, above, below, rows, cols):
    frames = pixels.shape[0]
    plan = ((((0, 2), (1, 1), (2, 0)), (), 0), (((0, 0),), (0, 1), 1))
    return pl.pallas_call(
        functools.partial(early_kernel, plan),
        name="down_early",
        out_shape=pltpu.HBM((6, rows, cols, 128), BF16),
        in_specs=vmem(1) + [smem()] + vmem(1) + [anywhere()] * 2,
        out_specs=anywhere(),
        scratch_shapes=[
            *down_scratch(frames, pixels, rows, cols),
            pltpu.VMEM((6, rows, cols, 128), BF16),
            pltpu.SemaphoreType.DMA((4,)),
        ],
        compiler_params=pltpu.CompilerParams(vmem_limit_bytes=VMEM_LIMIT),
        cost_estimate=pl.CostEstimate(
            flops=down_cost(plan, rows * cols), bytes_accessed=4 * 2**20, transcendentals=0
        ),
    )(weights, flags, near(pixels), far(above), far(below))


def down_late(weights, flags, pixels, above, below, rows, cols):
    frames, outs = pixels.shape[0], weights.shape[3]
    plan = ((((2, 2),), (3, 1), 0),)
    return call(
        functools.partial(late_kernel, frames - 2, plan),
        "down_late",
        pltpu.HBM((2, rows, cols, outs), F32),
        vmem(1) + [smem()] + vmem(1) + [anywhere()] * 2,
        down_scratch(2, pixels, rows, cols),
        down_cost(plan, rows * cols),
    )(weights, flags, near(pixels), far(above), far(below))


def back_kernel(
    held, parts_ref, w_hbm, tile_hbm, own_hbm, late_hbm, next_hbm, out_ref, stats_ref, *scratch
):
    main, rows_pair, frames_pair, rest, weights, tile_ref, own_ref, late_ref, next_ref, sems = scratch
    frames, rows, cols, chans = tile_ref.shape
    pairs = (
        (own_hbm.at[pl.ds(0, 2)], own_ref.at[pl.ds(0, 2)]),
        (own_hbm.at[pl.ds(4, 1)], own_ref.at[pl.ds(2, 1)]),
        (next_hbm, next_ref),
        (late_hbm, late_ref),
        (w_hbm, weights),
        (tile_hbm.at[:, pl.ds(2, rows)], tile_ref),
    )
    copies = [pltpu.make_async_copy(*pair, sems.at[k]) for k, pair in enumerate(pairs)]
    for copy in copies:
        copy.start()
    seqs = out_ref.shape[0]
    size = 2 * rows * cols
    mean, scale = group_stats(parts_ref, held)
    stats_ref[...] = jnp.concatenate([mean, scale], axis=0)
    buffer = Packed(main, rows_pair, frames_pair)
    buffer.clear()
    for copy in copies[:3]:
        copy.wait()
    for k in range(2):
        for at, ref in ((k, own_ref), (frames + k, next_ref)):
            block, tail = load_dense(ref, k)
            for r in range(rows + 2):
                buffer.put(at, r, block[r], tail[r])
    copies[3].wait()
    for k in range(2):
        block, tail = load_dense(next_ref, 2 + k)
        late = late_ref[k]
        block = (late[..., :128] + block.astype(F32)).astype(BF16)
        tail = (late[..., 128:] + tail.astype(F32)).astype(BF16)
        for r in range(rows + 2):
            buffer.put(frames - 2 + k, r, block[r], tail[r])
    for copy in copies[4:]:
        copy.wait()
    order = one_hot(
        size,
        size,
        lambda i: ((i >> 3) & 1) * (rows * cols) + (i & 3) * cols + 2 * (i >> 4) + ((i >> 2) & 1),
    )

    def two_frames(n, carry):
        first_sum, second_sum = carry
        t = 2 * n
        total = [jnp.zeros((size, chans), F32) for _ in range(3)]
        for lhs, holds in buffer.operands(t, 2, rows):
            for dc in range(3):
                taps = [
                    weights[2 - tap[0], 2 - tap[1], 2 - dc, :, PARTS[tap[2]]]
                    if tap
                    else jnp.zeros((chans, 64), BF16)
                    for tap in holds
                ]
                total[dc] = total[dc] + nt_dot(lhs, jnp.concatenate(taps, axis=1))
        total = total[1] + from_left(total[0], cols) + from_right(total[2], cols)
        tile = tile_ref[pl.ds(t, 2)].reshape(size, chans)
        normed = (tile.astype(F32) - mean) * scale
        sigmoid = 1.0 / (1.0 + jnp.exp(-normed))
        grad = total * sigmoid * (1.0 + normed * (1.0 - sigmoid))
        first_sum = first_sum + jnp.sum(grad, axis=0, keepdims=True)
        second_sum = second_sum + jnp.sum(grad * normed, axis=0, keepdims=True)
        own = [
            ref[pl.ds(t, 2), 1 : 1 + rows].reshape(size, 128) for ref in (main, rows_pair)
        ]
        own = jnp.concatenate(own, axis=1)[:, :chans].astype(F32)
        base = (own + grad * scale).astype(BF16)
        home = dot(order, base)
        block = home[:, :128].reshape(seqs, 16, 128).astype(BF16)
        out_ref[:, pl.ds(pl.multiple_of(16 * n, 16), 16)] = block
        tail = home[:, 128:].reshape(seqs, 2, 8, chans - 128)
        for k in range(2):
            rest[n, :, :, 64 * k : 64 * (k + 1)] = tail[:, k]
        return first_sum, second_sum

    none = jnp.zeros((1, chans), F32)
    sums = lax.fori_loop(0, frames // 2, two_frames, (none, none))
    both = jnp.concatenate([rest[n] for n in range(frames // 2)], axis=1)
    out_ref[:, 8 * frames : 12 * frames] = both.astype(BF16)
    extra = extra_rows(*sums).astype(BF16)
    out_ref[:, 12 * frames :] = jnp.broadcast_to(extra[None], (seqs, EXTRA, 128))


def back(parts, held, weights, tile, own, late, following, seqs):
    frames, ext, cols, chans = tile.shape
    rows = ext - 4
    return call(
        functools.partial(back_kernel, held),
        "back",
        (pltpu.HBM((seqs, 12 * frames + EXTRA, 128), BF16), kept((2, chans), F32)),
        vmem(1) + [anywhere()] * 5,
        [
            *packed_scratch(frames + 2, rows + 2, cols),
            pltpu.VMEM((frames // 2, seqs, 8, 128), F32),
            pltpu.VMEM(weights.shape, BF16),
            pltpu.VMEM((frames, rows, cols, chans), BF16),
            pltpu.VMEM((3, *own.shape[1:]), BF16),
            pltpu.VMEM(late.shape, F32),
            pltpu.VMEM(following.shape, BF16),
            pltpu.SemaphoreType.DMA((6,)),
        ],
        2 * frames * rows * cols * 21 * 65536,
    )(parts, far(weights), far(tile), far(own), far(late), far(following))


def sums_kernel(x_ref, out_ref):
    one, two = from_extra(x_ref[...])
    sums = [jnp.sum(v, axis=0, keepdims=True) for v in (one, two)]
    out_ref[...] = jnp.broadcast_to(jnp.concatenate(sums, axis=0)[None], out_ref.shape)


def local_sums(blocks, frames, chans, clips):
    seqs = blocks.shape[0]
    at = 12 * frames // EXTRA
    return pl.pallas_call(
        sums_kernel,
        name="local_sums",
        grid=(1,),
        out_shape=array((clips, 2, chans), F32),
        in_specs=[pl.BlockSpec((seqs, EXTRA, 128), lambda i: (0, at, 0))],
        out_specs=pl.BlockSpec((clips, 2, chans), lambda i: (0, 0, 0)),
        compiler_params=pltpu.CompilerParams(vmem_limit_bytes=VMEM_LIMIT),
        cost_estimate=pl.CostEstimate(flops=10**6, bytes_accessed=10**5, transcendentals=0),
    )(blocks)


def token_kernel(count, x_ref, tokens_ref, stats_ref, parts_ref, out_ref):
    frames, stripe, chans, height = tokens_ref.shape
    seqs = x_ref.shape[0]
    sums = jnp.sum(parts_ref[...], axis=0)
    sums = group_sum(jnp.concatenate([sums, jnp.zeros((6, chans), F32)], axis=0)) / count
    first, second = (jnp.broadcast_to(sums[k : k + 1], (128, chans)).T for k in range(2))
    mean, scale = (jnp.broadcast_to(stats_ref[k : k + 1], (128, chans)).T for k in range(2))
    eye = one_hot(128, 128, lambda i: i)
    lanes = 16 * seqs

    order = one_hot(lanes, lanes, lambda i: ((i >> 2) & 3) * height + (i >> 4) * 4 + (i & 3))

    def turned(at):
        block = x_ref[:, at : at + 16].reshape(lanes, 128)
        return dot(nt_dot(eye, block).astype(BF16), order)

    rest = turned(8 * frames)
    for n in range(frames // 2):
        main = turned(16 * n)
        for k in range(2 * stripe):
            t, c = 2 * n + k // stripe, k % stripe
            at = stripe * n + c
            base = jnp.concatenate(
                [
                    main[:, height * k : height * (k + 1)],
                    rest[64 * (k // stripe) : 64 * (k // stripe + 1), height * at : height * (at + 1)],
                ],
                axis=0,
            )
            normed = (tokens_ref[t, c].astype(F32) - mean) * scale
            out_ref[t, c] = (base - (first + normed * second) * scale).astype(BF16)


def token_gradient(blocks, tokens, stats, parts, count):
    return call(
        functools.partial(token_kernel, count),
        "token_gradient",
        array(tokens.shape),
        vmem(4),
        [],
        10**9,
    )(blocks, tokens, stats, parts)


class Packed:
    def __init__(self, main, rows_pair, frames_pair):
        self.main, self.rows_pair, self.frames_pair = main, rows_pair, frames_pair

    def clear(self):
        self.rows_pair[...] = jnp.zeros_like(self.rows_pair)
        self.frames_pair[...] = jnp.zeros_like(self.frames_pair)

    def put(self, t, r, main, rest):
        self.main[t, r] = main
        self.rows_pair[t, r, :, 0:64] = rest
        self.frames_pair[t, r, :, 0:64] = rest
        if r > 0:
            self.rows_pair[t, r - 1, :, 64:128] = rest
        if not (isinstance(t, int) and t == 0):
            self.frames_pair[t - 1, r, :, 64:128] = rest

    def operands(self, t, count, rows):
        def get(ref, dt, dr):
            block = ref[pl.ds(t + dt, count), dr : dr + rows]
            return block.reshape(count * rows * block.shape[2], 128)

        tiles = [(get(self.main, dt, dr), [(dt, dr, 0)]) for dt in range(3) for dr in range(3)]
        for dt in range(3):
            tiles.append((get(self.rows_pair, dt, 0), [(dt, 0, 1), (dt, 1, 1)]))
        tiles.append((get(self.frames_pair, 0, 2), [(0, 2, 1), (1, 2, 1)]))
        tiles.append((get(self.rows_pair, 2, 2), [(2, 2, 1), None]))
        return [
            (jnp.concatenate([one, two], axis=1), has + more)
            for (one, has), (two, more) in zip(tiles[::2], tiles[1::2])
        ]


def packed_scratch(frames, rows, cols):
    return [pltpu.VMEM((frames, rows, cols, 128), BF16) for _ in range(3)]


PARTS = (slice(0, 128), slice(128, 192))


def fetch(source, target, sems):
    copies = [pltpu.make_async_copy(source.at[k], target.at[k], sems.at[k]) for k in range(3)]
    for copy in copies:
        copy.start()
    return copies


def mid_kernel(
    flags, stats, w_hbm, tile_hbm, before_ref, out_ref, sent_ref, *scratch
):
    main, rows_pair, frames_pair, weights, sems, tile_ref, sem = scratch
    tile_copy = pltpu.make_async_copy(tile_hbm, tile_ref, sem)
    tile_copy.start()
    copies = fetch(w_hbm, weights, sems)
    frames, rows, cols, chans = out_ref.shape
    size = 2 * rows * cols
    mean = stats[0:1]
    scale = stats[1:2]

    def activate(value, row, later):
        normed = (value.astype(F32) - mean) * scale
        act = normed / (1.0 + jnp.exp(-normed))
        if row < 2:
            act = act * flags[0]
        if row >= rows:
            act = act * flags[1]
        if later:
            act = act * flags[2]
        return act.astype(BF16)

    buffer = Packed(main, rows_pair, frames_pair)
    buffer.clear()
    for t in range(2):
        for r in range(rows + 2):
            act = activate(before_ref[t, r], r, True)
            buffer.put(t, r, act[:, :128], act[:, 128:])
    tile_copy.wait()

    def one_frame(t, carry):
        for r in range(rows + 2):
            act = activate(tile_ref[t, r], r, False)
            buffer.put(t + 2, r, act[:, :128], act[:, 128:])
        return carry

    lax.fori_loop(0, frames, one_frame, 0)
    for copy in copies:
        copy.wait()

    def two_frames(n, carry):
        t = 2 * n
        total = [jnp.zeros((size, chans), F32) for _ in range(3)]
        for lhs, holds in buffer.operands(t, 2, rows):
            for dc in range(3):
                taps = [
                    weights[tap[0], tap[1], dc, PARTS[tap[2]]]
                    if tap
                    else jnp.zeros((64, chans), BF16)
                    for tap in holds
                ]
                total[dc] = total[dc] + dot(lhs, jnp.concatenate(taps, axis=0))
        total = total[1] + from_left(total[0], cols) + from_right(total[2], cols)
        total = total.reshape(2, rows, cols, chans)
        total = total + tile_ref[pl.ds(t, 2), 1 : 1 + rows].astype(F32)
        out_ref[pl.ds(t, 2), 0:1] = (total[:, 0:1] * flags[0]).astype(BF16)
        out_ref[pl.ds(t, 2), 1 : rows - 1] = total[:, 1 : rows - 1].astype(BF16)
        out_ref[pl.ds(t, 2), rows - 1 : rows] = (total[:, rows - 1 :] * flags[1]).astype(BF16)
        return carry

    lax.fori_loop(0, frames // 2, two_frames, 0)
    for k in range(2):
        store_dense(sent_ref, k, out_ref[frames - 2 + k])


def middle(flags, stats, weights, tile, before):
    frames, ext, cols, chans = tile.shape
    rows = ext - 2
    return call(
        mid_kernel,
        "middle",
        (kept((frames, rows, cols, chans)), array((3, rows, cols, 128))),
        [smem()] + vmem(1) + [anywhere()] * 2 + vmem(1),
        [
            *packed_scratch(frames + 2, ext, cols),
            pltpu.VMEM(weights.shape, BF16),
            pltpu.SemaphoreType.DMA((3,)),
            pltpu.VMEM(tile.shape, BF16),
            pltpu.SemaphoreType.DMA,
        ],
        2 * frames * rows * cols * 27 * 65536,
    )(flags, stats, far(weights), tile, before)


def bring_kernel(x_hbm, out_ref, sem):
    copy = pltpu.make_async_copy(x_hbm, out_ref, sem)
    copy.start()
    copy.wait()


def brought(x):
    scratch = [pltpu.SemaphoreType.DMA]
    return near(call(bring_kernel, "bring", kept(x.shape), [anywhere()], scratch, 10**6)(far(x)))


def decode_kernel(weights, before_ref, mid_ref, out_ref, main_ref, pair_ref, wide):
    frames, ext, cols, chans = mid_ref.shape
    lines, outs, _ = out_ref.shape[1:]
    rows = lines // 2
    pair_ref[:, ext - 1] = jnp.zeros_like(pair_ref[:, ext - 1])

    def put(at, main, rest):
        main_ref[at] = main
        pair_ref[at, :, :, 0:64] = rest
        pair_ref[at, 0 : ext - 1, :, 64:128] = rest[1:]

    for k in range(2):
        put(k, *load_dense(before_ref, k))

    def one_frame(t, carry):
        value = mid_ref[t]
        put(t + 2, value[..., :128], value[..., 128:])
        return carry

    lax.fori_loop(0, frames, one_frame, 0)
    eye = one_hot(outs, 128, lambda i: i)
    size = 2 * rows * cols

    for t in range(0, frames, 2):
        for i, taps in enumerate((((0, 3), (1, 1)), ((1, 2), (2, 0)))):
            here, aside = (jnp.zeros((size, 256), F32) for _ in range(2))
            tiles = []
            for dt in range(3):
                at = slice(t + dt, t + dt + 2)
                (dr, p), (below, q) = taps
                for ref, row, parts in (
                    (main_ref, dr, [(p, slice(0, 128))]),
                    (main_ref, below, [(q, slice(0, 128))]),
                    (pair_ref, dr, [(p, slice(128, 192)), (q, slice(128, 192))]),
                ):
                    lhs = ref[at, row : row + rows].reshape(size, 128)
                    tiles.append((lhs, [(weights.at[dt, tap], part) for tap, part in parts]))
            for n in range(0, len(tiles), 2):
                lhs = jnp.concatenate([lhs for lhs, _ in tiles[n : n + 2]], axis=1)
                taken = [tap for _, some in tiles[n : n + 2] for tap in some]
                for into, (one, two) in enumerate(((1, 2), (3, 0))):
                    rhs = [
                        jnp.concatenate([w[one, part], w[two, part]], axis=1) for w, part in taken
                    ]
                    rhs = jnp.concatenate(rhs, axis=0)
                    if into == 0:
                        here = here + dot(lhs, rhs)
                    else:
                        aside = aside + dot(lhs, rhs)
            even = (here[:, :128] + from_left(aside[:, :128], cols)).reshape(2, rows, cols, 128)
            odd = (here[:, 128:] + from_right(aside[:, 128:], cols)).reshape(2, rows, cols, 128)
            for k in range(2):
                for r in range(rows):
                    wide[k, 2 * r + i, pl.ds(0, cols, stride=2), :] = even[k, r]
                    wide[k, 2 * r + i, pl.ds(1, cols, stride=2), :] = odd[k, r]
        for k in range(2):
            for r in range(rows):
                pair = wide[k, 2 * r : 2 * r + 2].reshape(4 * cols, 128).astype(BF16)
                turned = nt_dot(eye, pair).astype(BF16)
                out_ref[t + k, 2 * r] = turned[:, 0 : 2 * cols]
                out_ref[t + k, 2 * r + 1] = turned[:, 2 * cols :]


def decode(weights, before, mid, outs):
    frames, ext, cols, chans = mid.shape
    rows = ext - 2
    return call(
        decode_kernel,
        "decode",
        array((frames, 2 * rows, outs, 2 * cols)),
        vmem(3),
        [
            pltpu.VMEM((frames + 2, ext, cols, 128), BF16),
            pltpu.VMEM((frames + 2, ext, cols, 128), BF16),
            pltpu.VMEM((2, 2 * rows, 2 * cols, 128), F32),
        ],
        2 * frames * rows * cols * 24 * 65536,
    )(weights, before, mid)


def moved(block, clip_step, seq_step):
    clips, seqs = lax.axis_size("clip"), lax.axis_size("seq")
    if clip_step == 0:
        route = [(i - seq_step, i) for i in range(seqs) if 0 <= i - seq_step < seqs]
        return lax.ppermute(block, "seq", route)
    if seq_step == 0:
        route = [(i - clip_step, i) for i in range(clips) if 0 <= i - clip_step < clips]
        return lax.ppermute(block, "clip", route)
    route = [
        ((s - seq_step) * clips + c - clip_step, s * clips + c)
        for s in range(seqs)
        for c in range(clips)
        if 0 <= c - clip_step < clips and 0 <= s - seq_step < seqs
    ]
    return lax.ppermute(block, ("seq", "clip"), route)


def exchanged(blocks, axis):
    return lax.all_to_all(blocks, axis, 0, 0, tiled=True)


def body(tokens, conv_one, conv_two, pixel_grad):
    frames, height, stripe, chans = tokens.shape
    lines, wide, outs = pixel_grad.shape[1:]
    rows, cols = lines // 2, wide // 2
    clips, seqs = lax.axis_size("clip"), lax.axis_size("seq")
    clip, seq = lax.axis_index("clip"), lax.axis_index("seq")
    flags = jnp.stack([seq != 0, seq != seqs - 1, clip != 0]).astype(F32)
    tokens = tokens.transpose(0, 2, 3, 1)
    pixels = pixel_grad.transpose(0, 1, 3, 2)
    held = float(frames * height * stripe)

    first, last, near_tokens = edges(pixels, tokens)
    above, below = moved(last, 0, 1), moved(first, 0, -1)
    packed = pack(near(near_tokens), seqs)
    both = combined_weights(conv_two)
    above, both, packed = lax.optimization_barrier((above, both, packed))

    blocks = exchanged(packed, "seq")
    own = far(down_early(near(both), flags, pixels, above, below, rows + 2, cols))
    following = moved(own, -1, 0)
    tile, tile_last, parts = unpack(blocks, frames, cols, chans, clips, held)
    tile = far(tile)
    late = down_late(near(both), flags, pixels, above, below, rows + 2, cols)
    parts, late = lax.optimization_barrier((exchanged(parts, "clip"), late))
    parts, tile_last = lax.optimization_barrier((parts, tile_last))
    tile_z = moved(tile_last, 1, 0)

    blocks, stats = back(parts, held * seqs, conv_one, tile, own, late, following, seqs)
    home, stats = exchanged(blocks, "seq"), near(stats)

    mid, mid_last = middle(flags, stats, conv_one, tile, tile_z)
    sums, both = lax.optimization_barrier((local_sums(home, frames, chans, clips), both))
    decoded = decode(brought(both), moved(mid_last, 1, 0), near(mid), outs)

    sums = exchanged(sums, "clip")
    sums, decoded = lax.optimization_barrier((sums, decoded))
    count = held * seqs * clips * (chans // GROUPS)
    token_grad = token_gradient(home, tokens, stats, sums, count)
    return (decoded.transpose(0, 1, 3, 2), token_grad.transpose(0, 3, 1, 2))


def solution(mesh):
    return jax.shard_map(
        body,
        mesh=mesh,
        in_specs=(P("clip", None, "seq", None), P(), P(), P("clip", "seq", None, None)),
        out_specs=(P("clip", "seq", None, None), P("clip", None, "seq", None)),
        check_vma=False,
    )
```
